32 devices in a mesh: rep: 2 (over x), ga: 16 (over z, y, core).
Axes of the slice: x: 2, y: 2, z: 4, core: 2. Of those that a mesh axis runs over, the one named last changes fastest.
Arguments:
- positions: float32 [64, 3, 768], P('rep', None, 'ga'), parts along dimension 0, may hold values from -3 to 23, as said below
- weights: int32 [1, 32], replicated, may hold values from 1 to 16
- psi: bfloat16 [2, 512, 2, 32768], P('rep', None, None, 'ga'), parts along dimension 0, may hold values from -5 to 5
- vloc: float32 [2, 32768], P('rep'), parts along dimension 0, may hold values from -8 to 8
Outputs:
- psi_new: bfloat16 [2, 512, 2, 32768], P('rep', None, None, 'ga'), parts along dimension 0
- bead_forces: float32 [64, 3, 768], P('rep', None, 'ga'), parts along dimension 0
The draws below stay inside these ranges and needn't reach their ends.
There are 2 independent parts, one for each index of `rep`. The reference program is written for one: setup_inputs(seed, part) draws one part's arguments, and reference() takes and returns one part's arrays. A program takes and returns all parts, laid end to end along the dimension named above; an argument that names none is the same for every part. Nothing has to cross between parts.
Inputs may be any that keep to these rules, and one draw needn't show every extreme that they name: `positions`: atom 3w is the oxygen of water w and atoms 3w+1 and 3w+2 are its hydrogens; in every bead each hydrogen lies between 1.0 and 2.6 from its oxygen.
All inputs are finite; a program needn't handle non-finite values.
Results may differ from the reference program's by a relative error of at most 0.0037.
The reference program's roundings to bfloat16 on the way (of `table`, `projections`, `trial` and `mixer`) count: a program that leaves them out, or rounds other values in their place, can miss the bound.
Values may be sent and summed in bfloat16 or wider, within the bound.
No kernel may reach another device: no remote copies, remote signals or barrier semaphores. Data moves between devices by JAX's collectives and lax.ppermute only.
A program may use at most 192 MiB of HBM per device.

```python
import jax
import jax.numpy as jnp
from jax import lax

BEADS = 32
CBEADS = 1
WATERS = 256
ATOMS = 768
BANDS = 512
NGRID = 32
GVECS = 32768


def draw_positions(key, part):
    subkeys = jax.random.split(jax.random.fold_in(key, 7), 5)
    oxygen = jax.random.uniform(subkeys[0], (3, WATERS), jnp.float32, 0.0, 20.0)
    first_dir = jax.random.normal(subkeys[1], (3, WATERS), jnp.float32)
    second_dir = jax.random.normal(subkeys[2], (3, WATERS), jnp.float32)
    first_dir = first_dir / jnp.sqrt(jnp.sum(first_dir * first_dir, axis=0, keepdims=True) + 1e-06)
    second_dir = second_dir / jnp.sqrt(jnp.sum(second_dir * second_dir, axis=0, keepdims=True) + 1e-06)
    lengths = jax.random.uniform(subkeys[3], (2, WATERS), jnp.float32, 1.5, 2.1)
    centroid = jnp.stack([oxygen, oxygen + lengths[0] * first_dir, oxygen + lengths[1] * second_dir], axis=2).reshape(3, ATOMS)
    spread = jax.random.uniform(subkeys[4], (BEADS, 3, ATOMS), jnp.float32, -0.12, 0.12)
    return centroid[None] + spread


def with_ends(array, stream_key, least, top_value):
    spot = [jax.random.randint(jax.random.fold_in(stream_key, axis), (), 0, length) for axis, length in enumerate(array.shape)]
    longest = array.shape.index(max(array.shape))
    next_to = spot[:longest] + [(spot[longest] + 1) % array.shape[longest]] + spot[longest + 1:]
    return array.at[tuple(spot)].set(least).at[tuple(next_to)].set(top_value)


def block_scale(rng, dims, pieces, low, top_value):
    loudness, own = 1.0, jax.random.fold_in(rng, 6)
    for axis_at, parts in pieces:
        steps = jnp.exp(jax.random.uniform(jax.random.fold_in(own, axis_at), (parts,), jnp.float32, low / len(pieces), top_value / len(pieces)))
        loudness = loudness * jnp.repeat(steps, dims[axis_at] // parts).reshape([-1 if axis == axis_at else 1 for axis in range(len(dims))])
    return loudness


def bell_draw(stream_key, extent, scale, most, shards=(), kind=jnp.bfloat16):
    entries = jax.random.normal(stream_key, extent, jnp.float32) * scale
    if len(shards) > 0:
        entries = block_scale(stream_key, extent, shards, -0.22, 0.18) * entries
    return jnp.clip(entries, min=-most, max=most).astype(kind)


def setup_inputs(seed: int = 0, part: int = 0) -> dict:
    streams_of = jax.random.split(jax.random.key(seed), 5)
    part_splits = jax.random.split(jax.random.fold_in(streams_of[4], part), 5)
    positions = draw_positions(jax.random.fold_in(jax.random.fold_in(streams_of[4], part), 71), part)
    weights = with_ends(jax.random.randint(streams_of[1], (CBEADS, BEADS), 1, 17), jax.random.fold_in(streams_of[1], 1), 1, 16).astype(jnp.int32)
    psi = bell_draw(part_splits[2], (CBEADS, BANDS, 2, GVECS), 0.7071, 5.0, ((3, 16),))
    vloc = jnp.clip(jax.random.uniform(part_splits[3], (CBEADS, GVECS), jnp.float32, -8.0, 8.0), -8.0, 8.0)
    return {"positions": positions, "weights": weights, "psi": psi, "vloc": vloc}


box_length = 20.0
bond_stiff = 0.5
bond_rest = 1.8
spring_stiff = 2.0
width_square = 0.09
step_size = 0.02
nonlocal_strength = 250.0
occupation = 2.0
highest = lax.Precision.HIGHEST

def frequency(index, count):
    signed = jnp.where(index < count // 2, index, index - count)
    return signed.astype(jnp.float32) * (2.0 * jnp.pi / box_length)

def field_forces(positions):
    oxygen = positions[:, :, 0::3]
    toward_one = positions[:, :, 1::3] - oxygen
    toward_two = positions[:, :, 2::3] - oxygen

    def stretch(offset):
        length = jnp.sqrt(lax.optimization_barrier(jnp.sum(offset * offset, axis=1, keepdims=True)))
        return -bond_stiff * (length - bond_rest) * offset / length
    pull_one = stretch(toward_one)
    pull_two = stretch(toward_two)
    bonds = jnp.stack([-(pull_one + pull_two), pull_one, pull_two], axis=3).reshape(positions.shape)
    springs = 2.0 * positions - jnp.roll(positions, 1, axis=0) - jnp.roll(positions, -1, axis=0)
    return bonds - spring_stiff * springs

def inner(left_mat, right_mat):
    return lax.dot_general(left_mat, right_mat, (((1,), (1,)), ((), ())), preferred_element_type=jnp.float32)

def reference(positions, weights, psi, vloc):
    near_forces = field_forces(positions)
    weight_float = weights.astype(jnp.float32)
    mixing = weight_float / lax.optimization_barrier(jnp.sum(weight_float, axis=1, keepdims=True))
    centres = jnp.einsum('cj,jan->can', mixing, positions, precision=highest)
    flat_index = jnp.arange(GVECS, dtype=jnp.int32)
    gvectors = jnp.stack([frequency(flat_index // (NGRID * NGRID), NGRID), frequency(flat_index // NGRID % NGRID, NGRID), frequency(flat_index % NGRID, NGRID)])
    square = lax.optimization_barrier(jnp.sum(gvectors * gvectors, axis=0))
    profile = jnp.exp(-0.5 * width_square * square)
    kinetic = 0.5 * square
    new_waves = []
    dft_forces = []
    for contracted in range(CBEADS):
        oxygens = centres[contracted][:, 0::3]
        phases = jnp.einsum('ai,ag->ig', oxygens, gvectors, precision=highest)
        wave_cos = profile * jnp.cos(phases)
        wave_sin = profile * jnp.sin(phases)
        table = jnp.concatenate([jnp.concatenate([wave_cos, -wave_sin], 1), jnp.concatenate([wave_sin, wave_cos], 1)], 0).astype(jnp.bfloat16)
        wavefunc = psi[contracted].reshape(BANDS, 2 * GVECS)
        real_part = wavefunc[:, :GVECS]
        imag_part = wavefunc[:, GVECS:]
        projections = (inner(table, wavefunc) * (1.0 / GVECS)).astype(jnp.bfloat16)
        nonlocal_term = lax.dot_general(projections, table, (((0,), (0,)), ((), ())), preferred_element_type=jnp.float32)
        paired = jnp.concatenate([wavefunc, jnp.concatenate([imag_part, -real_part], 1)], 0)
        side_by_side = jnp.concatenate([projections[:WATERS], projections[WATERS:]], 1)
        weighted = jnp.dot(side_by_side, paired, preferred_element_type=jnp.float32)
        mixed_wave = wave_cos * weighted[:, GVECS:] + wave_sin * weighted[:, :GVECS]
        oxygen_force = 2.0 * occupation * nonlocal_strength / GVECS * jnp.einsum('ag,ig->ai', gvectors, mixed_wave, precision=highest)
        hydrogen_zero = jnp.zeros_like(oxygen_force)
        dft_forces.append(jnp.stack([oxygen_force, hydrogen_zero, hydrogen_zero], axis=2).reshape(3, ATOMS))
        grid_potential = vloc[contracted].reshape(NGRID, NGRID, NGRID)

        def apply_block(band_block):
            complex_wave = (band_block[:, 0].astype(jnp.float32) + 1j * band_block[:, 1].astype(jnp.float32)).reshape(-1, NGRID, NGRID, NGRID)
            spread = jnp.fft.fftn(grid_potential * jnp.fft.ifftn(complex_wave, axes=(1, 2, 3)), axes=(1, 2, 3)).reshape(-1, GVECS)
            return jnp.stack([jnp.real(spread), jnp.imag(spread)], axis=1).astype(jnp.float32)
        blocks = min(64, BANDS)
        potential_term = lax.map(apply_block, psi[contracted].reshape(BANDS // blocks, blocks, 2, GVECS)).reshape(BANDS, 2, GVECS)
        wave_float = psi[contracted].astype(jnp.float32)
        hamil_re = kinetic * wave_float[:, 0] + potential_term[:, 0] + nonlocal_strength * nonlocal_term[:, :GVECS]
        hamil_im = kinetic * wave_float[:, 1] + potential_term[:, 1] + nonlocal_strength * nonlocal_term[:, GVECS:]
        trial = jnp.concatenate([wave_float[:, 0] - step_size * hamil_re, wave_float[:, 1] - step_size * hamil_im], 1).astype(jnp.bfloat16)
        rotated = jnp.concatenate([trial, jnp.concatenate([-trial[:, GVECS:], trial[:, :GVECS]], 1)], 0)
        margin = inner(trial, rotated) * (1.0 / GVECS)
        identity_rows = jnp.concatenate([jnp.eye(BANDS, dtype=jnp.float32), jnp.zeros((BANDS, BANDS), jnp.float32)], 1)
        mixer = (1.5 * identity_rows - 0.5 * margin).astype(jnp.bfloat16)
        updated = jnp.dot(mixer, rotated, preferred_element_type=jnp.float32).astype(jnp.bfloat16)
        new_waves.append(updated.reshape(BANDS, 2, GVECS))
    contracted_force = jnp.einsum('cj,can->jan', mixing, jnp.stack(dft_forces), precision=highest)
    bead_forces = near_forces + BEADS / CBEADS * contracted_force
    return (jnp.stack(new_waves), bead_forces)
```

```python
import functools

import jax
import jax.numpy as jnp
import numpy as np
from jax import lax
from jax.experimental import pallas as pl
from jax.experimental.pallas import tpu as pltpu
from jax.sharding import PartitionSpec as P

BEADS = 32
CBEADS = 1
WATERS = 256
NGRID = 32
GVECS = 32768


box_length = 20.0
bond_stiff = 0.5
bond_rest = 1.8
spring_stiff = 2.0
width_square = 0.09
step_size = 0.02
nonlocal_strength = 250.0
occupation = 2.0
highest = lax.Precision.HIGHEST
bf16 = jnp.bfloat16
f32 = jnp.float32

PLANE = NGRID * NGRID
GROUP = 8
LANES = 256
VMEM_BYTES = 56 * 2**20


def frequency(index, count):
    signed = jnp.where(index < count // 2, index, index - count)
    return signed.astype(jnp.float32) * (2.0 * jnp.pi / box_length)


def field_forces(positions):
    oxygen = positions[:, :, 0::3]
    toward_one = positions[:, :, 1::3] - oxygen
    toward_two = positions[:, :, 2::3] - oxygen

    def stretch(offset):
        length = jnp.sqrt(jnp.sum(offset * offset, axis=1, keepdims=True))
        return -bond_stiff * (length - bond_rest) * offset / length

    pull_one = stretch(toward_one)
    pull_two = stretch(toward_two)
    bonds = jnp.stack([-(pull_one + pull_two), pull_one, pull_two], axis=3).reshape(positions.shape)
    springs = 2.0 * positions - jnp.roll(positions, 1, axis=0) - jnp.roll(positions, -1, axis=0)
    return bonds - spring_stiff * springs


def inner(left_mat, right_mat):
    return lax.dot_general(
        left_mat, right_mat, (((1,), (1,)), ((), ())), preferred_element_type=jnp.float32
    )


def matmul(left_mat, right_mat):
    return jnp.dot(left_mat, right_mat, preferred_element_type=jnp.float32)


def exchange(blocks):
    return lax.all_to_all(blocks, "ga", split_axis=0, concat_axis=0, tiled=True)


def transform_tables():
    index = np.arange(PLANE)
    first, second = index // NGRID, index % NGRID
    product = (first[:, None] * first[None, :] + second[:, None] * second[None, :]) % NGRID
    angle = product * (2.0 * np.pi / NGRID)
    line = np.arange(NGRID)
    x_angle = (line[:, None] * line[None, :] % NGRID) * (2.0 * np.pi / NGRID)
    cosine, sine = np.cos(x_angle), np.sin(x_angle)
    same = np.eye(GROUP)
    rows = 2 * NGRID * GROUP

    def spread(mixing, order):
        return np.einsum("xycd,bm->" + order, mixing, same).reshape(rows, rows)

    def mixed(rr, ri, ir, ii):
        return np.stack([np.stack([rr, ri], -1), np.stack([ir, ii], -1)], -2)

    on_cosine = spread(mixed(cosine, -sine, sine, cosine), "xcbymd")
    on_sine = spread(mixed(-sine, -cosine, cosine, -sine), "xcbymd")
    backward = np.concatenate([on_cosine, on_sine], 1)
    forward = spread(mixed(cosine, sine, -sine, cosine), "xcbydm")
    return [
        jnp.asarray(table.astype(np.float32), dtype=bf16)
        for table in (np.cos(angle), np.sin(angle), backward, forward)
    ]


def potential_kernel(
    wave_ref, cos_ref, sin_ref, back_ref, fore_ref, pot_ref, out_ref, rows, planes, turned
):
    parts, local_g = wave_ref.shape[0], wave_ref.shape[3]
    band_rows = 2 * GROUP
    all_rows = NGRID * band_rows
    piece = min(local_g, PLANE)
    for start in range(0, NGRID * PLANE, piece):
        owner, offset = start // local_g, start % local_g
        x, column = start // PLANE, start % PLANE
        block = wave_ref[owner, :, :, offset : offset + piece]
        rows[x * band_rows : (x + 1) * band_rows, column : column + piece] = block.reshape(
            band_rows, piece
        )

    @pl.loop(0, PLANE // LANES)
    def _(step):
        columns = pl.ds(pl.multiple_of(step * LANES, LANES), LANES)
        planes[:all_rows, columns] = matmul(rows[...], cos_ref[:, columns]).astype(bf16)
        planes[all_rows:, columns] = matmul(rows[...], sin_ref[:, columns]).astype(bf16)

    @pl.loop(0, PLANE // LANES)
    def _(step):
        columns = pl.ds(pl.multiple_of(step * LANES, LANES), LANES)
        space = matmul(back_ref[...], planes[:, columns]).reshape(NGRID, band_rows, LANES)
        space = space * pot_ref[:, columns][:, None, :]
        space = space.reshape(all_rows, LANES).astype(bf16)
        waves = matmul(fore_ref[...], space)
        turned[:, columns] = waves.astype(bf16)
        halves = waves.reshape(NGRID, 2, GROUP, LANES)
        other = jnp.concatenate([halves[:, 1:], -halves[:, :1]], 1).reshape(all_rows, LANES)
        rows[:, columns] = other.astype(bf16)

    @pl.loop(0, PLANE // LANES)
    def _(step):
        columns = pl.ds(pl.multiple_of(step * LANES, LANES), LANES)
        waves = matmul(turned[...], cos_ref[:, columns]) + matmul(rows[...], sin_ref[:, columns])
        planes[:all_rows, columns] = waves.astype(bf16)

    for start in range(0, NGRID * PLANE, piece):
        owner, offset = start // local_g, start % local_g
        x, column = start // PLANE, start % PLANE
        out_ref[owner, 0, :, offset : offset + piece] = planes[
            x * band_rows : (x + 1) * band_rows, column : column + piece
        ]


def apply_potential(waves, tables, grid_potential):
    parts, band_count, _, local_g = waves.shape
    steps = band_count // GROUP
    band_rows = 2 * GROUP
    all_rows = NGRID * band_rows
    whole = lambda step: (0, 0)
    return pl.pallas_call(
        potential_kernel,
        grid=(steps,),
        in_specs=[
            pl.BlockSpec((parts, GROUP, 2, local_g), lambda step: (0, step, 0, 0)),
            pl.BlockSpec((PLANE, PLANE), whole),
            pl.BlockSpec((PLANE, PLANE), whole),
            pl.BlockSpec((all_rows, 2 * all_rows), whole),
            pl.BlockSpec((all_rows, all_rows), whole),
            pl.BlockSpec((NGRID, PLANE), whole),
        ],
        out_specs=pl.BlockSpec((parts, 1, band_rows, local_g), lambda step: (0, step, 0, 0)),
        out_shape=jax.ShapeDtypeStruct((parts, steps, band_rows, local_g), bf16),
        scratch_shapes=[
            pltpu.VMEM((all_rows, PLANE), bf16),
            pltpu.VMEM((2 * all_rows, PLANE), bf16),
            pltpu.VMEM((all_rows, PLANE), bf16),
        ],
        compiler_params=pltpu.CompilerParams(vmem_limit_bytes=VMEM_BYTES),
        cost_estimate=pl.CostEstimate(
            flops=steps * 2 * all_rows * PLANE * (4 * PLANE + 3 * all_rows),
            bytes_accessed=8 * steps * band_rows * parts * local_g + 8 * PLANE * PLANE,
            transcendentals=0,
        ),
    )(waves, *tables, grid_potential)


def trial_kernel(count, base_ref, *refs):
    potentials, (trial_ref, margin_ref, even, odd) = refs[:count], refs[count:]
    step = pl.program_id(0)
    bands = base_ref.shape[1]
    share = bands // count

    for chunk in range(count):
        block = potentials[chunk][...].astype(f32) * step_size
        block = block.reshape(share // GROUP, 2, GROUP, block.shape[1])
        inside = slice(chunk * share, (chunk + 1) * share)
        for half in range(2):
            taken = block[:, half].reshape(share, block.shape[3])
            trial_ref[half, inside, :] = (base_ref[half, inside, :] - taken).astype(bf16)
    real, imag = trial_ref[0], trial_ref[1]

    @pl.when(step == 0)
    def _():
        even[...] = jnp.zeros_like(even)
        odd[...] = jnp.zeros_like(odd)

    even[...] += inner(real, real) + inner(imag, imag)
    odd[...] += inner(imag, real)

    @pl.when(step == pl.num_programs(0) - 1)
    def _():
        across = odd[...]
        row = lax.broadcasted_iota(jnp.int32, even.shape, 0)
        column = lax.broadcasted_iota(jnp.int32, even.shape, 1)
        packed = jnp.where(row <= column, even[...], across - across.T)
        margin_ref[...] = (packed * (1.0 / GVECS)).astype(bf16)


def make_trial(base, potentials):
    _, bands, local_g = base.shape
    count = len(potentials)
    width = min(LANES, local_g)
    return pl.pallas_call(
        functools.partial(trial_kernel, count),
        grid=(local_g // width,),
        in_specs=[pl.BlockSpec((2, bands, width), lambda step: (0, 0, step))]
        + [pl.BlockSpec((2 * bands // count, width), lambda step: (0, step))] * count,
        out_specs=[
            pl.BlockSpec((2, bands, width), lambda step: (0, 0, step)),
            pl.BlockSpec((bands, bands), lambda step: (0, 0)),
        ],
        out_shape=[
            jax.ShapeDtypeStruct((2, bands, local_g), bf16),
            jax.ShapeDtypeStruct((bands, bands), bf16),
        ],
        scratch_shapes=[pltpu.VMEM((bands, bands), f32)] * 2,
        compiler_params=pltpu.CompilerParams(vmem_limit_bytes=VMEM_BYTES),
        cost_estimate=pl.CostEstimate(
            flops=6 * bands * bands * local_g,
            bytes_accessed=16 * bands * local_g,
            transcendentals=0,
        ),
    )(base, *potentials)


def update_kernel(mixer_ref, trial_ref, out_ref, even, odd):
    @pl.when(pl.program_id(0) == 0)
    def _():
        packed = mixer_ref[...].astype(f32)
        flipped = packed.T
        row = lax.broadcasted_iota(jnp.int32, packed.shape, 0)
        column = lax.broadcasted_iota(jnp.int32, packed.shape, 1)
        even[...] = jnp.where(row <= column, packed, flipped).astype(bf16)
        above = jnp.where(row == column, 0.0, -flipped)
        odd[...] = jnp.where(row > column, packed, above).astype(bf16)

    real, imag = trial_ref[0], trial_ref[1]
    out_ref[:, 0, :] = (matmul(even[...], real) - matmul(odd[...], imag)).astype(bf16)
    out_ref[:, 1, :] = (matmul(even[...], imag) + matmul(odd[...], real)).astype(bf16)


def update_waves(mixer, trial):
    _, bands, local_g = trial.shape
    width = min(LANES, local_g)
    return pl.pallas_call(
        update_kernel,
        grid=(local_g // width,),
        in_specs=[
            pl.BlockSpec((bands, bands), lambda step: (0, 0)),
            pl.BlockSpec((2, bands, width), lambda step: (0, 0, step)),
        ],
        out_specs=pl.BlockSpec((bands, 2, width), lambda step: (0, 0, step)),
        out_shape=jax.ShapeDtypeStruct((bands, 2, local_g), bf16),
        scratch_shapes=[pltpu.VMEM((bands, bands), bf16)] * 2,
        compiler_params=pltpu.CompilerParams(vmem_limit_bytes=VMEM_BYTES),
        cost_estimate=pl.CostEstimate(
            flops=8 * bands * bands * local_g,
            bytes_accessed=8 * bands * local_g,
            transcendentals=0,
        ),
    )(mixer, trial)


def per_device(positions, weights, psi, vloc):
    parts = lax.axis_size("ga")
    bands = psi.shape[1]
    local_g = psi.shape[3]

    weight_float = weights.astype(jnp.float32)
    mixing = weight_float / jnp.sum(weight_float, axis=1, keepdims=True)
    own_oxygens = jnp.einsum("cj,jan->can", mixing, positions[:, :, 0::3], precision=highest)[0]
    everyone = exchange(jnp.broadcast_to(own_oxygens[None], (parts,) + own_oxygens.shape))
    oxygens = jnp.swapaxes(everyone, 0, 1).reshape(3, WATERS)

    count = 2 if bands // parts % (2 * GROUP) == 0 else 1
    share = bands // count
    tables = transform_tables()
    grid_potential = vloc[0].reshape(NGRID, PLANE) * (1.0 / GVECS)
    potentials = []
    for chunk in range(count):
        sent = psi[0, chunk * share : (chunk + 1) * share].reshape(
            parts, share // parts, 2, local_g
        )
        moved = apply_potential(exchange(sent), tables, grid_potential)
        potentials.append(exchange(moved).reshape(2 * share, local_g))

    flat_index = lax.axis_index("ga") * local_g + jnp.arange(local_g, dtype=jnp.int32)
    gvectors = jnp.stack(
        [
            frequency(flat_index // (NGRID * NGRID), NGRID),
            frequency(flat_index // NGRID % NGRID, NGRID),
            frequency(flat_index % NGRID, NGRID),
        ]
    )
    square = jnp.sum(gvectors * gvectors, axis=0)
    profile = jnp.exp(-0.5 * width_square * square)
    kinetic = 0.5 * square
    phases = jnp.einsum("ai,ag->ig", oxygens, gvectors, precision=highest)
    wave_cos = profile * jnp.cos(phases)
    wave_sin = profile * jnp.sin(phases)
    table = jnp.concatenate(
        [jnp.concatenate([wave_cos, -wave_sin], 1), jnp.concatenate([wave_sin, wave_cos], 1)], 0
    ).astype(bf16)
    planes = jnp.swapaxes(psi[0], 0, 1)
    real_part, imag_part = planes[0], planes[1]
    partial_proj = (
        inner(table[:, :local_g], real_part) + inner(table[:, local_g:], imag_part)
    ) * (1.0 / GVECS)
    all_proj = lax.psum(partial_proj, "ga").astype(bf16)
    nonlocal_term = lax.dot_general(
        all_proj, table, (((0,), (0,)), ((), ())), preferred_element_type=jnp.float32
    )
    proj_re, proj_im = all_proj[:WATERS], all_proj[WATERS:]
    weighted_re = matmul(proj_re, real_part) + matmul(proj_im, imag_part)
    weighted_im = matmul(proj_re, imag_part) - matmul(proj_im, real_part)
    mixed_wave = wave_cos * weighted_im + wave_sin * weighted_re
    force_part = (
        2.0
        * occupation
        * nonlocal_strength
        / GVECS
        * jnp.einsum("ag,ig->ai", gvectors, mixed_wave, precision=highest)
    )
    force_blocks = jnp.swapaxes(force_part.reshape(3, parts, WATERS // parts), 0, 1)
    oxygen_force = jnp.sum(exchange(force_blocks), axis=0)
    hydrogen_zero = jnp.zeros_like(oxygen_force)
    dft_force = jnp.stack([oxygen_force, hydrogen_zero, hydrogen_zero], axis=2).reshape(1, 3, -1)

    pulled = jnp.stack([nonlocal_term[:, :local_g], nonlocal_term[:, local_g:]])
    wave_float = planes.astype(jnp.float32)
    base = wave_float - step_size * (kinetic * wave_float + nonlocal_strength * pulled)

    trial, margin = make_trial(base, potentials)
    rows = bands // parts
    summed = jnp.sum(exchange(margin.reshape(parts, rows, bands)).astype(jnp.float32), axis=0)
    row = lax.axis_index("ga") * rows + lax.broadcasted_iota(jnp.int32, (rows, bands), 0)
    column = lax.broadcasted_iota(jnp.int32, (rows, bands), 1)
    own_mixer = (jnp.where(row == column, 1.5, 0.0) - 0.5 * summed).astype(bf16)
    mixer = lax.all_gather(own_mixer, "ga", axis=0, tiled=True)
    psi_new = update_waves(mixer, trial)

    near_forces = field_forces(positions)
    contracted_force = jnp.einsum("cj,can->jan", mixing, dft_force, precision=highest)
    bead_forces = near_forces + BEADS / CBEADS * contracted_force
    return (psi_new[None], bead_forces)


def solution(mesh):
    placed = (P("rep", None, "ga"), P(), P("rep", None, None, "ga"), P("rep", None))
    return jax.shard_map(
        per_device,
        mesh=mesh,
        in_specs=placed,
        out_specs=(P("rep", None, None, "ga"), P("rep", None, "ga")),
        check_vma=False,
    )
```

```python
import functools

import jax
import jax.numpy as jnp
import numpy as np
from jax import lax
from jax.experimental import pallas as pl
from jax.experimental.pallas import tpu as pltpu
from jax.sharding import PartitionSpec as P

BEADS = 32
CBEADS = 1
WATERS = 256
NGRID = 32
GVECS = 32768


box_length = 20.0
bond_stiff = 0.5
bond_rest = 1.8
spring_stiff = 2.0
width_square = 0.09
step_size = 0.02
nonlocal_strength = 250.0
occupation = 2.0
highest = lax.Precision.HIGHEST
bf16 = jnp.bfloat16
f32 = jnp.float32

PLANE = NGRID * NGRID
GROUP = 8
SLAB = 128
LANES = 256
VMEM_BYTES = 56 * 2**20


def frequency(index, count):
    signed = jnp.where(index < count // 2, index, index - count)
    return signed.astype(jnp.float32) * (2.0 * jnp.pi / box_length)


def field_forces(positions):
    oxygen = positions[:, :, 0::3]
    toward_one = positions[:, :, 1::3] - oxygen
    toward_two = positions[:, :, 2::3] - oxygen

    def stretch(offset):
        length = jnp.sqrt(jnp.sum(offset * offset, axis=1, keepdims=True))
        return -bond_stiff * (length - bond_rest) * offset / length

    pull_one = stretch(toward_one)
    pull_two = stretch(toward_two)
    bonds = jnp.stack([-(pull_one + pull_two), pull_one, pull_two], axis=3).reshape(positions.shape)
    springs = 2.0 * positions - jnp.roll(positions, 1, axis=0) - jnp.roll(positions, -1, axis=0)
    return bonds - spring_stiff * springs


def inner(left_mat, right_mat):
    return lax.dot_general(
        left_mat, right_mat, (((1,), (1,)), ((), ())), preferred_element_type=jnp.float32
    )


def matmul(left_mat, right_mat):
    return jnp.dot(left_mat, right_mat, preferred_element_type=jnp.float32)


def exchange(blocks, groups=None):
    return lax.all_to_all(
        blocks, "ga", split_axis=0, concat_axis=0, tiled=True, axis_index_groups=groups
    )


def other_core(block, parts):
    return lax.ppermute(block, "ga", [(device, device ^ 1) for device in range(parts)])


def transform_tables():
    index = np.arange(PLANE)
    first, second = index // NGRID, index % NGRID
    product = (first[:, None] * first[None, :] + second[:, None] * second[None, :]) % NGRID
    angle = product * (2.0 * np.pi / NGRID)
    line = np.arange(NGRID)
    x_angle = (line[:, None] * line[None, :] % NGRID) * (2.0 * np.pi / NGRID)
    cosine, sine = np.cos(x_angle), np.sin(x_angle)
    same = np.eye(GROUP)
    rows = 2 * NGRID * GROUP

    def spread(mixing, order):
        return np.einsum("xycd,bm->" + order, mixing, same).reshape(rows, rows)

    def mixed(rr, ri, ir, ii):
        return np.stack([np.stack([rr, ri], -1), np.stack([ir, ii], -1)], -2)

    on_cosine = spread(mixed(cosine, -sine, sine, cosine), "xcbymd")
    on_sine = spread(mixed(-sine, -cosine, cosine, -sine), "xcbymd")
    backward = np.concatenate([on_cosine, on_sine], 1)
    forward = spread(mixed(cosine, sine, -sine, cosine), "xcbydm")
    return [
        jnp.asarray(table.astype(np.float32), dtype=bf16)
        for table in (np.cos(angle), np.sin(angle), backward, forward)
    ]


def cosine_and_sine(phases):
    turns = jnp.round(phases * (0.5 / np.pi))
    left = (phases - turns * 6.28125) - turns * (2.0 * np.pi - 6.28125)
    quarter = left * 0.25
    square = quarter * quarter
    sine = 1.0 + square * (
        -1.0 / 6 + square * (1.0 / 120 + square * (-1.0 / 5040 + square * (1.0 / 362880)))
    )
    sine = quarter * sine
    versine = square * (
        0.5
        + square
        * (-1.0 / 24 + square * (1.0 / 720 + square * (-1.0 / 40320 + square * (1.0 / 3628800))))
    )
    for _ in range(2):
        sine, versine = 2.0 * sine * (1.0 - versine), 2.0 * sine * sine
    return 1.0 - versine, sine


def projector_tables(oxygens):
    line = frequency(jnp.arange(NGRID, dtype=jnp.int32), NGRID)
    second, third = jnp.repeat(line, NGRID), jnp.tile(line, NGRID)
    envelope = jnp.exp(-0.5 * width_square * (second * second + third * third))
    cosine, sine = cosine_and_sine(
        oxygens[1][:, None] * second[None, :] + oxygens[2][:, None] * third[None, :]
    )
    in_plane = jnp.concatenate([envelope * cosine, envelope * sine], 0)
    in_plane = jnp.concatenate([in_plane, second * in_plane, third * in_plane], 0).astype(bf16)
    envelope = jnp.exp(-0.5 * width_square * line * line)[:, None]
    cosine, sine = cosine_and_sine(line[:, None] * oxygens[0][None, :])
    cosine, sine = envelope * cosine, envelope * sine
    along = jnp.stack([cosine, sine, line[:, None] * cosine, line[:, None] * sine])
    return in_plane, along


def wave_kernel(
    wave_ref,
    cos_ref,
    sin_ref,
    back_ref,
    fore_ref,
    pot_ref,
    in_plane_ref,
    along_ref,
    out_ref,
    force_ref,
    rows,
    planes,
    turned,
    sums,
    pulls,
):
    parts, local_g = wave_ref.shape[0], wave_ref.shape[3]
    waters = along_ref.shape[2]
    band_rows = 2 * GROUP
    all_rows = NGRID * band_rows
    piece = min(local_g, PLANE)
    for start in range(0, NGRID * PLANE, piece):
        owner, offset = start // local_g, start % local_g
        x, column = start // PLANE, start % PLANE
        block = wave_ref[owner, :, :, offset : offset + piece]
        rows[x * band_rows : (x + 1) * band_rows, column : column + piece] = block.reshape(
            band_rows, piece
        )

    @pl.loop(0, sums.shape[0] // 2)
    def _(step):
        columns = pl.ds(pl.multiple_of(step * 2 * SLAB, 2 * SLAB), 2 * SLAB)
        found = inner(rows[...], in_plane_ref[columns, :])
        sums[2 * step] = found[:, :SLAB]
        sums[2 * step + 1] = found[:, SLAB:]

    @pl.when(pl.program_id(0) == 0)
    def _():
        force_ref[...] = jnp.zeros_like(force_ref)

    slabs = waters // SLAB
    real, imag = (pl.ds(first, all_rows // 2, stride=2) for first in range(2))
    shape = (NGRID, GROUP, SLAB)
    for slab in range(slabs):
        inside = slice(slab * SLAB, (slab + 1) * SLAB)
        factors = [along_ref[which, :, inside][:, None, :] for which in range(4)]

        def planewise(factor):
            first = 2 * factor * slabs + slab
            second = first + slabs
            found_re = sums[first, real, :] - sums[second, imag, :]
            found_im = sums[second, real, :] + sums[first, imag, :]
            return found_re.reshape(shape), found_im.reshape(shape)

        def over_x(found, cosines, sines):
            return (
                jnp.sum(found[0] * cosines - found[1] * sines, axis=0),
                jnp.sum(found[0] * sines + found[1] * cosines, axis=0),
            )

        plain = planewise(0)
        proj_re, proj_im = over_x(plain, *factors[:2])
        proj_re = (proj_re * (1.0 / GVECS)).astype(bf16).astype(f32)
        proj_im = (proj_im * (1.0 / GVECS)).astype(bf16).astype(f32)
        for axis in range(3):
            if axis == 0:
                slope_re, slope_im = over_x(plain, *factors[2:])
            else:
                slope_re, slope_im = over_x(planewise(axis), *factors[:2])
            force_ref[axis, :, inside] += proj_re * slope_im - proj_im * slope_re

        cosines, sines = factors[:2]
        pull_re = nonlocal_strength * (cosines * proj_re[None] + sines * proj_im[None])
        pull_im = nonlocal_strength * (cosines * proj_im[None] - sines * proj_re[None])
        for half, pull in enumerate(((pull_re, pull_im), (pull_im, -pull_re))):
            both = jnp.concatenate(pull, 1).reshape(all_rows, SLAB).astype(bf16)
            start = half * waters + slab * SLAB
            pulls[:, start : start + SLAB] = both

    @pl.loop(0, PLANE // LANES)
    def _(step):
        columns = pl.ds(pl.multiple_of(step * LANES, LANES), LANES)
        planes[:all_rows, columns] = matmul(rows[...], cos_ref[:, columns]).astype(bf16)
        planes[all_rows:, columns] = matmul(rows[...], sin_ref[:, columns]).astype(bf16)

    @pl.loop(0, PLANE // LANES)
    def _(step):
        columns = pl.ds(pl.multiple_of(step * LANES, LANES), LANES)
        space = matmul(back_ref[...], planes[:, columns]).reshape(NGRID, band_rows, LANES)
        space = space * pot_ref[:, columns][:, None, :]
        space = space.reshape(all_rows, LANES).astype(bf16)
        waves = matmul(fore_ref[...], space)
        turned[:, columns] = waves.astype(bf16)
        halves = waves.reshape(NGRID, 2, GROUP, LANES)
        other = jnp.concatenate([halves[:, 1:], -halves[:, :1]], 1).reshape(all_rows, LANES)
        rows[:, columns] = other.astype(bf16)

    @pl.loop(0, PLANE // LANES)
    def _(step):
        columns = pl.ds(pl.multiple_of(step * LANES, LANES), LANES)
        waves = matmul(turned[...], cos_ref[:, columns]) + matmul(rows[...], sin_ref[:, columns])
        waves += matmul(pulls[...], in_plane_ref[: 2 * waters, columns])
        planes[:all_rows, columns] = waves.astype(bf16)

    for start in range(0, NGRID * PLANE, piece):
        owner, offset = start // local_g, start % local_g
        x, column = start // PLANE, start % PLANE
        out_ref[owner, 0, :, offset : offset + piece] = planes[
            x * band_rows : (x + 1) * band_rows, column : column + piece
        ]


def apply_hamiltonian(waves, tables, grid_potential, in_plane, along):
    parts, band_count, _, local_g = waves.shape
    waters = along.shape[2]
    steps = band_count // GROUP
    band_rows = 2 * GROUP
    all_rows = NGRID * band_rows
    whole = lambda step: (0, 0)
    return pl.pallas_call(
        wave_kernel,
        grid=(steps,),
        in_specs=[
            pl.BlockSpec((parts, GROUP, 2, local_g), lambda step: (0, step, 0, 0)),
            pl.BlockSpec((PLANE, PLANE), whole),
            pl.BlockSpec((PLANE, PLANE), whole),
            pl.BlockSpec((all_rows, 2 * all_rows), whole),
            pl.BlockSpec((all_rows, all_rows), whole),
            pl.BlockSpec((NGRID, PLANE), whole),
            pl.BlockSpec((6 * waters, PLANE), whole),
            pl.BlockSpec((4, NGRID, waters), lambda step: (0, 0, 0)),
        ],
        out_specs=[
            pl.BlockSpec((parts, 1, band_rows, local_g), lambda step: (0, step, 0, 0)),
            pl.BlockSpec((3, GROUP, waters), lambda step: (0, 0, 0)),
        ],
        out_shape=[
            jax.ShapeDtypeStruct((parts, steps, band_rows, local_g), bf16),
            jax.ShapeDtypeStruct((3, GROUP, waters), f32),
        ],
        scratch_shapes=[
            pltpu.VMEM((all_rows, PLANE), bf16),
            pltpu.VMEM((2 * all_rows, PLANE), bf16),
            pltpu.VMEM((all_rows, PLANE), bf16),
            pltpu.VMEM((6 * waters // SLAB, all_rows, SLAB), f32),
            pltpu.VMEM((all_rows, 2 * waters), bf16),
        ],
        compiler_params=pltpu.CompilerParams(vmem_limit_bytes=VMEM_BYTES),
        cost_estimate=pl.CostEstimate(
            flops=steps * 2 * all_rows * PLANE * (4 * PLANE + 3 * all_rows + 8 * waters),
            bytes_accessed=8 * steps * band_rows * parts * local_g + 8 * PLANE * PLANE,
            transcendentals=0,
        ),
    )(waves, *tables, grid_potential, in_plane, along)


def trial_kernel(count, core_ref, kinetic_ref, planes_ref, *refs):
    potentials, (trial_ref, mine_ref, other_ref, even, odd) = refs[:count], refs[count:]
    step = pl.program_id(0)
    bands = planes_ref.shape[1]
    share = bands // count
    kept = 1.0 - step_size * kinetic_ref[...]

    for chunk in range(count):
        block = potentials[chunk][...].astype(f32) * step_size
        block = block.reshape(share // GROUP, 2, GROUP, block.shape[1])
        inside = slice(chunk * share, (chunk + 1) * share)
        for half in range(2):
            taken = block[:, half].reshape(share, block.shape[3])
            wave = planes_ref[half, inside, :].astype(f32)
            trial_ref[half, inside, :] = (wave * kept - taken).astype(bf16)
    real, imag = trial_ref[0], trial_ref[1]

    @pl.when(step == 0)
    def _():
        even[...] = jnp.zeros_like(even)
        odd[...] = jnp.zeros_like(odd)

    even[...] += inner(real, real) + inner(imag, imag)
    odd[...] += inner(imag, real)

    @pl.when(step == pl.num_programs(0) - 1)
    def _():
        across = odd[...]
        row = lax.broadcasted_iota(jnp.int32, even.shape, 0)
        column = lax.broadcasted_iota(jnp.int32, even.shape, 1)
        packed = jnp.where(row <= column, even[...], across - across.T)
        even[...] = packed * (1.0 / GVECS)
        half = bands // 2
        core = core_ref[0]
        mine_ref[...] = even[pl.ds(pl.multiple_of(core * half, half), half), :]
        others = even[pl.ds(pl.multiple_of((1 - core) * half, half), half), :]
        other_ref[...] = others.astype(bf16)


def make_trial(core, kinetic, planes, potentials):
    _, bands, local_g = planes.shape
    count = len(potentials)
    width = min(LANES, local_g)
    return pl.pallas_call(
        functools.partial(trial_kernel, count),
        grid=(local_g // width,),
        in_specs=[
            pl.BlockSpec(memory_space=pltpu.SMEM),
            pl.BlockSpec((1, width), lambda step: (0, step)),
            pl.BlockSpec((2, bands, width), lambda step: (0, 0, step)),
        ]
        + [pl.BlockSpec((2 * bands // count, width), lambda step: (0, step))] * count,
        out_specs=[
            pl.BlockSpec((2, bands, width), lambda step: (0, 0, step)),
            pl.BlockSpec((bands // 2, bands), lambda step: (0, 0)),
            pl.BlockSpec((bands // 2, bands), lambda step: (0, 0)),
        ],
        out_shape=[
            jax.ShapeDtypeStruct((2, bands, local_g), bf16),
            jax.ShapeDtypeStruct((bands // 2, bands), f32),
            jax.ShapeDtypeStruct((bands // 2, bands), bf16),
        ],
        scratch_shapes=[pltpu.VMEM((bands, bands), f32)] * 2,
        compiler_params=pltpu.CompilerParams(vmem_limit_bytes=VMEM_BYTES),
        cost_estimate=pl.CostEstimate(
            flops=6 * bands * bands * local_g,
            bytes_accessed=12 * bands * local_g,
            transcendentals=0,
        ),
    )(core, kinetic, planes, *potentials)


def update_kernel(core_ref, mine_ref, other_ref, trial_ref, out_ref, even, odd):
    @pl.when(pl.program_id(0) == 0)
    def _():
        mine, others = mine_ref[...].astype(f32), other_ref[...].astype(f32)
        first = core_ref[0] == 0
        packed = jnp.concatenate(
            [jnp.where(first, mine, others), jnp.where(first, others, mine)], 0
        )
        flipped = packed.T
        row = lax.broadcasted_iota(jnp.int32, packed.shape, 0)
        column = lax.broadcasted_iota(jnp.int32, packed.shape, 1)
        even[...] = jnp.where(row <= column, packed, flipped).astype(bf16)
        above = jnp.where(row == column, 0.0, -flipped)
        odd[...] = jnp.where(row > column, packed, above).astype(bf16)

    real, imag = trial_ref[0], trial_ref[1]
    out_ref[:, 0, :] = (matmul(even[...], real) - matmul(odd[...], imag)).astype(bf16)
    out_ref[:, 1, :] = (matmul(even[...], imag) + matmul(odd[...], real)).astype(bf16)


def update_waves(core, mine, others, trial):
    _, bands, local_g = trial.shape
    width = min(LANES, local_g)
    return pl.pallas_call(
        update_kernel,
        grid=(local_g // width,),
        in_specs=[
            pl.BlockSpec(memory_space=pltpu.SMEM),
            pl.BlockSpec((bands // 2, bands), lambda step: (0, 0)),
            pl.BlockSpec((bands // 2, bands), lambda step: (0, 0)),
            pl.BlockSpec((2, bands, width), lambda step: (0, 0, step)),
        ],
        out_specs=pl.BlockSpec((bands, 2, width), lambda step: (0, 0, step)),
        out_shape=jax.ShapeDtypeStruct((bands, 2, local_g), bf16),
        scratch_shapes=[pltpu.VMEM((bands, bands), bf16)] * 2,
        compiler_params=pltpu.CompilerParams(vmem_limit_bytes=VMEM_BYTES),
        cost_estimate=pl.CostEstimate(
            flops=8 * bands * bands * local_g,
            bytes_accessed=8 * bands * local_g,
            transcendentals=0,
        ),
    )(core, mine, others, trial)


def per_device(positions, weights, psi, vloc):
    parts = lax.axis_size("ga")
    bands = psi.shape[1]
    local_g = psi.shape[3]

    weight_float = weights.astype(jnp.float32)
    mixing = weight_float / jnp.sum(weight_float, axis=1, keepdims=True)
    own_oxygens = jnp.einsum("cj,jan->can", mixing, positions[:, :, 0::3], precision=highest)[0]
    count = 2 if bands // parts % (2 * GROUP) == 0 else 1
    share = bands // count

    def outgoing(whole_psi, chunk):
        block = whole_psi[0, chunk * share : (chunk + 1) * share]
        return block.reshape(parts, share // parts, 2, local_g)

    waves = [exchange(outgoing(psi, 0))]
    later_psi, own_oxygens = lax.optimization_barrier((psi, own_oxygens))
    later = [outgoing(later_psi, chunk) for chunk in range(1, count)]
    waves[0], own_oxygens, *later = lax.optimization_barrier((waves[0], own_oxygens, *later))
    everyone = exchange(jnp.broadcast_to(own_oxygens[None], (parts,) + own_oxygens.shape))
    everyone, *later = lax.optimization_barrier((everyone, *later))
    waves += [exchange(block) for block in later]
    oxygens = jnp.swapaxes(everyone, 0, 1).reshape(3, WATERS)
    tables = transform_tables()
    in_plane, along = projector_tables(oxygens)
    grid_potential = vloc[0].reshape(NGRID, PLANE) * (1.0 / GVECS)
    potentials, forces = [], []
    for wave in waves:
        moved, force = apply_hamiltonian(wave, tables, grid_potential, in_plane, along)
        potentials.append(exchange(moved).reshape(2 * share, local_g))
        forces.append(force)
    force_part = jnp.sum(sum(forces), axis=1) * (2.0 * occupation * nonlocal_strength / GVECS)

    flat_index = lax.axis_index("ga") * local_g + jnp.arange(local_g, dtype=jnp.int32)
    square = (
        frequency(flat_index // PLANE, NGRID) ** 2
        + frequency(flat_index // NGRID % NGRID, NGRID) ** 2
        + frequency(flat_index % NGRID, NGRID) ** 2
    )
    kinetic = (0.5 * square)[None]
    planes = jnp.swapaxes(psi[0], 0, 1)

    chip, core = lax.axis_index("ga") // 2, lax.axis_index("ga") % 2
    chips = parts // 2
    same_core = [[2 * number + which for number in range(chips)] for which in range(2)]
    core_ref = core.reshape(1).astype(jnp.int32)
    trial, mine, others = make_trial(core_ref, kinetic, planes, potentials)
    rows = bands // parts
    pair = (mine + other_core(others, parts).astype(f32)).astype(bf16)
    near_chip = WATERS // chips
    pieces, left = [], force_part
    for _ in range(3):
        pieces.append(lax.reduce_precision(left, 8, 7))
        left = left - pieces[-1]
    pieces = jnp.swapaxes(jnp.stack(pieces).reshape(9, chips, near_chip), 0, 1)
    pieces = jnp.pad(pieces.reshape(chips, -1), ((0, 0), (0, GROUP * bands - 9 * near_chip)))
    sent = [pair.reshape(chips, rows, bands), pieces.reshape(chips, GROUP, bands).astype(bf16)]
    summed = jnp.sum(exchange(jnp.concatenate(sent, 1), same_core).astype(f32), axis=0)
    summed, found = summed[:rows], summed[rows:].reshape(-1)[: 9 * near_chip]
    found = jnp.sum(found.reshape(3, 3, near_chip), axis=0)
    found = (found + other_core(found, parts)).reshape(3, 2, near_chip // 2)
    oxygen_force = lax.dynamic_index_in_dim(found, core, 1, keepdims=False)
    row = (core * chips + chip) * rows + lax.broadcasted_iota(jnp.int32, (rows, bands), 0)
    column = lax.broadcasted_iota(jnp.int32, (rows, bands), 1)
    own_mixer = (jnp.where(row == column, 1.5, 0.0) - 0.5 * summed).astype(bf16)
    half_mixer = exchange(
        jnp.broadcast_to(own_mixer[None], (chips, rows, bands)), same_core
    ).reshape(bands // 2, bands)
    psi_new = update_waves(core_ref, half_mixer, other_core(half_mixer, parts), trial)

    hydrogen_zero = jnp.zeros_like(oxygen_force)
    dft_force = jnp.stack([oxygen_force, hydrogen_zero, hydrogen_zero], axis=2).reshape(1, 3, -1)

    near_forces = field_forces(positions)
    contracted_force = jnp.einsum("cj,can->jan", mixing, dft_force, precision=highest)
    bead_forces = near_forces + BEADS / CBEADS * contracted_force
    return (psi_new[None], bead_forces)


def solution(mesh):
    placed = (P("rep", None, "ga"), P(), P("rep", None, None, "ga"), P("rep", None))
    return jax.shard_map(
        per_device,
        mesh=mesh,
        in_specs=placed,
        out_specs=(P("rep", None, None, "ga"), P("rep", None, "ga")),
        check_vma=False,
    )
```

```python
import functools

import jax
import jax.numpy as jnp
import numpy as np
from jax import lax
from jax.experimental import pallas as pl
from jax.experimental.pallas import tpu as pltpu
from jax.sharding import PartitionSpec as P

BEADS = 32
CBEADS = 1
WATERS = 256
NGRID = 32
GVECS = 32768


box_length = 20.0
bond_stiff = 0.5
bond_rest = 1.8
spring_stiff = 2.0
width_square = 0.09
step_size = 0.02
nonlocal_strength = 250.0
occupation = 2.0
highest = lax.Precision.HIGHEST
bf16 = jnp.bfloat16
f32 = jnp.float32

PLANE = NGRID * NGRID
GROUP = 8
SLAB = 128
LANES = 256
WIDE = 512
VMEM_BYTES = 56 * 2**20
TAIL_VMEM_BYTES = 60 * 2**20


def frequency(index, count):
    signed = jnp.where(index < count // 2, index, index - count)
    return signed.astype(jnp.float32) * (2.0 * jnp.pi / box_length)


def field_forces(positions):
    oxygen = positions[:, :, 0::3]
    toward_one = positions[:, :, 1::3] - oxygen
    toward_two = positions[:, :, 2::3] - oxygen

    def stretch(offset):
        length = jnp.sqrt(jnp.sum(offset * offset, axis=1, keepdims=True))
        return -bond_stiff * (length - bond_rest) * offset / length

    pull_one = stretch(toward_one)
    pull_two = stretch(toward_two)
    bonds = jnp.stack([-(pull_one + pull_two), pull_one, pull_two], axis=3).reshape(positions.shape)
    springs = 2.0 * positions - jnp.roll(positions, 1, axis=0) - jnp.roll(positions, -1, axis=0)
    return bonds - spring_stiff * springs


def inner(left_mat, right_mat):
    return lax.dot_general(
        left_mat, right_mat, (((1,), (1,)), ((), ())), preferred_element_type=jnp.float32
    )


def matmul(left_mat, right_mat):
    return jnp.dot(left_mat, right_mat, preferred_element_type=jnp.float32)


def exchange(blocks, groups=None):
    return lax.all_to_all(
        blocks, "ga", split_axis=0, concat_axis=0, tiled=True, axis_index_groups=groups
    )


def other_core(block, parts):
    return lax.ppermute(block, "ga", [(device, device ^ 1) for device in range(parts)])


def transform_tables():
    index = np.arange(PLANE)
    first, second = index // NGRID, index % NGRID
    product = (first[:, None] * first[None, :] + second[:, None] * second[None, :]) % NGRID
    angle = product * (2.0 * np.pi / NGRID)
    line = np.arange(NGRID)
    x_angle = (line[:, None] * line[None, :] % NGRID) * (2.0 * np.pi / NGRID)
    cosine, sine = np.cos(x_angle), np.sin(x_angle)
    same = np.eye(GROUP)
    rows = 2 * NGRID * GROUP

    def spread(mixing, order):
        return np.einsum("xycd,bm->" + order, mixing, same).reshape(rows, rows)

    def mixed(rr, ri, ir, ii):
        return np.stack([np.stack([rr, ri], -1), np.stack([ir, ii], -1)], -2)

    on_cosine = spread(mixed(cosine, -sine, sine, cosine), "xcbymd")
    on_sine = spread(mixed(-sine, -cosine, cosine, -sine), "xcbymd")
    backward = np.concatenate([on_cosine, on_sine], 1)
    forward = spread(mixed(cosine, sine, -sine, cosine), "xcbydm")
    return [
        jnp.asarray(table.astype(np.float32), dtype=bf16)
        for table in (np.cos(angle), np.sin(angle), backward, forward)
    ]


def cosine_and_sine(phases):
    turns = jnp.round(phases * (0.5 / np.pi))
    left = (phases - turns * 6.28125) - turns * (2.0 * np.pi - 6.28125)
    quarter = left * 0.25
    square = quarter * quarter
    sine = 1.0 + square * (
        -1.0 / 6 + square * (1.0 / 120 + square * (-1.0 / 5040 + square * (1.0 / 362880)))
    )
    sine = quarter * sine
    versine = square * (
        0.5
        + square
        * (-1.0 / 24 + square * (1.0 / 720 + square * (-1.0 / 40320 + square * (1.0 / 3628800))))
    )
    for _ in range(2):
        sine, versine = 2.0 * sine * (1.0 - versine), 2.0 * sine * sine
    return 1.0 - versine, sine


def pack_kernel(positions_ref, weights_ref, psi_ref, out_ref, lanes, stage, in_sems, out_sems):
    parts, total, _, local_g = out_ref.shape
    extra = lanes.shape[0] // 2
    own = total - extra
    arrivals = [
        pltpu.make_async_copy(
            psi_ref.at[0, pl.ds(owner * own, own)],
            stage.at[owner, pl.ds(0, own)],
            in_sems.at[owner],
        )
        for owner in range(parts)
    ]
    for copy in arrivals:
        copy.start()
    weights = weights_ref[...].astype(f32)
    mixing = weights / jnp.sum(weights, axis=1, keepdims=True)
    lanes[...] = jnp.zeros_like(lanes)
    atoms = positions_ref.shape[2]
    for axis in range(3):
        left = jnp.dot(
            mixing, positions_ref[axis], precision=highest, preferred_element_type=jnp.float32
        )
        for piece in range(3):
            sent = left.astype(bf16).astype(f32)
            left = left - sent
            place = (3 * piece + axis) * SLAB
            row, column = 2 * (place // local_g), place % local_g
            lanes[row : row + 1, column : column + atoms] = sent
    for row in range(extra):
        ending = lanes[2 * row : 2 * row + 2, :].astype(bf16)
        for owner in range(parts):
            stage[owner, own + row] = ending
    departures = [
        pltpu.make_async_copy(stage.at[owner], out_ref.at[owner], out_sems.at[owner])
        for owner in range(parts)
    ]
    for arrival, departure in zip(arrivals, departures):
        arrival.wait()
        departure.start()
    for copy in departures:
        copy.wait()


def pack_first(positions, weights, psi, parts, share):
    local_g = psi.shape[3]
    beads, _, atoms = positions.shape
    extra = -(-9 * SLAB // local_g)
    return pl.pallas_call(
        pack_kernel,
        in_specs=[
            pl.BlockSpec(memory_space=pltpu.VMEM),
            pl.BlockSpec(memory_space=pltpu.VMEM),
            pl.BlockSpec(memory_space=pl.ANY),
        ],
        out_specs=pl.BlockSpec(memory_space=pl.ANY),
        out_shape=jax.ShapeDtypeStruct((parts, share // parts + extra, 2, local_g), bf16),
        scratch_shapes=[
            pltpu.VMEM((2 * extra, local_g), f32),
            pltpu.VMEM((parts, share // parts + extra, 2, local_g), bf16),
            pltpu.SemaphoreType.DMA((parts,)),
            pltpu.SemaphoreType.DMA((parts,)),
        ],
        compiler_params=pltpu.CompilerParams(vmem_limit_bytes=TAIL_VMEM_BYTES),
        cost_estimate=pl.CostEstimate(
            flops=0, bytes_accessed=8 * share * local_g, transcendentals=0
        ),
    )(jnp.swapaxes(positions, 0, 1), weights, psi)


def unpack_oxygens(rows, atoms):
    parts = rows.shape[0]
    pieces = rows.reshape(parts, -1)[:, : 9 * SLAB].reshape(parts, 3, 3, SLAB)
    found = jnp.sum(pieces[..., 0:atoms:3].astype(f32), axis=1)
    return jnp.swapaxes(found, 0, 1).reshape(3, -1)


def projector_tables(oxygens):
    line = frequency(jnp.arange(NGRID, dtype=jnp.int32), NGRID)
    second, third = jnp.repeat(line, NGRID), jnp.tile(line, NGRID)
    envelope = jnp.exp(-0.5 * width_square * (second * second + third * third))
    cosine, sine = cosine_and_sine(
        oxygens[1][:, None] * second[None, :] + oxygens[2][:, None] * third[None, :]
    )
    in_plane = jnp.concatenate([envelope * cosine, envelope * sine], 0)
    in_plane = jnp.concatenate([in_plane, second * in_plane, third * in_plane], 0).astype(bf16)
    envelope = jnp.exp(-0.5 * width_square * line * line)[:, None]
    cosine, sine = cosine_and_sine(line[:, None] * oxygens[0][None, :])
    cosine, sine = envelope * cosine, envelope * sine
    along = jnp.stack([cosine, sine, line[:, None] * cosine, line[:, None] * sine])
    return in_plane, along


def wave_kernel(
    wave_ref,
    cos_ref,
    sin_ref,
    back_ref,
    fore_ref,
    pot_ref,
    in_plane_ref,
    along_ref,
    out_ref,
    force_ref,
    rows,
    planes,
    turned,
    sums,
    pulls,
):
    parts, local_g = wave_ref.shape[0], wave_ref.shape[3]
    waters = along_ref.shape[2]
    band_rows = 2 * GROUP
    all_rows = NGRID * band_rows
    piece = min(local_g, PLANE)
    for start in range(0, NGRID * PLANE, piece):
        owner, offset = start // local_g, start % local_g
        x, column = start // PLANE, start % PLANE
        block = wave_ref[owner, :, :, offset : offset + piece]
        rows[x * band_rows : (x + 1) * band_rows, column : column + piece] = block.reshape(
            band_rows, piece
        )

    @pl.loop(0, sums.shape[0] // 2)
    def _(step):
        columns = pl.ds(pl.multiple_of(step * 2 * SLAB, 2 * SLAB), 2 * SLAB)
        found = inner(rows[...], in_plane_ref[columns, :])
        sums[2 * step] = found[:, :SLAB]
        sums[2 * step + 1] = found[:, SLAB:]

    @pl.when(pl.program_id(0) == 0)
    def _():
        force_ref[...] = jnp.zeros_like(force_ref)

    slabs = waters // SLAB
    real, imag = (pl.ds(first, all_rows // 2, stride=2) for first in range(2))
    shape = (NGRID, GROUP, SLAB)
    for slab in range(slabs):
        inside = slice(slab * SLAB, (slab + 1) * SLAB)
        factors = [along_ref[which, :, inside][:, None, :] for which in range(4)]

        def planewise(factor):
            first = 2 * factor * slabs + slab
            second = first + slabs
            found_re = sums[first, real, :] - sums[second, imag, :]
            found_im = sums[second, real, :] + sums[first, imag, :]
            return found_re.reshape(shape), found_im.reshape(shape)

        def over_x(found, cosines, sines):
            return (
                jnp.sum(found[0] * cosines - found[1] * sines, axis=0),
                jnp.sum(found[0] * sines + found[1] * cosines, axis=0),
            )

        plain = planewise(0)
        proj_re, proj_im = over_x(plain, *factors[:2])
        proj_re = (proj_re * (1.0 / GVECS)).astype(bf16).astype(f32)
        proj_im = (proj_im * (1.0 / GVECS)).astype(bf16).astype(f32)
        for axis in range(3):
            if axis == 0:
                slope_re, slope_im = over_x(plain, *factors[2:])
            else:
                slope_re, slope_im = over_x(planewise(axis), *factors[:2])
            force_ref[axis, :, inside] += proj_re * slope_im - proj_im * slope_re

        cosines, sines = factors[:2]
        pull_re = nonlocal_strength * (cosines * proj_re[None] + sines * proj_im[None])
        pull_im = nonlocal_strength * (cosines * proj_im[None] - sines * proj_re[None])
        for half, pull in enumerate(((pull_re, pull_im), (pull_im, -pull_re))):
            both = jnp.concatenate(pull, 1).reshape(all_rows, SLAB).astype(bf16)
            start = half * waters + slab * SLAB
            pulls[:, start : start + SLAB] = both

    @pl.loop(0, PLANE // LANES)
    def _(step):
        columns = pl.ds(pl.multiple_of(step * LANES, LANES), LANES)
        planes[:all_rows, columns] = matmul(rows[...], cos_ref[:, columns]).astype(bf16)
        planes[all_rows:, columns] = matmul(rows[...], sin_ref[:, columns]).astype(bf16)

    @pl.loop(0, PLANE // LANES)
    def _(step):
        columns = pl.ds(pl.multiple_of(step * LANES, LANES), LANES)
        space = matmul(back_ref[...], planes[:, columns]).reshape(NGRID, band_rows, LANES)
        space = space * pot_ref[:, columns][:, None, :]
        space = space.reshape(all_rows, LANES).astype(bf16)
        waves = matmul(fore_ref[...], space)
        turned[:, columns] = waves.astype(bf16)
        halves = waves.reshape(NGRID, 2, GROUP, LANES)
        other = jnp.concatenate([halves[:, 1:], -halves[:, :1]], 1).reshape(all_rows, LANES)
        rows[:, columns] = other.astype(bf16)

    @pl.loop(0, PLANE // LANES)
    def _(step):
        columns = pl.ds(pl.multiple_of(step * LANES, LANES), LANES)
        waves = matmul(turned[...], cos_ref[:, columns]) + matmul(rows[...], sin_ref[:, columns])
        waves += matmul(pulls[...], in_plane_ref[: 2 * waters, columns])
        planes[:all_rows, columns] = waves.astype(bf16)

    for start in range(0, NGRID * PLANE, piece):
        owner, offset = start // local_g, start % local_g
        x, column = start // PLANE, start % PLANE
        out_ref[owner, 0, :, offset : offset + piece] = planes[
            x * band_rows : (x + 1) * band_rows, column : column + piece
        ]


def apply_hamiltonian(waves, band_count, tables, grid_potential, in_plane, along):
    parts, _, _, local_g = waves.shape
    waters = along.shape[2]
    steps = band_count // GROUP
    band_rows = 2 * GROUP
    all_rows = NGRID * band_rows
    whole = lambda step: (0, 0)
    return pl.pallas_call(
        wave_kernel,
        grid=(steps,),
        in_specs=[
            pl.BlockSpec((parts, GROUP, 2, local_g), lambda step: (0, step, 0, 0)),
            pl.BlockSpec((PLANE, PLANE), whole),
            pl.BlockSpec((PLANE, PLANE), whole),
            pl.BlockSpec((all_rows, 2 * all_rows), whole),
            pl.BlockSpec((all_rows, all_rows), whole),
            pl.BlockSpec((NGRID, PLANE), whole),
            pl.BlockSpec((6 * waters, PLANE), whole),
            pl.BlockSpec((4, NGRID, waters), lambda step: (0, 0, 0)),
        ],
        out_specs=[
            pl.BlockSpec((parts, 1, band_rows, local_g), lambda step: (0, step, 0, 0)),
            pl.BlockSpec((3, GROUP, waters), lambda step: (0, 0, 0)),
        ],
        out_shape=[
            jax.ShapeDtypeStruct((parts, steps, band_rows, local_g), bf16),
            jax.ShapeDtypeStruct((3, GROUP, waters), f32),
        ],
        scratch_shapes=[
            pltpu.VMEM((all_rows, PLANE), bf16),
            pltpu.VMEM((2 * all_rows, PLANE), bf16),
            pltpu.VMEM((all_rows, PLANE), bf16),
            pltpu.VMEM((6 * waters // SLAB, all_rows, SLAB), f32),
            pltpu.VMEM((all_rows, 2 * waters), bf16),
        ],
        compiler_params=pltpu.CompilerParams(vmem_limit_bytes=VMEM_BYTES),
        cost_estimate=pl.CostEstimate(
            flops=steps * 2 * all_rows * PLANE * (4 * PLANE + 3 * all_rows + 8 * waters),
            bytes_accessed=8 * steps * band_rows * parts * local_g + 8 * PLANE * PLANE,
            transcendentals=0,
        ),
    )(waves, *tables, grid_potential, in_plane, along)


def trial_kernel(
    first, last, core_ref, kinetic_ref, wave_ref, potential_ref, pieces_ref, before_ref,
    margin_ref, trial_ref, mine_ref, other_ref, even, odd, packed,
):
    step = pl.program_id(0)
    share, width = wave_ref.shape[1:]
    kept = 1.0 - step_size * kinetic_ref[...]
    block = potential_ref[...].astype(f32) * step_size
    block = block.reshape(share // GROUP, 2, GROUP, width)
    for half in range(2):
        taken = block[:, half].reshape(share, width)
        trial_ref[half] = (wave_ref[half].astype(f32) * kept - taken).astype(bf16)
    real, imag = trial_ref[0], trial_ref[1]
    if first:
        all_real, all_imag = real, imag
    else:
        all_real = jnp.concatenate([before_ref[0], real], 0)
        all_imag = jnp.concatenate([before_ref[1], imag], 0)

    @pl.when(step == 0)
    def _():
        even[...] = jnp.zeros_like(even)
        odd[...] = jnp.zeros_like(odd)

    even[...] += inner(real, all_real) + inner(imag, all_imag)
    odd[...] += inner(imag, all_real) - inner(real, all_imag)

    @pl.when(step == pl.num_programs(0) - 1)
    def _():
        start = even.shape[1] - share
        row = lax.broadcasted_iota(jnp.int32, (share, share), 0)
        column = lax.broadcasted_iota(jnp.int32, (share, share), 1)
        own = jnp.where(row <= column, even[:, start:], odd[:, start:]) * (1.0 / GVECS)
        if not last:
            mine_ref[...] = own
        else:
            packed[start:, start:] = own
            if not first:
                packed[:start, :start] = margin_ref[...]
                packed[start:, :start] = odd[:, :start] * (1.0 / GVECS)
                packed[:start, start:] = even[:, :start] * (1.0 / GVECS)
            chips, rows, bands = mine_ref.shape
            rows -= GROUP
            half = chips * rows
            core = core_ref[0]
            mine = packed[pl.ds(pl.multiple_of(core * half, half), half), :]
            others = packed[pl.ds(pl.multiple_of((1 - core) * half, half), half), :]
            mine_ref[:, :rows, :] = mine.reshape(chips, rows, bands)
            mine_ref[:, rows:, :] = pieces_ref[...]
            other_ref[:, :rows, :] = others.reshape(chips, rows, bands).astype(bf16)
            other_ref[:, rows:, :] = jnp.zeros((chips, GROUP, bands), bf16)


def make_trial(chunk, count, core, kinetic, planes, potential, pieces, before, margin):
    _, bands, local_g = planes.shape
    chips = pieces.shape[0]
    share = bands // count
    first, last = chunk == 0, chunk == count - 1
    width = min(WIDE, local_g)
    deep = lambda step: (0, 0, step)
    if last:
        rows = bands // (2 * chips) + GROUP
        out_specs = [pl.BlockSpec((chips, rows, bands), lambda step: (0, 0, 0))] * 2
        out_shape = [
            jax.ShapeDtypeStruct((chips, rows, bands), f32),
            jax.ShapeDtypeStruct((chips, rows, bands), bf16),
        ]
    else:
        out_specs = [pl.BlockSpec((share, share), lambda step: (0, 0))]
        out_shape = [jax.ShapeDtypeStruct((share, share), f32)]
    operands = [core, kinetic, planes, potential]
    in_specs = [
        pl.BlockSpec(memory_space=pltpu.SMEM),
        pl.BlockSpec((1, width), lambda step: (0, step)),
        pl.BlockSpec((2, share, width), lambda step: (0, chunk, step)),
        pl.BlockSpec((2 * share, width), lambda step: (0, step)),
    ]
    if last:
        operands.append(pieces)
        in_specs.append(pl.BlockSpec(pieces.shape, lambda step: (0, 0, 0)))
    if not first:
        operands += [before, margin]
        in_specs.append(pl.BlockSpec((2, share, width), deep))
        in_specs.append(pl.BlockSpec((share, share), lambda step: (0, 0)))

    def body(core_ref, kinetic_ref, wave_ref, potential_ref, *refs):
        refs = list(refs)
        pieces_ref = refs.pop(0) if last else None
        before_ref = None if first else refs.pop(0)
        margin_ref = None if first else refs.pop(0)
        trial_ref, mine_ref = refs.pop(0), refs.pop(0)
        other_ref = refs.pop(0) if last else None
        trial_kernel(
            first, last, core_ref, kinetic_ref, wave_ref, potential_ref, pieces_ref, before_ref,
            margin_ref, trial_ref, mine_ref, other_ref, *refs,
        )

    seen = (chunk + 1) * share
    return pl.pallas_call(
        body,
        grid=(local_g // width,),
        in_specs=in_specs,
        out_specs=[pl.BlockSpec((2, share, width), deep)] + out_specs,
        out_shape=[jax.ShapeDtypeStruct((2, share, local_g), bf16)] + out_shape,
        scratch_shapes=[
            pltpu.VMEM((share, seen), f32),
            pltpu.VMEM((share, seen), f32),
            pltpu.VMEM((bands, bands), f32),
        ],
        compiler_params=pltpu.CompilerParams(vmem_limit_bytes=TAIL_VMEM_BYTES),
        cost_estimate=pl.CostEstimate(
            flops=8 * share * seen * local_g,
            bytes_accessed=12 * seen * local_g,
            transcendentals=0,
        ),
    )(*operands)


def update_kernel(count, core_ref, mine_ref, other_ref, *refs):
    trials, (out_ref, even, odd) = refs[:count], refs[count:]

    @pl.when(pl.program_id(0) == 0)
    def _():
        mine, others = mine_ref[...].astype(f32), other_ref[...].astype(f32)
        first = core_ref[0] == 0
        packed = jnp.concatenate(
            [jnp.where(first, mine, others), jnp.where(first, others, mine)], 0
        )
        share = packed.shape[0] // count
        row = lax.broadcasted_iota(jnp.int32, (share, share), 0)
        column = lax.broadcasted_iota(jnp.int32, (share, share), 1)
        spans = [slice(chunk * share, (chunk + 1) * share) for chunk in range(count)]
        for lower, down in enumerate(spans):
            own = packed[down, down]
            flipped = own.T
            even[down, down] = jnp.where(row <= column, own, flipped).astype(bf16)
            above = jnp.where(row == column, 0.0, -flipped)
            odd[down, down] = jnp.where(row > column, own, above).astype(bf16)
            for over in spans[:lower]:
                both, opposite = packed[over, down], packed[down, over]
                even[down, over] = both.astype(bf16)
                even[over, down] = both.T.astype(bf16)
                odd[down, over] = opposite.astype(bf16)
                odd[over, down] = -opposite.T.astype(bf16)

    real = jnp.concatenate([trial[0] for trial in trials], 0)
    imag = jnp.concatenate([trial[1] for trial in trials], 0)
    out_ref[:, 0, :] = (matmul(even[...], real) - matmul(odd[...], imag)).astype(bf16)
    out_ref[:, 1, :] = (matmul(even[...], imag) + matmul(odd[...], real)).astype(bf16)


def update_waves(core, mine, others, trials):
    _, share, local_g = trials[0].shape
    count = len(trials)
    bands = share * count
    width = min(WIDE, local_g)
    return pl.pallas_call(
        functools.partial(update_kernel, count),
        grid=(local_g // width,),
        in_specs=[
            pl.BlockSpec(memory_space=pltpu.SMEM),
            pl.BlockSpec((bands // 2, bands), lambda step: (0, 0)),
            pl.BlockSpec((bands // 2, bands), lambda step: (0, 0)),
        ]
        + [pl.BlockSpec((2, share, width), lambda step: (0, 0, step))] * count,
        out_specs=pl.BlockSpec((bands, 2, width), lambda step: (0, 0, step)),
        out_shape=jax.ShapeDtypeStruct((bands, 2, local_g), bf16),
        scratch_shapes=[pltpu.VMEM((bands, bands), bf16)] * 2,
        compiler_params=pltpu.CompilerParams(vmem_limit_bytes=TAIL_VMEM_BYTES),
        cost_estimate=pl.CostEstimate(
            flops=8 * bands * bands * local_g,
            bytes_accessed=8 * bands * local_g,
            transcendentals=0,
        ),
    )(core, mine, others, *trials)


def per_device(positions, weights, psi, vloc):
    parts = lax.axis_size("ga")
    bands = psi.shape[1]
    local_g = psi.shape[3]

    weight_float = weights.astype(jnp.float32)
    mixing = weight_float / jnp.sum(weight_float, axis=1, keepdims=True)
    count = 2 if bands // parts % (2 * GROUP) == 0 else 1
    share = bands // count

    sent = pack_first(positions, weights, psi, parts, share)
    waves = [exchange(sent)]
    for chunk in range(1, count):
        block = psi[0, chunk * share : (chunk + 1) * share]
        waves.append(exchange(block.reshape(parts, share // parts, 2, local_g)))
    oxygens = unpack_oxygens(waves[0][:, share // parts :, 0, :], positions.shape[2])
    tables = transform_tables()
    in_plane, along = projector_tables(oxygens)
    grid_potential = vloc[0].reshape(NGRID, PLANE) * (1.0 / GVECS)
    potentials, forces = [], []
    for wave in waves:
        moved, force = apply_hamiltonian(
            wave, share // parts, tables, grid_potential, in_plane, along
        )
        potentials.append(exchange(moved).reshape(2 * share, local_g))
        forces.append(force)
    force_part = jnp.sum(sum(forces), axis=1) * (2.0 * occupation * nonlocal_strength / GVECS)

    flat_index = lax.axis_index("ga") * local_g + jnp.arange(local_g, dtype=jnp.int32)
    square = (
        frequency(flat_index // PLANE, NGRID) ** 2
        + frequency(flat_index // NGRID % NGRID, NGRID) ** 2
        + frequency(flat_index % NGRID, NGRID) ** 2
    )
    kinetic = (0.5 * square)[None]
    planes = jnp.swapaxes(psi[0], 0, 1)

    chip, core = lax.axis_index("ga") // 2, lax.axis_index("ga") % 2
    chips = parts // 2
    rows = bands // parts
    same_core = [[2 * number + which for number in range(chips)] for which in range(2)]
    core_ref = core.reshape(1).astype(jnp.int32)
    near_chip = WATERS // chips
    pieces, left = [], force_part
    for _ in range(3):
        pieces.append(lax.reduce_precision(left, 8, 7))
        left = left - pieces[-1]
    pieces = jnp.swapaxes(jnp.stack(pieces).reshape(9, chips, near_chip), 0, 1)
    pieces = jnp.pad(pieces.reshape(chips, -1), ((0, 0), (0, GROUP * bands - 9 * near_chip)))
    pieces = pieces.reshape(chips, GROUP, bands)
    trials, margin = [], None
    for chunk, potential in enumerate(potentials):
        before = trials[-1] if trials else None
        trial, margin, *others = make_trial(
            chunk, count, core_ref, kinetic, planes, potential, pieces, before, margin
        )
        trials.append(trial)
    pair = (margin + other_core(others[0], parts).astype(f32)).astype(bf16)
    summed = jnp.sum(exchange(pair, same_core).astype(f32), axis=0)
    summed, found = summed[:rows], summed[rows:].reshape(-1)[: 9 * near_chip]
    found = jnp.sum(found.reshape(3, 3, near_chip), axis=0)
    found = (found + other_core(found, parts)).reshape(3, 2, near_chip // 2)
    oxygen_force = lax.dynamic_index_in_dim(found, core, 1, keepdims=False)
    row = (core * chips + chip) * rows + lax.broadcasted_iota(jnp.int32, (rows, bands), 0)
    column = lax.broadcasted_iota(jnp.int32, (rows, bands), 1)
    own_mixer = (jnp.where(row == column, 1.5, 0.0) - 0.5 * summed).astype(bf16)
    half_mixer = exchange(
        jnp.broadcast_to(own_mixer[None], (chips, rows, bands)), same_core
    ).reshape(bands // 2, bands)
    psi_new = update_waves(core_ref, half_mixer, other_core(half_mixer, parts), trials)

    hydrogen_zero = jnp.zeros_like(oxygen_force)
    dft_force = jnp.stack([oxygen_force, hydrogen_zero, hydrogen_zero], axis=2).reshape(1, 3, -1)

    near_forces = field_forces(positions)
    contracted_force = jnp.einsum("cj,can->jan", mixing, dft_force, precision=highest)
    bead_forces = near_forces + BEADS / CBEADS * contracted_force
    return (psi_new[None], bead_forces)


def solution(mesh):
    placed = (P("rep", None, "ga"), P(), P("rep", None, None, "ga"), P("rep", None))
    return jax.shard_map(
        per_device,
        mesh=mesh,
        in_specs=placed,
        out_specs=(P("rep", None, None, "ga"), P("rep", None, "ga")),
        check_vma=False,
    )
```

```python
import functools

import jax
import jax.numpy as jnp
import numpy as np
from jax import lax
from jax.experimental import pallas as pl
from jax.experimental.pallas import tpu as pltpu
from jax.sharding import PartitionSpec as P

BEADS = 32
CBEADS = 1
WATERS = 256
NGRID = 32
GVECS = 32768


box_length = 20.0
bond_stiff = 0.5
bond_rest = 1.8
spring_stiff = 2.0
width_square = 0.09
step_size = 0.02
nonlocal_strength = 250.0
occupation = 2.0
highest = lax.Precision.HIGHEST
bf16 = jnp.bfloat16
f32 = jnp.float32

PLANE = NGRID * NGRID
GROUP = 8
SLAB = 128
LANES = 256
WIDE = 512
TRIAL_WIDE = 2048
VMEM_BYTES = 56 * 2**20
TAIL_VMEM_BYTES = 60 * 2**20
LAST_VMEM_BYTES = 28 * 2**20


def frequency(index, count):
    signed = jnp.where(index < count // 2, index, index - count)
    return signed.astype(jnp.float32) * (2.0 * jnp.pi / box_length)


def field_forces(positions):
    oxygen = positions[:, :, 0::3]
    toward_one = positions[:, :, 1::3] - oxygen
    toward_two = positions[:, :, 2::3] - oxygen

    def stretch(offset):
        length = jnp.sqrt(jnp.sum(offset * offset, axis=1, keepdims=True))
        return -bond_stiff * (length - bond_rest) * offset / length

    pull_one = stretch(toward_one)
    pull_two = stretch(toward_two)
    bonds = jnp.stack([-(pull_one + pull_two), pull_one, pull_two], axis=3).reshape(positions.shape)
    springs = 2.0 * positions - jnp.roll(positions, 1, axis=0) - jnp.roll(positions, -1, axis=0)
    return bonds - spring_stiff * springs


def inner(left_mat, right_mat):
    return lax.dot_general(
        left_mat, right_mat, (((1,), (1,)), ((), ())), preferred_element_type=jnp.float32
    )


def matmul(left_mat, right_mat):
    return jnp.dot(left_mat, right_mat, preferred_element_type=jnp.float32)


def exchange(blocks, groups=None):
    return lax.all_to_all(
        blocks, "ga", split_axis=0, concat_axis=0, tiled=True, axis_index_groups=groups
    )


def other_core(block, parts):
    return lax.ppermute(block, "ga", [(device, device ^ 1) for device in range(parts)])


def transform_tables():
    index = np.arange(PLANE)
    first, second = index // NGRID, index % NGRID
    product = (first[:, None] * first[None, :] + second[:, None] * second[None, :]) % NGRID
    angle = product * (2.0 * np.pi / NGRID)
    line = np.arange(NGRID)
    x_angle = (line[:, None] * line[None, :] % NGRID) * (2.0 * np.pi / NGRID)
    cosine, sine = np.cos(x_angle), np.sin(x_angle)
    same = np.eye(GROUP)
    rows = 2 * NGRID * GROUP

    def spread(mixing, order):
        return np.einsum("xycd,bm->" + order, mixing, same).reshape(rows, rows)

    def mixed(rr, ri, ir, ii):
        return np.stack([np.stack([rr, ri], -1), np.stack([ir, ii], -1)], -2)

    on_cosine = spread(mixed(cosine, -sine, sine, cosine), "xcbymd")
    on_sine = spread(mixed(-sine, -cosine, cosine, -sine), "xcbymd")
    backward = np.concatenate([on_cosine, on_sine], 1)
    forward = spread(mixed(cosine, sine, -sine, cosine), "xcbydm")
    return [
        jnp.asarray(table.astype(np.float32), dtype=bf16)
        for table in (np.cos(angle), np.sin(angle), backward, forward)
    ]


def cosine_and_sine(phases):
    turns = jnp.round(phases * (0.5 / np.pi))
    left = (phases - turns * 6.28125) - turns * (2.0 * np.pi - 6.28125)
    quarter = left * 0.25
    square = quarter * quarter
    sine = 1.0 + square * (
        -1.0 / 6 + square * (1.0 / 120 + square * (-1.0 / 5040 + square * (1.0 / 362880)))
    )
    sine = quarter * sine
    versine = square * (
        0.5
        + square
        * (-1.0 / 24 + square * (1.0 / 720 + square * (-1.0 / 40320 + square * (1.0 / 3628800))))
    )
    for _ in range(2):
        sine, versine = 2.0 * sine * (1.0 - versine), 2.0 * sine * sine
    return 1.0 - versine, sine


def pack_kernel(positions_ref, weights_ref, psi_ref, out_ref, lanes, stage, in_sems, out_sems):
    parts, total, _, local_g = out_ref.shape
    extra = lanes.shape[0] // 2
    own = total - extra
    arrivals = [
        pltpu.make_async_copy(
            psi_ref.at[0, pl.ds(owner * own, own)],
            stage.at[owner, pl.ds(0, own)],
            in_sems.at[owner],
        )
        for owner in range(parts)
    ]
    for copy in arrivals:
        copy.start()
    weights = weights_ref[...].astype(f32)
    mixing = weights / jnp.sum(weights, axis=1, keepdims=True)
    lanes[...] = jnp.zeros_like(lanes)
    atoms = positions_ref.shape[2]
    for axis in range(3):
        left = jnp.dot(
            mixing, positions_ref[axis], precision=highest, preferred_element_type=jnp.float32
        )
        for piece in range(3):
            sent = left.astype(bf16).astype(f32)
            left = left - sent
            place = (3 * piece + axis) * SLAB
            row, column = 2 * (place // local_g), place % local_g
            lanes[row : row + 1, column : column + atoms] = sent
    for row in range(extra):
        ending = lanes[2 * row : 2 * row + 2, :].astype(bf16)
        for owner in range(parts):
            stage[owner, own + row] = ending
    departures = [
        pltpu.make_async_copy(stage.at[owner], out_ref.at[owner], out_sems.at[owner])
        for owner in range(parts)
    ]
    for arrival, departure in zip(arrivals, departures):
        arrival.wait()
        departure.start()
    for copy in departures:
        copy.wait()


def pack_first(positions, weights, psi, parts, share):
    local_g = psi.shape[3]
    beads, _, atoms = positions.shape
    extra = -(-9 * SLAB // local_g)
    return pl.pallas_call(
        pack_kernel,
        in_specs=[
            pl.BlockSpec(memory_space=pltpu.VMEM),
            pl.BlockSpec(memory_space=pltpu.VMEM),
            pl.BlockSpec(memory_space=pl.ANY),
        ],
        out_specs=pl.BlockSpec(memory_space=pl.ANY),
        out_shape=jax.ShapeDtypeStruct((parts, share // parts + extra, 2, local_g), bf16),
        scratch_shapes=[
            pltpu.VMEM((2 * extra, local_g), f32),
            pltpu.VMEM((parts, share // parts + extra, 2, local_g), bf16),
            pltpu.SemaphoreType.DMA((parts,)),
            pltpu.SemaphoreType.DMA((parts,)),
        ],
        compiler_params=pltpu.CompilerParams(vmem_limit_bytes=TAIL_VMEM_BYTES),
        cost_estimate=pl.CostEstimate(
            flops=0, bytes_accessed=8 * share * local_g, transcendentals=0
        ),
    )(jnp.swapaxes(positions, 0, 1), weights, psi)


def unpack_oxygens(rows, atoms):
    parts = rows.shape[0]
    pieces = rows.reshape(parts, -1)[:, : 9 * SLAB].reshape(parts, 3, 3, SLAB)
    found = jnp.sum(pieces[..., 0:atoms:3].astype(f32), axis=1)
    return jnp.swapaxes(found, 0, 1).reshape(3, -1)


def projector_tables(oxygens):
    line = frequency(jnp.arange(NGRID, dtype=jnp.int32), NGRID)
    second, third = jnp.repeat(line, NGRID), jnp.tile(line, NGRID)
    envelope = jnp.exp(-0.5 * width_square * (second * second + third * third))
    cosine, sine = cosine_and_sine(
        oxygens[1][:, None] * second[None, :] + oxygens[2][:, None] * third[None, :]
    )
    in_plane = jnp.concatenate([envelope * cosine, envelope * sine], 0)
    in_plane = jnp.concatenate([in_plane, second * in_plane, third * in_plane], 0).astype(bf16)
    envelope = jnp.exp(-0.5 * width_square * line * line)[:, None]
    cosine, sine = cosine_and_sine(line[:, None] * oxygens[0][None, :])
    cosine, sine = envelope * cosine, envelope * sine
    along = jnp.stack([cosine, sine, line[:, None] * cosine, line[:, None] * sine])
    return in_plane, along


def wave_kernel(
    wave_ref,
    cos_ref,
    sin_ref,
    back_ref,
    fore_ref,
    pot_ref,
    in_plane_ref,
    along_ref,
    out_ref,
    force_ref,
    rows,
    planes,
    turned,
    sums,
    pulls,
):
    parts, local_g = wave_ref.shape[0], wave_ref.shape[3]
    waters = along_ref.shape[2]
    band_rows = 2 * GROUP
    all_rows = NGRID * band_rows
    piece = min(local_g, PLANE)
    for start in range(0, NGRID * PLANE, piece):
        owner, offset = start // local_g, start % local_g
        x, column = start // PLANE, start % PLANE
        block = wave_ref[owner, :, :, offset : offset + piece]
        rows[x * band_rows : (x + 1) * band_rows, column : column + piece] = block.reshape(
            band_rows, piece
        )

    @pl.loop(0, sums.shape[0] // 2)
    def _(step):
        columns = pl.ds(pl.multiple_of(step * 2 * SLAB, 2 * SLAB), 2 * SLAB)
        found = inner(rows[...], in_plane_ref[columns, :])
        sums[2 * step] = found[:, :SLAB]
        sums[2 * step + 1] = found[:, SLAB:]

    @pl.when(pl.program_id(0) == 0)
    def _():
        force_ref[...] = jnp.zeros_like(force_ref)

    slabs = waters // SLAB
    real, imag = (pl.ds(first, all_rows // 2, stride=2) for first in range(2))
    shape = (NGRID, GROUP, SLAB)
    for slab in range(slabs):
        inside = slice(slab * SLAB, (slab + 1) * SLAB)
        factors = [along_ref[which, :, inside][:, None, :] for which in range(4)]

        def planewise(factor):
            first = 2 * factor * slabs + slab
            second = first + slabs
            found_re = sums[first, real, :] - sums[second, imag, :]
            found_im = sums[second, real, :] + sums[first, imag, :]
            return found_re.reshape(shape), found_im.reshape(shape)

        def over_x(found, cosines, sines):
            return (
                jnp.sum(found[0] * cosines - found[1] * sines, axis=0),
                jnp.sum(found[0] * sines + found[1] * cosines, axis=0),
            )

        plain = planewise(0)
        proj_re, proj_im = over_x(plain, *factors[:2])
        proj_re = (proj_re * (1.0 / GVECS)).astype(bf16).astype(f32)
        proj_im = (proj_im * (1.0 / GVECS)).astype(bf16).astype(f32)
        for axis in range(3):
            if axis == 0:
                slope_re, slope_im = over_x(plain, *factors[2:])
            else:
                slope_re, slope_im = over_x(planewise(axis), *factors[:2])
            force_ref[axis, :, inside] += proj_re * slope_im - proj_im * slope_re

        cosines, sines = factors[:2]
        pull_re = nonlocal_strength * (cosines * proj_re[None] + sines * proj_im[None])
        pull_im = nonlocal_strength * (cosines * proj_im[None] - sines * proj_re[None])
        for half, pull in enumerate(((pull_re, pull_im), (pull_im, -pull_re))):
            both = jnp.concatenate(pull, 1).reshape(all_rows, SLAB).astype(bf16)
            start = half * waters + slab * SLAB
            pulls[:, start : start + SLAB] = both

    @pl.loop(0, PLANE // LANES)
    def _(step):
        columns = pl.ds(pl.multiple_of(step * LANES, LANES), LANES)
        planes[:all_rows, columns] = matmul(rows[...], cos_ref[:, columns]).astype(bf16)
        planes[all_rows:, columns] = matmul(rows[...], sin_ref[:, columns]).astype(bf16)

    @pl.loop(0, PLANE // LANES)
    def _(step):
        columns = pl.ds(pl.multiple_of(step * LANES, LANES), LANES)
        space = matmul(back_ref[...], planes[:, columns]).reshape(NGRID, band_rows, LANES)
        space = space * pot_ref[:, columns][:, None, :]
        space = space.reshape(all_rows, LANES).astype(bf16)
        waves = matmul(fore_ref[...], space)
        turned[:, columns] = waves.astype(bf16)
        halves = waves.reshape(NGRID, 2, GROUP, LANES)
        other = jnp.concatenate([halves[:, 1:], -halves[:, :1]], 1).reshape(all_rows, LANES)
        rows[:, columns] = other.astype(bf16)

    @pl.loop(0, PLANE // LANES)
    def _(step):
        columns = pl.ds(pl.multiple_of(step * LANES, LANES), LANES)
        waves = matmul(turned[...], cos_ref[:, columns]) + matmul(rows[...], sin_ref[:, columns])
        waves += matmul(pulls[...], in_plane_ref[: 2 * waters, columns])
        planes[:all_rows, columns] = waves.astype(bf16)

    for start in range(0, NGRID * PLANE, piece):
        owner, offset = start // local_g, start % local_g
        x, column = start // PLANE, start % PLANE
        out_ref[owner, 0, :, offset : offset + piece] = planes[
            x * band_rows : (x + 1) * band_rows, column : column + piece
        ]


def apply_hamiltonian(waves, band_count, tables, grid_potential, in_plane, along):
    parts, _, _, local_g = waves.shape
    waters = along.shape[2]
    steps = band_count // GROUP
    band_rows = 2 * GROUP
    all_rows = NGRID * band_rows
    whole = lambda step: (0, 0)
    return pl.pallas_call(
        wave_kernel,
        grid=(steps,),
        in_specs=[
            pl.BlockSpec((parts, GROUP, 2, local_g), lambda step: (0, step, 0, 0)),
            pl.BlockSpec((PLANE, PLANE), whole),
            pl.BlockSpec((PLANE, PLANE), whole),
            pl.BlockSpec((all_rows, 2 * all_rows), whole),
            pl.BlockSpec((all_rows, all_rows), whole),
            pl.BlockSpec((NGRID, PLANE), whole),
            pl.BlockSpec((6 * waters, PLANE), whole),
            pl.BlockSpec((4, NGRID, waters), lambda step: (0, 0, 0)),
        ],
        out_specs=[
            pl.BlockSpec((parts, 1, band_rows, local_g), lambda step: (0, step, 0, 0)),
            pl.BlockSpec((3, GROUP, waters), lambda step: (0, 0, 0)),
        ],
        out_shape=[
            jax.ShapeDtypeStruct((parts, steps, band_rows, local_g), bf16),
            jax.ShapeDtypeStruct((3, GROUP, waters), f32),
        ],
        scratch_shapes=[
            pltpu.VMEM((all_rows, PLANE), bf16),
            pltpu.VMEM((2 * all_rows, PLANE), bf16),
            pltpu.VMEM((all_rows, PLANE), bf16),
            pltpu.VMEM((6 * waters // SLAB, all_rows, SLAB), f32),
            pltpu.VMEM((all_rows, 2 * waters), bf16),
        ],
        compiler_params=pltpu.CompilerParams(vmem_limit_bytes=VMEM_BYTES),
        cost_estimate=pl.CostEstimate(
            flops=steps * 2 * all_rows * PLANE * (4 * PLANE + 3 * all_rows + 8 * waters),
            bytes_accessed=8 * steps * band_rows * parts * local_g + 8 * PLANE * PLANE,
            transcendentals=0,
        ),
    )(waves, *tables, grid_potential, in_plane, along)


def trial_kernel(
    first, last, core_ref, kinetic_ref, wave_ref, potential_ref, pieces_ref, before_ref,
    margin_ref, trial_ref, mine_ref, other_ref, even, odd, packed,
):
    step = pl.program_id(0)
    share, width = wave_ref.shape[1:]
    kept = 1.0 - step_size * kinetic_ref[...]
    block = potential_ref[...].astype(f32) * step_size
    block = block.reshape(share // GROUP, 2, GROUP, width)
    for half in range(2):
        taken = block[:, half].reshape(share, width)
        trial_ref[half] = (wave_ref[half].astype(f32) * kept - taken).astype(bf16)
    real, imag = trial_ref[0], trial_ref[1]
    if first:
        all_real, all_imag = real, imag
    else:
        all_real = jnp.concatenate([before_ref[0], real], 0)
        all_imag = jnp.concatenate([before_ref[1], imag], 0)

    @pl.when(step == 0)
    def _():
        even[...] = jnp.zeros_like(even)
        odd[...] = jnp.zeros_like(odd)

    even[...] += inner(real, all_real) + inner(imag, all_imag)
    odd[...] += inner(imag, all_real) - inner(real, all_imag)

    @pl.when(step == pl.num_programs(0) - 1)
    def _():
        start = even.shape[1] - share
        row = lax.broadcasted_iota(jnp.int32, (share, share), 0)
        column = lax.broadcasted_iota(jnp.int32, (share, share), 1)
        own = jnp.where(row <= column, even[:, start:], odd[:, start:]) * (1.0 / GVECS)
        if not last:
            mine_ref[...] = own
        else:
            packed[start:, start:] = own
            if not first:
                packed[:start, :start] = margin_ref[...]
                packed[start:, :start] = odd[:, :start] * (1.0 / GVECS)
                packed[:start, start:] = even[:, :start] * (1.0 / GVECS)
            chips, rows, bands = mine_ref.shape
            rows -= GROUP
            half = chips * rows
            core = core_ref[0]
            mine = packed[pl.ds(pl.multiple_of(core * half, half), half), :]
            others = packed[pl.ds(pl.multiple_of((1 - core) * half, half), half), :]
            mine_ref[:, :rows, :] = mine.reshape(chips, rows, bands)
            mine_ref[:, rows:, :] = pieces_ref[...]
            other_ref[:, :rows, :] = others.reshape(chips, rows, bands).astype(bf16)
            other_ref[:, rows:, :] = jnp.zeros((chips, GROUP, bands), bf16)


def make_trial(chunk, count, core, kinetic, planes, potential, pieces, before, margin):
    _, share, local_g = planes.shape
    chips = pieces.shape[0]
    bands = share * count
    first, last = chunk == 0, chunk == count - 1
    width = min(TRIAL_WIDE, local_g)
    deep = lambda step: (0, 0, step)
    if last:
        rows = bands // (2 * chips) + GROUP
        out_specs = [pl.BlockSpec((chips, rows, bands), lambda step: (0, 0, 0))] * 2
        out_shape = [
            jax.ShapeDtypeStruct((chips, rows, bands), f32),
            jax.ShapeDtypeStruct((chips, rows, bands), bf16),
        ]
    else:
        out_specs = [pl.BlockSpec((share, share), lambda step: (0, 0))]
        out_shape = [jax.ShapeDtypeStruct((share, share), f32)]
    operands = [core, kinetic, planes, potential]
    in_specs = [
        pl.BlockSpec(memory_space=pltpu.SMEM),
        pl.BlockSpec((1, width), lambda step: (0, step)),
        pl.BlockSpec((2, share, width), deep),
        pl.BlockSpec((2 * share, width), lambda step: (0, step)),
    ]
    if last:
        operands.append(pieces)
        in_specs.append(pl.BlockSpec(pieces.shape, lambda step: (0, 0, 0)))
    if not first:
        operands += [before, margin]
        in_specs.append(pl.BlockSpec((2, share, width), deep))
        in_specs.append(pl.BlockSpec((share, share), lambda step: (0, 0)))

    def body(core_ref, kinetic_ref, wave_ref, potential_ref, *refs):
        refs = list(refs)
        pieces_ref = refs.pop(0) if last else None
        before_ref = None if first else refs.pop(0)
        margin_ref = None if first else refs.pop(0)
        trial_ref, mine_ref = refs.pop(0), refs.pop(0)
        other_ref = refs.pop(0) if last else None
        trial_kernel(
            first, last, core_ref, kinetic_ref, wave_ref, potential_ref, pieces_ref, before_ref,
            margin_ref, trial_ref, mine_ref, other_ref, *refs,
        )

    seen = (chunk + 1) * share
    return pl.pallas_call(
        body,
        grid=(local_g // width,),
        in_specs=in_specs,
        out_specs=[pl.BlockSpec((2, share, width), deep)] + out_specs,
        out_shape=[jax.ShapeDtypeStruct((2, share, local_g), bf16)] + out_shape,
        scratch_shapes=[
            pltpu.VMEM((share, seen), f32),
            pltpu.VMEM((share, seen), f32),
            pltpu.VMEM((bands, bands), f32),
        ],
        compiler_params=pltpu.CompilerParams(vmem_limit_bytes=LAST_VMEM_BYTES),
        cost_estimate=pl.CostEstimate(
            flops=8 * share * seen * local_g,
            bytes_accessed=12 * seen * local_g,
            transcendentals=0,
        ),
    )(*operands)


def update_kernel(count, core_ref, mine_ref, other_ref, *refs):
    trials, (out_ref, even, odd) = refs[:count], refs[count:]

    @pl.when(pl.program_id(0) == 0)
    def _():
        mine, others = mine_ref[...].astype(f32), other_ref[...].astype(f32)
        first = core_ref[0] == 0
        packed = jnp.concatenate(
            [jnp.where(first, mine, others), jnp.where(first, others, mine)], 0
        )
        share = packed.shape[0] // count
        row = lax.broadcasted_iota(jnp.int32, (share, share), 0)
        column = lax.broadcasted_iota(jnp.int32, (share, share), 1)
        spans = [slice(chunk * share, (chunk + 1) * share) for chunk in range(count)]
        for lower, down in enumerate(spans):
            own = packed[down, down]
            flipped = own.T
            even[down, down] = jnp.where(row <= column, own, flipped).astype(bf16)
            above = jnp.where(row == column, 0.0, -flipped)
            odd[down, down] = jnp.where(row > column, own, above).astype(bf16)
            for over in spans[:lower]:
                both, opposite = packed[over, down], packed[down, over]
                even[down, over] = both.astype(bf16)
                even[over, down] = both.T.astype(bf16)
                odd[down, over] = opposite.astype(bf16)
                odd[over, down] = -opposite.T.astype(bf16)

    real = jnp.concatenate([trial[0] for trial in trials], 0)
    imag = jnp.concatenate([trial[1] for trial in trials], 0)
    out_ref[:, 0, :] = (matmul(even[...], real) - matmul(odd[...], imag)).astype(bf16)
    out_ref[:, 1, :] = (matmul(even[...], imag) + matmul(odd[...], real)).astype(bf16)


def update_waves(core, mine, others, trials):
    _, share, local_g = trials[0].shape
    count = len(trials)
    bands = share * count
    width = min(WIDE, local_g)
    return pl.pallas_call(
        functools.partial(update_kernel, count),
        grid=(local_g // width,),
        in_specs=[
            pl.BlockSpec(memory_space=pltpu.SMEM),
            pl.BlockSpec((bands // 2, bands), lambda step: (0, 0)),
            pl.BlockSpec((bands // 2, bands), lambda step: (0, 0)),
        ]
        + [pl.BlockSpec((2, share, width), lambda step: (0, 0, step))] * count,
        out_specs=pl.BlockSpec((bands, 2, width), lambda step: (0, 0, step)),
        out_shape=jax.ShapeDtypeStruct((bands, 2, local_g), bf16),
        scratch_shapes=[pltpu.VMEM((bands, bands), bf16)] * 2,
        compiler_params=pltpu.CompilerParams(vmem_limit_bytes=LAST_VMEM_BYTES),
        cost_estimate=pl.CostEstimate(
            flops=8 * bands * bands * local_g,
            bytes_accessed=8 * bands * local_g,
            transcendentals=0,
        ),
    )(core, mine, others, *trials)


def per_device(positions, weights, psi, vloc):
    parts = lax.axis_size("ga")
    bands = psi.shape[1]
    local_g = psi.shape[3]

    weight_float = weights.astype(jnp.float32)
    mixing = weight_float / jnp.sum(weight_float, axis=1, keepdims=True)
    count = 2 if bands // parts % (2 * GROUP) == 0 else 1
    share = bands // count

    sent = pack_first(positions, weights, psi, parts, share)
    waves = [exchange(sent)]
    for chunk in range(1, count):
        block = psi[0, chunk * share : (chunk + 1) * share]
        waves.append(exchange(block.reshape(parts, share // parts, 2, local_g)))
    oxygens = unpack_oxygens(waves[0][:, share // parts :, 0, :], positions.shape[2])
    tables = transform_tables()
    in_plane, along = projector_tables(oxygens)
    grid_potential = vloc[0].reshape(NGRID, PLANE) * (1.0 / GVECS)
    potentials, forces = [], []
    for wave in waves:
        moved, force = apply_hamiltonian(
            wave, share // parts, tables, grid_potential, in_plane, along
        )
        potentials.append(exchange(moved).reshape(2 * share, local_g))
        forces.append(force)
    force_part = jnp.sum(sum(forces), axis=1) * (2.0 * occupation * nonlocal_strength / GVECS)

    flat_index = lax.axis_index("ga") * local_g + jnp.arange(local_g, dtype=jnp.int32)
    square = (
        frequency(flat_index // PLANE, NGRID) ** 2
        + frequency(flat_index // NGRID % NGRID, NGRID) ** 2
        + frequency(flat_index % NGRID, NGRID) ** 2
    )
    kinetic = (0.5 * square)[None]
    planes = [
        jnp.swapaxes(psi[0, chunk * share : (chunk + 1) * share], 0, 1) for chunk in range(count)
    ]

    chip, core = lax.axis_index("ga") // 2, lax.axis_index("ga") % 2
    chips = parts // 2
    rows = bands // parts
    same_core = [[2 * number + which for number in range(chips)] for which in range(2)]
    core_ref = core.reshape(1).astype(jnp.int32)
    near_chip = WATERS // chips
    pieces, left = [], force_part
    for _ in range(3):
        pieces.append(lax.reduce_precision(left, 8, 7))
        left = left - pieces[-1]
    pieces = jnp.swapaxes(jnp.stack(pieces).reshape(9, chips, near_chip), 0, 1)
    pieces = jnp.pad(pieces.reshape(chips, -1), ((0, 0), (0, GROUP * bands - 9 * near_chip)))
    pieces = pieces.reshape(chips, GROUP, bands)
    trials, margin = [], None
    for chunk, potential in enumerate(potentials):
        before = trials[-1] if trials else None
        trial, margin, *others = make_trial(
            chunk, count, core_ref, kinetic, planes[chunk], potential, pieces, before, margin
        )
        trials.append(trial)
    pair = (margin + other_core(others[0], parts).astype(f32)).astype(bf16)
    summed = jnp.sum(exchange(pair, same_core).astype(f32), axis=0)
    summed, found = summed[:rows], summed[rows:].reshape(-1)[: 9 * near_chip]
    found = jnp.sum(found.reshape(3, 3, near_chip), axis=0)
    found = (found + other_core(found, parts)).reshape(3, 2, near_chip // 2)
    oxygen_force = lax.dynamic_index_in_dim(found, core, 1, keepdims=False)
    row = (core * chips + chip) * rows + lax.broadcasted_iota(jnp.int32, (rows, bands), 0)
    column = lax.broadcasted_iota(jnp.int32, (rows, bands), 1)
    own_mixer = (jnp.where(row == column, 1.5, 0.0) - 0.5 * summed).astype(bf16)
    half_mixer = exchange(
        jnp.broadcast_to(own_mixer[None], (chips, rows, bands)), same_core
    ).reshape(bands // 2, bands)
    psi_new = update_waves(core_ref, half_mixer, other_core(half_mixer, parts), trials)

    hydrogen_zero = jnp.zeros_like(oxygen_force)
    dft_force = jnp.stack([oxygen_force, hydrogen_zero, hydrogen_zero], axis=2).reshape(1, 3, -1)

    near_forces = field_forces(positions)
    contracted_force = jnp.einsum("cj,can->jan", mixing, dft_force, precision=highest)
    bead_forces = near_forces + BEADS / CBEADS * contracted_force
    return (psi_new[None], bead_forces)


def solution(mesh):
    placed = (P("rep", None, "ga"), P(), P("rep", None, None, "ga"), P("rep", None))
    return jax.shard_map(
        per_device,
        mesh=mesh,
        in_specs=placed,
        out_specs=(P("rep", None, None, "ga"), P("rep", None, "ga")),
        check_vma=False,
    )
```

```python
import functools

import jax
import jax.numpy as jnp
import numpy as np
from jax import lax
from jax.experimental import pallas as pl
from jax.experimental.pallas import tpu as pltpu
from jax.sharding import PartitionSpec as P

BEADS = 32
CBEADS = 1
WATERS = 256
NGRID = 32
GVECS = 32768


box_length = 20.0
bond_stiff = 0.5
bond_rest = 1.8
spring_stiff = 2.0
width_square = 0.09
step_size = 0.02
nonlocal_strength = 250.0
occupation = 2.0
highest = lax.Precision.HIGHEST
bf16 = jnp.bfloat16
f32 = jnp.float32

PLANE = NGRID * NGRID
GROUP = 8
SLAB = 128
LANES = 256
WIDE = 512
VMEM_BYTES = 56 * 2**20
TAIL_VMEM_BYTES = 60 * 2**20
LAST_VMEM_BYTES = 28 * 2**20


def frequency(index, count):
    signed = jnp.where(index < count // 2, index, index - count)
    return signed.astype(jnp.float32) * (2.0 * jnp.pi / box_length)


def field_forces(positions):
    oxygen = positions[:, :, 0::3]
    toward_one = positions[:, :, 1::3] - oxygen
    toward_two = positions[:, :, 2::3] - oxygen

    def stretch(offset):
        length = jnp.sqrt(jnp.sum(offset * offset, axis=1, keepdims=True))
        return -bond_stiff * (length - bond_rest) * offset / length

    pull_one = stretch(toward_one)
    pull_two = stretch(toward_two)
    bonds = jnp.stack([-(pull_one + pull_two), pull_one, pull_two], axis=3).reshape(positions.shape)
    springs = 2.0 * positions - jnp.roll(positions, 1, axis=0) - jnp.roll(positions, -1, axis=0)
    return bonds - spring_stiff * springs


def inner(left_mat, right_mat):
    return lax.dot_general(
        left_mat, right_mat, (((1,), (1,)), ((), ())), preferred_element_type=jnp.float32
    )


def matmul(left_mat, right_mat):
    return jnp.dot(left_mat, right_mat, preferred_element_type=jnp.float32)


def exchange(blocks, groups=None):
    return lax.all_to_all(
        blocks, "ga", split_axis=0, concat_axis=0, tiled=True, axis_index_groups=groups
    )


def other_core(block, parts):
    return lax.ppermute(block, "ga", [(device, device ^ 1) for device in range(parts)])


def transform_tables():
    index = np.arange(PLANE)
    first, second = index // NGRID, index % NGRID
    product = (first[:, None] * first[None, :] + second[:, None] * second[None, :]) % NGRID
    angle = product * (2.0 * np.pi / NGRID)
    line = np.arange(NGRID)
    x_angle = (line[:, None] * line[None, :] % NGRID) * (2.0 * np.pi / NGRID)
    cosine, sine = np.cos(x_angle), np.sin(x_angle)
    same = np.eye(GROUP)
    rows = 2 * NGRID * GROUP

    def spread(mixing, order):
        return np.einsum("xycd,bm->" + order, mixing, same).reshape(rows, rows)

    def mixed(rr, ri, ir, ii):
        return np.stack([np.stack([rr, ri], -1), np.stack([ir, ii], -1)], -2)

    on_cosine = spread(mixed(cosine, -sine, sine, cosine), "xcbymd")
    on_sine = spread(mixed(-sine, -cosine, cosine, -sine), "xcbymd")
    backward = np.concatenate([on_cosine, on_sine], 1)
    forward = spread(mixed(cosine, sine, -sine, cosine), "xcbydm")
    still, none = np.eye(NGRID), np.zeros((NGRID, NGRID))
    order = spread(mixed(still, none, none, still), "xcbymd")
    return [
        jnp.asarray(table.astype(np.float32), dtype=bf16)
        for table in (np.cos(angle), np.sin(angle), backward, forward, order)
    ]


def cosine_and_sine(phases):
    turns = jnp.round(phases * (0.5 / np.pi))
    left = (phases - turns * 6.28125) - turns * (2.0 * np.pi - 6.28125)
    quarter = left * 0.25
    square = quarter * quarter
    sine = 1.0 + square * (
        -1.0 / 6 + square * (1.0 / 120 + square * (-1.0 / 5040 + square * (1.0 / 362880)))
    )
    sine = quarter * sine
    versine = square * (
        0.5
        + square
        * (-1.0 / 24 + square * (1.0 / 720 + square * (-1.0 / 40320 + square * (1.0 / 3628800))))
    )
    for _ in range(2):
        sine, versine = 2.0 * sine * (1.0 - versine), 2.0 * sine * sine
    return 1.0 - versine, sine


def pack_kernel(positions_ref, weights_ref, psi_ref, out_ref, lanes, stage, in_sems, out_sems):
    parts, total, _, local_g = out_ref.shape
    extra = lanes.shape[0] // 2
    own = total - extra
    arrivals = [
        pltpu.make_async_copy(
            psi_ref.at[0, pl.ds(owner * own, own)],
            stage.at[owner, pl.ds(0, own)],
            in_sems.at[owner],
        )
        for owner in range(parts)
    ]
    for copy in arrivals:
        copy.start()
    weights = weights_ref[...].astype(f32)
    mixing = weights / jnp.sum(weights, axis=1, keepdims=True)
    lanes[...] = jnp.zeros_like(lanes)
    atoms = positions_ref.shape[2]
    for axis in range(3):
        left = jnp.dot(
            mixing, positions_ref[axis], precision=highest, preferred_element_type=jnp.float32
        )
        for piece in range(3):
            sent = left.astype(bf16).astype(f32)
            left = left - sent
            place = (3 * piece + axis) * SLAB
            row, column = 2 * (place // local_g), place % local_g
            lanes[row : row + 1, column : column + atoms] = sent
    for row in range(extra):
        ending = lanes[2 * row : 2 * row + 2, :].astype(bf16)
        for owner in range(parts):
            stage[owner, own + row] = ending
    departures = [
        pltpu.make_async_copy(stage.at[owner], out_ref.at[owner], out_sems.at[owner])
        for owner in range(parts)
    ]
    for arrival, departure in zip(arrivals, departures):
        arrival.wait()
        departure.start()
    for copy in departures:
        copy.wait()


def pack_first(positions, weights, psi, parts, share):
    local_g = psi.shape[3]
    beads, _, atoms = positions.shape
    extra = -(-9 * SLAB // local_g)
    return pl.pallas_call(
        pack_kernel,
        in_specs=[
            pl.BlockSpec(memory_space=pltpu.VMEM),
            pl.BlockSpec(memory_space=pltpu.VMEM),
            pl.BlockSpec(memory_space=pl.ANY),
        ],
        out_specs=pl.BlockSpec(memory_space=pl.ANY),
        out_shape=jax.ShapeDtypeStruct((parts, share // parts + extra, 2, local_g), bf16),
        scratch_shapes=[
            pltpu.VMEM((2 * extra, local_g), f32),
            pltpu.VMEM((parts, share // parts + extra, 2, local_g), bf16),
            pltpu.SemaphoreType.DMA((parts,)),
            pltpu.SemaphoreType.DMA((parts,)),
        ],
        compiler_params=pltpu.CompilerParams(vmem_limit_bytes=TAIL_VMEM_BYTES),
        cost_estimate=pl.CostEstimate(
            flops=0, bytes_accessed=8 * share * local_g, transcendentals=0
        ),
    )(jnp.swapaxes(positions, 0, 1), weights, psi)


def unpack_oxygens(rows, atoms):
    parts = rows.shape[0]
    pieces = rows.reshape(parts, -1)[:, : 9 * SLAB].reshape(parts, 3, 3, SLAB)
    found = jnp.sum(pieces[..., 0:atoms:3].astype(f32), axis=1)
    return jnp.swapaxes(found, 0, 1).reshape(3, -1)


def projector_tables(oxygens):
    line = frequency(jnp.arange(NGRID, dtype=jnp.int32), NGRID)
    second, third = jnp.repeat(line, NGRID), jnp.tile(line, NGRID)
    envelope = jnp.exp(-0.5 * width_square * (second * second + third * third))
    cosine, sine = cosine_and_sine(
        oxygens[1][:, None] * second[None, :] + oxygens[2][:, None] * third[None, :]
    )
    in_plane = jnp.concatenate([envelope * cosine, envelope * sine], 0)
    in_plane = jnp.concatenate([in_plane, second * in_plane, third * in_plane], 0).astype(bf16)
    envelope = jnp.exp(-0.5 * width_square * line * line)[:, None]
    cosine, sine = cosine_and_sine(line[:, None] * oxygens[0][None, :])
    cosine, sine = envelope * cosine, envelope * sine
    along = jnp.stack([cosine, sine, line[:, None] * cosine, line[:, None] * sine])
    return in_plane, along


def wave_kernel(
    wave_ref,
    cos_ref,
    sin_ref,
    back_ref,
    fore_ref,
    order_ref,
    pot_ref,
    kept_ref,
    in_plane_ref,
    along_ref,
    out_ref,
    force_ref,
    rows,
    planes,
    turned,
    sums,
    pulls,
    kinetic,
):
    parts, local_g = wave_ref.shape[0], wave_ref.shape[3]
    waters = along_ref.shape[2]
    band_rows = 2 * GROUP
    all_rows = NGRID * band_rows
    piece = min(local_g, PLANE)
    for start in range(0, NGRID * PLANE, piece):
        owner, offset = start // local_g, start % local_g
        x, column = start // PLANE, start % PLANE
        block = wave_ref[owner, :, :, offset : offset + piece]
        rows[x * band_rows : (x + 1) * band_rows, column : column + piece] = block.reshape(
            band_rows, piece
        )

    @pl.loop(0, sums.shape[0] // 2)
    def _(step):
        columns = pl.ds(pl.multiple_of(step * 2 * SLAB, 2 * SLAB), 2 * SLAB)
        found = inner(rows[...], in_plane_ref[columns, :])
        sums[2 * step] = found[:, :SLAB]
        sums[2 * step + 1] = found[:, SLAB:]

    @pl.when(pl.program_id(0) == 0)
    def _():
        force_ref[...] = jnp.zeros_like(force_ref)

    slabs = waters // SLAB
    real, imag = (pl.ds(first, all_rows // 2, stride=2) for first in range(2))
    shape = (NGRID, GROUP, SLAB)
    for slab in range(slabs):
        inside = slice(slab * SLAB, (slab + 1) * SLAB)
        factors = [along_ref[which, :, inside][:, None, :] for which in range(4)]

        def planewise(factor):
            first = 2 * factor * slabs + slab
            second = first + slabs
            found_re = sums[first, real, :] - sums[second, imag, :]
            found_im = sums[second, real, :] + sums[first, imag, :]
            return found_re.reshape(shape), found_im.reshape(shape)

        def over_x(found, cosines, sines):
            return (
                jnp.sum(found[0] * cosines - found[1] * sines, axis=0),
                jnp.sum(found[0] * sines + found[1] * cosines, axis=0),
            )

        plain = planewise(0)
        proj_re, proj_im = over_x(plain, *factors[:2])
        proj_re = (proj_re * (1.0 / GVECS)).astype(bf16).astype(f32)
        proj_im = (proj_im * (1.0 / GVECS)).astype(bf16).astype(f32)
        for axis in range(3):
            if axis == 0:
                slope_re, slope_im = over_x(plain, *factors[2:])
            else:
                slope_re, slope_im = over_x(planewise(axis), *factors[:2])
            force_ref[axis, :, inside] += proj_re * slope_im - proj_im * slope_re

        cosines, sines = factors[:2]
        strength = step_size * nonlocal_strength
        pull_re = strength * (cosines * proj_re[None] + sines * proj_im[None])
        pull_im = strength * (cosines * proj_im[None] - sines * proj_re[None])
        for half, pull in enumerate(((pull_re, pull_im), (pull_im, -pull_re))):
            both = jnp.concatenate(pull, 1).reshape(all_rows, SLAB).astype(bf16)
            start = half * waters + slab * SLAB
            pulls[:, start : start + SLAB] = both

    @pl.loop(0, PLANE // LANES)
    def _(step):
        columns = pl.ds(pl.multiple_of(step * LANES, LANES), LANES)
        planes[:all_rows, columns] = matmul(rows[...], cos_ref[:, columns]).astype(bf16)
        planes[all_rows:, columns] = matmul(rows[...], sin_ref[:, columns]).astype(bf16)
        moved = matmul(order_ref[...], rows[:, columns]).reshape(NGRID, band_rows, LANES)
        kinetic[:, columns] = (moved * kept_ref[:, columns][:, None, :]).reshape(all_rows, LANES)

    @pl.loop(0, PLANE // LANES)
    def _(step):
        columns = pl.ds(pl.multiple_of(step * LANES, LANES), LANES)
        space = matmul(back_ref[...], planes[:, columns]).reshape(NGRID, band_rows, LANES)
        space = space * pot_ref[:, columns][:, None, :]
        space = space.reshape(all_rows, LANES).astype(bf16)
        waves = matmul(fore_ref[...], space)
        turned[:, columns] = waves.astype(bf16)
        halves = waves.reshape(NGRID, 2, GROUP, LANES)
        other = jnp.concatenate([halves[:, 1:], -halves[:, :1]], 1).reshape(all_rows, LANES)
        rows[:, columns] = other.astype(bf16)

    @pl.loop(0, PLANE // LANES)
    def _(step):
        columns = pl.ds(pl.multiple_of(step * LANES, LANES), LANES)
        waves = matmul(turned[...], cos_ref[:, columns]) + matmul(rows[...], sin_ref[:, columns])
        waves += matmul(pulls[...], in_plane_ref[: 2 * waters, columns])
        planes[:all_rows, columns] = (kinetic[:, columns] - waves).astype(bf16)

    for start in range(0, NGRID * PLANE, piece):
        owner, offset = start // local_g, start % local_g
        x, column = start // PLANE, start % PLANE
        out_ref[owner, 0, :, offset : offset + piece] = planes[
            x * band_rows : (x + 1) * band_rows, column : column + piece
        ]


def make_trial(waves, band_count, tables, grid_potential, kept, in_plane, along):
    parts, _, _, local_g = waves.shape
    waters = along.shape[2]
    steps = band_count // GROUP
    band_rows = 2 * GROUP
    all_rows = NGRID * band_rows
    whole = lambda step: (0, 0)
    return pl.pallas_call(
        wave_kernel,
        grid=(steps,),
        in_specs=[
            pl.BlockSpec((parts, GROUP, 2, local_g), lambda step: (0, step, 0, 0)),
            pl.BlockSpec((PLANE, PLANE), whole),
            pl.BlockSpec((PLANE, PLANE), whole),
            pl.BlockSpec((all_rows, 2 * all_rows), whole),
            pl.BlockSpec((all_rows, all_rows), whole),
            pl.BlockSpec((all_rows, all_rows), whole),
            pl.BlockSpec((NGRID, PLANE), whole),
            pl.BlockSpec((NGRID, PLANE), whole),
            pl.BlockSpec((6 * waters, PLANE), whole),
            pl.BlockSpec((4, NGRID, waters), lambda step: (0, 0, 0)),
        ],
        out_specs=[
            pl.BlockSpec((parts, 1, band_rows, local_g), lambda step: (0, step, 0, 0)),
            pl.BlockSpec((3, GROUP, waters), lambda step: (0, 0, 0)),
        ],
        out_shape=[
            jax.ShapeDtypeStruct((parts, steps, band_rows, local_g), bf16),
            jax.ShapeDtypeStruct((3, GROUP, waters), f32),
        ],
        scratch_shapes=[
            pltpu.VMEM((all_rows, PLANE), bf16),
            pltpu.VMEM((2 * all_rows, PLANE), bf16),
            pltpu.VMEM((all_rows, PLANE), bf16),
            pltpu.VMEM((6 * waters // SLAB, all_rows, SLAB), f32),
            pltpu.VMEM((all_rows, 2 * waters), bf16),
            pltpu.VMEM((all_rows, PLANE), f32),
        ],
        compiler_params=pltpu.CompilerParams(vmem_limit_bytes=VMEM_BYTES),
        cost_estimate=pl.CostEstimate(
            flops=steps * 2 * all_rows * PLANE * (4 * PLANE + 4 * all_rows + 8 * waters),
            bytes_accessed=8 * steps * band_rows * parts * local_g + 8 * PLANE * PLANE,
            transcendentals=0,
        ),
    )(waves, *tables, grid_potential, kept, in_plane, along)


def split_rows(block):
    count, width = block.shape
    block = block.astype(f32).reshape(count // (2 * GROUP), 2, GROUP, width)
    return [block[:, half].reshape(count // 2, width).astype(bf16) for half in range(2)]


def margin_kernel(first, last, core_ref, trial_ref, *refs):
    refs = list(refs)
    pieces_ref = refs.pop(0) if last else None
    before_ref, margin_ref = (None, None) if first else (refs.pop(0), refs.pop(0))
    mine_ref = refs.pop(0)
    real, imag = split_rows(trial_ref[...])
    share = real.shape[0]

    def margins(other_real, other_imag):
        even = inner(real, other_real) + inner(imag, other_imag)
        odd = inner(imag, other_real) - inner(real, other_imag)
        return even * (1.0 / GVECS), odd * (1.0 / GVECS)

    even, odd = margins(real, imag)
    row = lax.broadcasted_iota(jnp.int32, (share, share), 0)
    column = lax.broadcasted_iota(jnp.int32, (share, share), 1)
    own = jnp.where(row <= column, even, odd)
    if not last:
        mine_ref[...] = own
        return
    other_ref, packed = refs
    start = packed.shape[0] - share
    packed[start:, start:] = own
    if not first:
        even, odd = margins(*split_rows(before_ref[...]))
        packed[:start, :start] = margin_ref[...]
        packed[start:, :start] = odd
        packed[:start, start:] = even
    chips, rows, bands = mine_ref.shape
    rows -= GROUP
    half = chips * rows
    core = core_ref[0]
    mine = packed[pl.ds(pl.multiple_of(core * half, half), half), :]
    others = packed[pl.ds(pl.multiple_of((1 - core) * half, half), half), :]
    mine_ref[:, :rows, :] = mine.reshape(chips, rows, bands)
    mine_ref[:, rows:, :] = pieces_ref[...]
    other_ref[:, :rows, :] = others.reshape(chips, rows, bands).astype(bf16)
    other_ref[:, rows:, :] = jnp.zeros((chips, GROUP, bands), bf16)


def make_margin(first, last, bands, core, trial, pieces, before, margin):
    share, local_g = trial.shape[0] // 2, trial.shape[1]
    chips = pieces.shape[0]
    if last:
        rows = bands // (2 * chips) + GROUP
        out_shape = [
            jax.ShapeDtypeStruct((chips, rows, bands), f32),
            jax.ShapeDtypeStruct((chips, rows, bands), bf16),
        ]
    else:
        out_shape = [jax.ShapeDtypeStruct((share, share), f32)]
    operands = [core, trial] + ([pieces] if last else []) + ([] if first else [before, margin])
    inside = pl.BlockSpec(memory_space=pltpu.VMEM)
    return pl.pallas_call(
        functools.partial(margin_kernel, first, last),
        in_specs=[pl.BlockSpec(memory_space=pltpu.SMEM)] + [inside] * (len(operands) - 1),
        out_specs=[inside] * len(out_shape),
        out_shape=out_shape,
        scratch_shapes=[pltpu.VMEM((bands, bands), f32)] if last else [],
        compiler_params=pltpu.CompilerParams(vmem_limit_bytes=LAST_VMEM_BYTES),
        cost_estimate=pl.CostEstimate(
            flops=8 * share * (share if first else 2 * share) * local_g,
            bytes_accessed=8 * share * local_g,
            transcendentals=0,
        ),
    )(*operands)


def update_kernel(count, core_ref, mine_ref, other_ref, *refs):
    trials, (out_ref, even, odd) = refs[:count], refs[count:]

    @pl.when(pl.program_id(0) == 0)
    def _():
        mine, others = mine_ref[...].astype(f32), other_ref[...].astype(f32)
        first = core_ref[0] == 0
        packed = jnp.concatenate(
            [jnp.where(first, mine, others), jnp.where(first, others, mine)], 0
        )
        share = packed.shape[0] // count
        row = lax.broadcasted_iota(jnp.int32, (share, share), 0)
        column = lax.broadcasted_iota(jnp.int32, (share, share), 1)
        spans = [slice(chunk * share, (chunk + 1) * share) for chunk in range(count)]
        for lower, down in enumerate(spans):
            own = packed[down, down]
            flipped = own.T
            even[down, down] = jnp.where(row <= column, own, flipped).astype(bf16)
            above = jnp.where(row == column, 0.0, -flipped)
            odd[down, down] = jnp.where(row > column, own, above).astype(bf16)
            for over in spans[:lower]:
                both, opposite = packed[over, down], packed[down, over]
                even[down, over] = both.astype(bf16)
                even[over, down] = both.T.astype(bf16)
                odd[down, over] = opposite.astype(bf16)
                odd[over, down] = -opposite.T.astype(bf16)

    parted = [split_rows(trial[...]) for trial in trials]
    real = jnp.concatenate([part[0] for part in parted], 0)
    imag = jnp.concatenate([part[1] for part in parted], 0)
    out_ref[:, 0, :] = (matmul(even[...], real) - matmul(odd[...], imag)).astype(bf16)
    out_ref[:, 1, :] = (matmul(even[...], imag) + matmul(odd[...], real)).astype(bf16)


def update_waves(core, mine, others, trials):
    rows, local_g = trials[0].shape
    count = len(trials)
    bands = rows // 2 * count
    width = min(WIDE, local_g)
    return pl.pallas_call(
        functools.partial(update_kernel, count),
        grid=(local_g // width,),
        in_specs=[
            pl.BlockSpec(memory_space=pltpu.SMEM),
            pl.BlockSpec((bands // 2, bands), lambda step: (0, 0)),
            pl.BlockSpec((bands // 2, bands), lambda step: (0, 0)),
        ]
        + [pl.BlockSpec((rows, width), lambda step: (0, step))] * count,
        out_specs=pl.BlockSpec((bands, 2, width), lambda step: (0, 0, step)),
        out_shape=jax.ShapeDtypeStruct((bands, 2, local_g), bf16),
        scratch_shapes=[pltpu.VMEM((bands, bands), bf16)] * 2,
        compiler_params=pltpu.CompilerParams(vmem_limit_bytes=LAST_VMEM_BYTES),
        cost_estimate=pl.CostEstimate(
            flops=8 * bands * bands * local_g,
            bytes_accessed=8 * bands * local_g,
            transcendentals=0,
        ),
    )(core, mine, others, *trials)


def per_device(positions, weights, psi, vloc):
    parts = lax.axis_size("ga")
    bands = psi.shape[1]
    local_g = psi.shape[3]

    weight_float = weights.astype(jnp.float32)
    mixing = weight_float / jnp.sum(weight_float, axis=1, keepdims=True)
    count = 2 if bands // parts % (2 * GROUP) == 0 else 1
    share = bands // count

    sent = pack_first(positions, weights, psi, parts, share)
    waves = [exchange(sent)]
    for chunk in range(1, count):
        block = psi[0, chunk * share : (chunk + 1) * share]
        waves.append(exchange(block.reshape(parts, share // parts, 2, local_g)))
    oxygens = unpack_oxygens(waves[0][:, share // parts :, 0, :], positions.shape[2])
    tables = transform_tables()
    in_plane, along = projector_tables(oxygens)
    grid_potential = vloc[0].reshape(NGRID, PLANE) * (step_size / GVECS)
    line = frequency(jnp.arange(NGRID, dtype=jnp.int32), NGRID) ** 2
    square = line[:, None, None] + line[None, :, None] + line[None, None, :]
    kept = (1.0 - step_size * 0.5 * square).reshape(NGRID, PLANE)
    trials, forces = [], []
    for wave in waves:
        moved, force = make_trial(
            wave, share // parts, tables, grid_potential, kept, in_plane, along
        )
        trials.append(exchange(moved).reshape(2 * share, local_g))
        forces.append(force)
    force_part = jnp.sum(sum(forces), axis=1) * (2.0 * occupation * nonlocal_strength / GVECS)

    chip, core = lax.axis_index("ga") // 2, lax.axis_index("ga") % 2
    chips = parts // 2
    rows = bands // parts
    same_core = [[2 * number + which for number in range(chips)] for which in range(2)]
    core_ref = core.reshape(1).astype(jnp.int32)
    near_chip = WATERS // chips
    pieces, left = [], force_part
    for _ in range(3):
        pieces.append(lax.reduce_precision(left, 8, 7))
        left = left - pieces[-1]
    pieces = jnp.swapaxes(jnp.stack(pieces).reshape(9, chips, near_chip), 0, 1)
    pieces = jnp.pad(pieces.reshape(chips, -1), ((0, 0), (0, GROUP * bands - 9 * near_chip)))
    pieces = pieces.reshape(chips, GROUP, bands)
    before, margin = None, None
    for chunk, trial in enumerate(trials):
        margin, *others = make_margin(
            chunk == 0, chunk == count - 1, bands, core_ref, trial, pieces, before, margin
        )
        before = trial
    pair = (margin + other_core(others[0], parts).astype(f32)).astype(bf16)
    summed = jnp.sum(exchange(pair, same_core).astype(f32), axis=0)
    summed, found = summed[:rows], summed[rows:].reshape(-1)[: 9 * near_chip]
    found = jnp.sum(found.reshape(3, 3, near_chip), axis=0)
    found = (found + other_core(found, parts)).reshape(3, 2, near_chip // 2)
    oxygen_force = lax.dynamic_index_in_dim(found, core, 1, keepdims=False)
    row = (core * chips + chip) * rows + lax.broadcasted_iota(jnp.int32, (rows, bands), 0)
    column = lax.broadcasted_iota(jnp.int32, (rows, bands), 1)
    own_mixer = (jnp.where(row == column, 1.5, 0.0) - 0.5 * summed).astype(bf16)
    half_mixer = exchange(
        jnp.broadcast_to(own_mixer[None], (chips, rows, bands)), same_core
    ).reshape(bands // 2, bands)
    psi_new = update_waves(core_ref, half_mixer, other_core(half_mixer, parts), trials)

    hydrogen_zero = jnp.zeros_like(oxygen_force)
    dft_force = jnp.stack([oxygen_force, hydrogen_zero, hydrogen_zero], axis=2).reshape(1, 3, -1)

    near_forces = field_forces(positions)
    contracted_force = jnp.einsum("cj,can->jan", mixing, dft_force, precision=highest)
    bead_forces = near_forces + BEADS / CBEADS * contracted_force
    return (psi_new[None], bead_forces)


def solution(mesh):
    placed = (P("rep", None, "ga"), P(), P("rep", None, None, "ga"), P("rep", None))
    return jax.shard_map(
        per_device,
        mesh=mesh,
        in_specs=placed,
        out_specs=(P("rep", None, None, "ga"), P("rep", None, "ga")),
        check_vma=False,
    )
```

```python
import functools

import jax
import jax.numpy as jnp
import numpy as np
from jax import lax
from jax.experimental import pallas as pl
from jax.experimental.pallas import tpu as pltpu
from jax.sharding import PartitionSpec as P

BEADS = 32
CBEADS = 1
WATERS = 256
NGRID = 32
GVECS = 32768


box_length = 20.0
bond_stiff = 0.5
bond_rest = 1.8
spring_stiff = 2.0
width_square = 0.09
step_size = 0.02
nonlocal_strength = 250.0
occupation = 2.0
highest = lax.Precision.HIGHEST
bf16 = jnp.bfloat16
f32 = jnp.float32

PLANE = NGRID * NGRID
GROUP = 8
SLAB = 128
LANES = 256
WIDE = 1024
PIECE = 512
VMEM_BYTES = 56 * 2**20
TAIL_VMEM_BYTES = 60 * 2**20
LAST_VMEM_BYTES = 28 * 2**20


def frequency(index, count):
    signed = jnp.where(index < count // 2, index, index - count)
    return signed.astype(jnp.float32) * (2.0 * jnp.pi / box_length)


def field_forces(positions):
    oxygen = positions[:, :, 0::3]
    toward_one = positions[:, :, 1::3] - oxygen
    toward_two = positions[:, :, 2::3] - oxygen

    def stretch(offset):
        length = jnp.sqrt(jnp.sum(offset * offset, axis=1, keepdims=True))
        return -bond_stiff * (length - bond_rest) * offset / length

    pull_one = stretch(toward_one)
    pull_two = stretch(toward_two)
    bonds = jnp.stack([-(pull_one + pull_two), pull_one, pull_two], axis=3).reshape(positions.shape)
    springs = 2.0 * positions - jnp.roll(positions, 1, axis=0) - jnp.roll(positions, -1, axis=0)
    return bonds - spring_stiff * springs


def inner(left_mat, right_mat):
    return lax.dot_general(
        left_mat, right_mat, (((1,), (1,)), ((), ())), preferred_element_type=jnp.float32
    )


def matmul(left_mat, right_mat):
    return jnp.dot(left_mat, right_mat, preferred_element_type=jnp.float32)


def exchange(blocks, groups=None):
    return lax.all_to_all(
        blocks, "ga", split_axis=0, concat_axis=0, tiled=True, axis_index_groups=groups
    )


def other_core(block, parts):
    return lax.ppermute(block, "ga", [(device, device ^ 1) for device in range(parts)])


def transform_tables():
    index = np.arange(PLANE)
    first, second = index // NGRID, index % NGRID
    product = (first[:, None] * first[None, :] + second[:, None] * second[None, :]) % NGRID
    angle = product * (2.0 * np.pi / NGRID)
    line = np.arange(NGRID)
    x_angle = (line[:, None] * line[None, :] % NGRID) * (2.0 * np.pi / NGRID)
    cosine, sine = np.cos(x_angle), np.sin(x_angle)
    same = np.eye(GROUP)
    rows = 2 * NGRID * GROUP

    def spread(mixing, order):
        return np.einsum("xycd,bm->" + order, mixing, same).reshape(rows, rows)

    def mixed(rr, ri, ir, ii):
        return np.stack([np.stack([rr, ri], -1), np.stack([ir, ii], -1)], -2)

    on_cosine = spread(mixed(cosine, -sine, sine, cosine), "xcbymd")
    on_sine = spread(mixed(-sine, -cosine, cosine, -sine), "xcbymd")
    backward = np.concatenate([on_cosine, on_sine], 1)
    forward = spread(mixed(cosine, sine, -sine, cosine), "xcbydm")
    still, none = np.eye(NGRID), np.zeros((NGRID, NGRID))
    order = spread(mixed(still, none, none, still), "xcbymd")
    return [
        jnp.asarray(table.astype(np.float32), dtype=bf16)
        for table in (np.cos(angle), np.sin(angle), backward, forward, order)
    ]


def cosine_and_sine(phases):
    turns = jnp.round(phases * (0.5 / np.pi))
    left = (phases - turns * 6.28125) - turns * (2.0 * np.pi - 6.28125)
    quarter = left * 0.25
    square = quarter * quarter
    sine = 1.0 + square * (
        -1.0 / 6 + square * (1.0 / 120 + square * (-1.0 / 5040 + square * (1.0 / 362880)))
    )
    sine = quarter * sine
    versine = square * (
        0.5
        + square
        * (-1.0 / 24 + square * (1.0 / 720 + square * (-1.0 / 40320 + square * (1.0 / 3628800))))
    )
    for _ in range(2):
        sine, versine = 2.0 * sine * (1.0 - versine), 2.0 * sine * sine
    return 1.0 - versine, sine


def pack_kernel(positions_ref, weights_ref, psi_ref, out_ref, lanes, stage, in_sems, out_sems):
    parts, total, _, width = out_ref.shape
    extra = lanes.shape[0] // 2
    pieces = psi_ref.shape[3] // width
    own = (total - extra) // pieces
    arrivals = [
        [
            pltpu.make_async_copy(
                psi_ref.at[0, pl.ds(owner * own, own), :, pl.ds(piece * width, width)],
                stage.at[owner, pl.ds(piece * own, own)],
                in_sems.at[owner, piece],
            )
            for piece in range(pieces)
        ]
        for owner in range(parts)
    ]
    for copies in arrivals:
        for copy in copies:
            copy.start()
    weights = weights_ref[...].astype(f32)
    mixing = weights / jnp.sum(weights, axis=1, keepdims=True)
    lanes[...] = jnp.zeros_like(lanes)
    atoms = positions_ref.shape[2]
    for axis in range(3):
        left = jnp.dot(
            mixing, positions_ref[axis], precision=highest, preferred_element_type=jnp.float32
        )
        for piece in range(3):
            sent = left.astype(bf16).astype(f32)
            left = left - sent
            place = (3 * piece + axis) * segment(atoms)
            row, column = place // width, place % width
            lanes[row : row + 1, column : column + atoms] = sent
    for row in range(extra):
        ending = lanes[2 * row : 2 * row + 2, :].astype(bf16)
        for owner in range(parts):
            stage[owner, own * pieces + row] = ending
    departures = [
        pltpu.make_async_copy(stage.at[owner], out_ref.at[owner], out_sems.at[owner])
        for owner in range(parts)
    ]
    for copies, departure in zip(arrivals, departures):
        for copy in copies:
            copy.wait()
        departure.start()
    for copy in departures:
        copy.wait()


def segment(atoms):
    return -(-atoms // 64) * 64


def pack_first(positions, weights, psi, parts, share):
    local_g = psi.shape[3]
    atoms = positions.shape[2]
    width = min(PIECE, local_g)
    pieces = local_g // width
    extra = -(-9 * segment(atoms) // (2 * width))
    block = (parts, pieces * share // parts + extra, 2, width)
    return pl.pallas_call(
        pack_kernel,
        in_specs=[
            pl.BlockSpec(memory_space=pltpu.VMEM),
            pl.BlockSpec(memory_space=pltpu.VMEM),
            pl.BlockSpec(memory_space=pl.ANY),
        ],
        out_specs=pl.BlockSpec(memory_space=pl.ANY),
        out_shape=jax.ShapeDtypeStruct(block, bf16),
        scratch_shapes=[
            pltpu.VMEM((2 * extra, width), f32),
            pltpu.VMEM(block, bf16),
            pltpu.SemaphoreType.DMA((parts, pieces)),
            pltpu.SemaphoreType.DMA((parts,)),
        ],
        compiler_params=pltpu.CompilerParams(vmem_limit_bytes=TAIL_VMEM_BYTES),
        cost_estimate=pl.CostEstimate(
            flops=0, bytes_accessed=8 * share * local_g, transcendentals=0
        ),
    )(jnp.swapaxes(positions, 0, 1), weights, psi)


def unpack_oxygens(rows, atoms):
    parts, each = rows.shape[0], segment(atoms)
    pieces = rows.reshape(parts, -1)[:, : 9 * each].reshape(parts, 3, 3, each)
    found = jnp.sum(pieces[..., 0:atoms:3].astype(f32), axis=1)
    return jnp.swapaxes(found, 0, 1).reshape(3, -1)


def projector_tables(oxygens):
    line = frequency(jnp.arange(NGRID, dtype=jnp.int32), NGRID)
    second, third = jnp.repeat(line, NGRID), jnp.tile(line, NGRID)
    envelope = jnp.exp(-0.5 * width_square * (second * second + third * third))
    cosine, sine = cosine_and_sine(
        oxygens[1][:, None] * second[None, :] + oxygens[2][:, None] * third[None, :]
    )
    in_plane = jnp.concatenate([envelope * cosine, envelope * sine], 0)
    in_plane = jnp.concatenate([in_plane, second * in_plane, third * in_plane], 0).astype(bf16)
    envelope = jnp.exp(-0.5 * width_square * line * line)[:, None]
    cosine, sine = cosine_and_sine(line[:, None] * oxygens[0][None, :])
    cosine, sine = envelope * cosine, envelope * sine
    along = jnp.stack([cosine, sine, line[:, None] * cosine, line[:, None] * sine])
    return in_plane, along


def wave_kernel(
    band_count,
    wave_ref,
    cos_ref,
    sin_ref,
    back_ref,
    fore_ref,
    order_ref,
    pot_ref,
    kept_ref,
    in_plane_ref,
    along_ref,
    out_ref,
    force_ref,
    rows,
    planes,
    turned,
    sums,
    pulls,
    kinetic,
):
    parts, _, _, local_g = out_ref.shape
    width = wave_ref.shape[3]
    waters = along_ref.shape[2]
    band_rows = 2 * GROUP
    all_rows = NGRID * band_rows
    piece = min(width, PLANE)
    first = pl.program_id(0) * GROUP if width < local_g else 0
    for start in range(0, NGRID * PLANE, piece):
        owner, offset = start // local_g, start % local_g
        x, column = start // PLANE, start % PLANE
        bands = pl.ds(first + offset // width * band_count, GROUP)
        block = wave_ref[owner, bands, :, offset % width : offset % width + piece]
        rows[x * band_rows : (x + 1) * band_rows, column : column + piece] = block.reshape(
            band_rows, piece
        )

    @pl.loop(0, sums.shape[0] // 2)
    def _(step):
        columns = pl.ds(pl.multiple_of(step * 2 * SLAB, 2 * SLAB), 2 * SLAB)
        found = inner(rows[...], in_plane_ref[columns, :])
        sums[2 * step] = found[:, :SLAB]
        sums[2 * step + 1] = found[:, SLAB:]

    @pl.when(pl.program_id(0) == 0)
    def _():
        force_ref[...] = jnp.zeros_like(force_ref)

    slabs = waters // SLAB
    real, imag = (pl.ds(first, all_rows // 2, stride=2) for first in range(2))
    shape = (NGRID, GROUP, SLAB)
    for slab in range(slabs):
        inside = slice(slab * SLAB, (slab + 1) * SLAB)
        factors = [along_ref[which, :, inside][:, None, :] for which in range(4)]

        def planewise(factor):
            first = 2 * factor * slabs + slab
            second = first + slabs
            found_re = sums[first, real, :] - sums[second, imag, :]
            found_im = sums[second, real, :] + sums[first, imag, :]
            return found_re.reshape(shape), found_im.reshape(shape)

        def over_x(found, cosines, sines):
            return (
                jnp.sum(found[0] * cosines - found[1] * sines, axis=0),
                jnp.sum(found[0] * sines + found[1] * cosines, axis=0),
            )

        plain = planewise(0)
        proj_re, proj_im = over_x(plain, *factors[:2])
        proj_re = (proj_re * (1.0 / GVECS)).astype(bf16).astype(f32)
        proj_im = (proj_im * (1.0 / GVECS)).astype(bf16).astype(f32)
        for axis in range(3):
            if axis == 0:
                slope_re, slope_im = over_x(plain, *factors[2:])
            else:
                slope_re, slope_im = over_x(planewise(axis), *factors[:2])
            force_ref[axis, :, inside] += proj_re * slope_im - proj_im * slope_re

        cosines, sines = factors[:2]
        strength = step_size * nonlocal_strength
        pull_re = strength * (cosines * proj_re[None] + sines * proj_im[None])
        pull_im = strength * (cosines * proj_im[None] - sines * proj_re[None])
        for half, pull in enumerate(((pull_re, pull_im), (pull_im, -pull_re))):
            both = jnp.concatenate(pull, 1).reshape(all_rows, SLAB).astype(bf16)
            start = half * waters + slab * SLAB
            pulls[:, start : start + SLAB] = both

    @pl.loop(0, PLANE // LANES)
    def _(step):
        columns = pl.ds(pl.multiple_of(step * LANES, LANES), LANES)
        planes[:all_rows, columns] = matmul(rows[...], cos_ref[:, columns]).astype(bf16)
        planes[all_rows:, columns] = matmul(rows[...], sin_ref[:, columns]).astype(bf16)
        moved = matmul(order_ref[...], rows[:, columns]).reshape(NGRID, band_rows, LANES)
        kinetic[:, columns] = (moved * kept_ref[:, columns][:, None, :]).reshape(all_rows, LANES)

    @pl.loop(0, PLANE // LANES)
    def _(step):
        columns = pl.ds(pl.multiple_of(step * LANES, LANES), LANES)
        space = matmul(back_ref[...], planes[:, columns]).reshape(NGRID, band_rows, LANES)
        space = space * pot_ref[:, columns][:, None, :]
        space = space.reshape(all_rows, LANES).astype(bf16)
        waves = matmul(fore_ref[...], space)
        turned[:, columns] = waves.astype(bf16)
        halves = waves.reshape(NGRID, 2, GROUP, LANES)
        other = jnp.concatenate([halves[:, 1:], -halves[:, :1]], 1).reshape(all_rows, LANES)
        rows[:, columns] = other.astype(bf16)

    @pl.loop(0, PLANE // LANES)
    def _(step):
        columns = pl.ds(pl.multiple_of(step * LANES, LANES), LANES)
        waves = matmul(turned[...], cos_ref[:, columns]) + matmul(rows[...], sin_ref[:, columns])
        waves += matmul(pulls[...], in_plane_ref[: 2 * waters, columns])
        planes[:all_rows, columns] = (kinetic[:, columns] - waves).astype(bf16)

    piece = min(local_g, PLANE)
    for start in range(0, NGRID * PLANE, piece):
        owner, offset = start // local_g, start % local_g
        x, column = start // PLANE, start % PLANE
        out_ref[owner, 0, :, offset : offset + piece] = planes[
            x * band_rows : (x + 1) * band_rows, column : column + piece
        ]


def make_trial(waves, band_count, local_g, tables, grid_potential, kept, in_plane, along):
    parts, total, _, width = waves.shape
    if width < local_g:
        taken = pl.BlockSpec((parts, total, 2, width), lambda step: (0, 0, 0, 0))
    else:
        taken = pl.BlockSpec((parts, GROUP, 2, width), lambda step: (0, step, 0, 0))
    waters = along.shape[2]
    steps = band_count // GROUP
    band_rows = 2 * GROUP
    all_rows = NGRID * band_rows
    whole = lambda step: (0, 0)
    return pl.pallas_call(
        functools.partial(wave_kernel, band_count),
        grid=(steps,),
        in_specs=[
            taken,
            pl.BlockSpec((PLANE, PLANE), whole),
            pl.BlockSpec((PLANE, PLANE), whole),
            pl.BlockSpec((all_rows, 2 * all_rows), whole),
            pl.BlockSpec((all_rows, all_rows), whole),
            pl.BlockSpec((all_rows, all_rows), whole),
            pl.BlockSpec((NGRID, PLANE), whole),
            pl.BlockSpec((NGRID, PLANE), whole),
            pl.BlockSpec((6 * waters, PLANE), whole),
            pl.BlockSpec((4, NGRID, waters), lambda step: (0, 0, 0)),
        ],
        out_specs=[
            pl.BlockSpec((parts, 1, band_rows, local_g), lambda step: (0, step, 0, 0)),
            pl.BlockSpec((3, GROUP, waters), lambda step: (0, 0, 0)),
        ],
        out_shape=[
            jax.ShapeDtypeStruct((parts, steps, band_rows, local_g), bf16),
            jax.ShapeDtypeStruct((3, GROUP, waters), f32),
        ],
        scratch_shapes=[
            pltpu.VMEM((all_rows, PLANE), bf16),
            pltpu.VMEM((2 * all_rows, PLANE), bf16),
            pltpu.VMEM((all_rows, PLANE), bf16),
            pltpu.VMEM((6 * waters // SLAB, all_rows, SLAB), f32),
            pltpu.VMEM((all_rows, 2 * waters), bf16),
            pltpu.VMEM((all_rows, PLANE), f32),
        ],
        compiler_params=pltpu.CompilerParams(vmem_limit_bytes=VMEM_BYTES),
        cost_estimate=pl.CostEstimate(
            flops=steps * 2 * all_rows * PLANE * (4 * PLANE + 4 * all_rows + 8 * waters),
            bytes_accessed=8 * steps * band_rows * parts * local_g + 8 * PLANE * PLANE,
            transcendentals=0,
        ),
    )(waves, *tables, grid_potential, kept, in_plane, along)


def split_rows(block):
    count, width = block.shape
    block = block.astype(f32).reshape(count // (2 * GROUP), 2, GROUP, width)
    return [block[:, half].reshape(count // 2, width).astype(bf16) for half in range(2)]


def margin_kernel(first, last, core_ref, trial_ref, *refs):
    refs = list(refs)
    pieces_ref = refs.pop(0) if last else None
    before_ref, margin_ref = (None, None) if first else (refs.pop(0), refs.pop(0))
    mine_ref = refs.pop(0)
    real, imag = split_rows(trial_ref[...])
    share = real.shape[0]

    def margins(other_real, other_imag):
        even = inner(real, other_real) + inner(imag, other_imag)
        odd = inner(imag, other_real) - inner(real, other_imag)
        return even * (1.0 / GVECS), odd * (1.0 / GVECS)

    even, odd = margins(real, imag)
    row = lax.broadcasted_iota(jnp.int32, (share, share), 0)
    column = lax.broadcasted_iota(jnp.int32, (share, share), 1)
    own = jnp.where(row <= column, even, odd)
    if not last:
        mine_ref[...] = own
        return
    other_ref, packed = refs
    start = packed.shape[0] - share
    packed[start:, start:] = own
    if not first:
        even, odd = margins(*split_rows(before_ref[...]))
        packed[:start, :start] = margin_ref[...]
        packed[start:, :start] = odd
        packed[:start, start:] = even
    chips, rows, bands = mine_ref.shape
    rows -= GROUP
    half = chips * rows
    core = core_ref[0]
    mine = packed[pl.ds(pl.multiple_of(core * half, half), half), :]
    others = packed[pl.ds(pl.multiple_of((1 - core) * half, half), half), :]
    mine_ref[:, :rows, :] = mine.reshape(chips, rows, bands)
    mine_ref[:, rows:, :] = pieces_ref[...]
    other_ref[:, :rows, :] = others.reshape(chips, rows, bands).astype(bf16)
    other_ref[:, rows:, :] = jnp.zeros((chips, GROUP, bands), bf16)


def make_margin(first, last, bands, core, trial, pieces, before, margin):
    share, local_g = trial.shape[0] // 2, trial.shape[1]
    chips = pieces.shape[0]
    if last:
        rows = bands // (2 * chips) + GROUP
        out_shape = [
            jax.ShapeDtypeStruct((chips, rows, bands), f32),
            jax.ShapeDtypeStruct((chips, rows, bands), bf16),
        ]
    else:
        out_shape = [jax.ShapeDtypeStruct((share, share), f32)]
    operands = [core, trial] + ([pieces] if last else []) + ([] if first else [before, margin])
    inside = pl.BlockSpec(memory_space=pltpu.VMEM)
    return pl.pallas_call(
        functools.partial(margin_kernel, first, last),
        in_specs=[pl.BlockSpec(memory_space=pltpu.SMEM)] + [inside] * (len(operands) - 1),
        out_specs=[inside] * len(out_shape),
        out_shape=out_shape,
        scratch_shapes=[pltpu.VMEM((bands, bands), f32)] if last else [],
        compiler_params=pltpu.CompilerParams(vmem_limit_bytes=LAST_VMEM_BYTES),
        cost_estimate=pl.CostEstimate(
            flops=8 * share * (share if first else 2 * share) * local_g,
            bytes_accessed=8 * share * local_g,
            transcendentals=0,
        ),
    )(*operands)


def update_kernel(count, core_ref, mine_ref, other_ref, *refs):
    trials, (out_ref, even, odd) = refs[:count], refs[count:]

    @pl.when(pl.program_id(0) == 0)
    def _():
        mine, others = mine_ref[...].astype(f32), other_ref[...].astype(f32)
        first = core_ref[0] == 0
        packed = jnp.concatenate(
            [jnp.where(first, mine, others), jnp.where(first, others, mine)], 0
        )
        share = packed.shape[0] // count
        row = lax.broadcasted_iota(jnp.int32, (share, share), 0)
        column = lax.broadcasted_iota(jnp.int32, (share, share), 1)
        spans = [slice(chunk * share, (chunk + 1) * share) for chunk in range(count)]
        for lower, down in enumerate(spans):
            own = packed[down, down]
            flipped = own.T
            even[down, down] = jnp.where(row <= column, own, flipped).astype(bf16)
            above = jnp.where(row == column, 0.0, -flipped)
            odd[down, down] = jnp.where(row > column, own, above).astype(bf16)
            for over in spans[:lower]:
                both, opposite = packed[over, down], packed[down, over]
                even[down, over] = both.astype(bf16)
                even[over, down] = both.T.astype(bf16)
                odd[down, over] = opposite.astype(bf16)
                odd[over, down] = -opposite.T.astype(bf16)

    parted = [split_rows(trial[...]) for trial in trials]
    real = jnp.concatenate([part[0] for part in parted], 0)
    imag = jnp.concatenate([part[1] for part in parted], 0)
    out_ref[:, 0, :] = (matmul(even[...], real) - matmul(odd[...], imag)).astype(bf16)
    out_ref[:, 1, :] = (matmul(even[...], imag) + matmul(odd[...], real)).astype(bf16)


def update_waves(core, mine, others, trials):
    rows, local_g = trials[0].shape
    count = len(trials)
    bands = rows // 2 * count
    width = min(WIDE, local_g)
    return pl.pallas_call(
        functools.partial(update_kernel, count),
        grid=(local_g // width,),
        in_specs=[
            pl.BlockSpec(memory_space=pltpu.SMEM),
            pl.BlockSpec((bands // 2, bands), lambda step: (0, 0)),
            pl.BlockSpec((bands // 2, bands), lambda step: (0, 0)),
        ]
        + [pl.BlockSpec((rows, width), lambda step: (0, step))] * count,
        out_specs=pl.BlockSpec((bands, 2, width), lambda step: (0, 0, step)),
        out_shape=jax.ShapeDtypeStruct((bands, 2, local_g), bf16),
        scratch_shapes=[pltpu.VMEM((bands, bands), bf16)] * 2,
        compiler_params=pltpu.CompilerParams(vmem_limit_bytes=LAST_VMEM_BYTES),
        cost_estimate=pl.CostEstimate(
            flops=8 * bands * bands * local_g,
            bytes_accessed=8 * bands * local_g,
            transcendentals=0,
        ),
    )(core, mine, others, *trials)


def per_device(positions, weights, psi, vloc):
    parts = lax.axis_size("ga")
    bands = psi.shape[1]
    local_g = psi.shape[3]

    weight_float = weights.astype(jnp.float32)
    mixing = weight_float / jnp.sum(weight_float, axis=1, keepdims=True)
    count = 2 if bands // parts % (2 * GROUP) == 0 else 1
    share = bands // count

    sent = pack_first(positions, weights, psi, parts, share)
    waves = [exchange(sent)]
    for chunk in range(1, count):
        block = psi[0, chunk * share : (chunk + 1) * share]
        waves.append(exchange(block.reshape(parts, share // parts, 2, local_g)))
    psi_rows = local_g // sent.shape[3] * share // parts
    oxygens = unpack_oxygens(waves[0][:, psi_rows:], positions.shape[2])
    tables = transform_tables()
    in_plane, along = projector_tables(oxygens)
    grid_potential = vloc[0].reshape(NGRID, PLANE) * (step_size / GVECS)
    line = frequency(jnp.arange(NGRID, dtype=jnp.int32), NGRID) ** 2
    square = line[:, None, None] + line[None, :, None] + line[None, None, :]
    kept = (1.0 - step_size * 0.5 * square).reshape(NGRID, PLANE)
    trials, forces = [], []
    for wave in waves:
        moved, force = make_trial(
            wave, share // parts, local_g, tables, grid_potential, kept, in_plane, along
        )
        trials.append(exchange(moved).reshape(2 * share, local_g))
        forces.append(force)
    force_part = jnp.sum(sum(forces), axis=1) * (2.0 * occupation * nonlocal_strength / GVECS)

    chip, core = lax.axis_index("ga") // 2, lax.axis_index("ga") % 2
    chips = parts // 2
    rows = bands // parts
    same_core = [[2 * number + which for number in range(chips)] for which in range(2)]
    core_ref = core.reshape(1).astype(jnp.int32)
    near_chip = WATERS // chips
    pieces, left = [], force_part
    for _ in range(3):
        pieces.append(lax.reduce_precision(left, 8, 7))
        left = left - pieces[-1]
    pieces = jnp.swapaxes(jnp.stack(pieces).reshape(9, chips, near_chip), 0, 1)
    pieces = jnp.pad(pieces.reshape(chips, -1), ((0, 0), (0, GROUP * bands - 9 * near_chip)))
    pieces = pieces.reshape(chips, GROUP, bands)
    before, margin = None, None
    for chunk, trial in enumerate(trials):
        margin, *others = make_margin(
            chunk == 0, chunk == count - 1, bands, core_ref, trial, pieces, before, margin
        )
        before = trial
    pair = (margin + other_core(others[0], parts).astype(f32)).astype(bf16)
    summed = jnp.sum(exchange(pair, same_core).astype(f32), axis=0)
    summed, found = summed[:rows], summed[rows:].reshape(-1)[: 9 * near_chip]
    found = jnp.sum(found.reshape(3, 3, near_chip), axis=0)
    found = (found + other_core(found, parts)).reshape(3, 2, near_chip // 2)
    oxygen_force = lax.dynamic_index_in_dim(found, core, 1, keepdims=False)
    row = (core * chips + chip) * rows + lax.broadcasted_iota(jnp.int32, (rows, bands), 0)
    column = lax.broadcasted_iota(jnp.int32, (rows, bands), 1)
    own_mixer = (jnp.where(row == column, 1.5, 0.0) - 0.5 * summed).astype(bf16)
    half_mixer = exchange(
        jnp.broadcast_to(own_mixer[None], (chips, rows, bands)), same_core
    ).reshape(bands // 2, bands)
    psi_new = update_waves(core_ref, half_mixer, other_core(half_mixer, parts), trials)

    hydrogen_zero = jnp.zeros_like(oxygen_force)
    dft_force = jnp.stack([oxygen_force, hydrogen_zero, hydrogen_zero], axis=2).reshape(1, 3, -1)

    near_forces = field_forces(positions)
    contracted_force = jnp.einsum("cj,can->jan", mixing, dft_force, precision=highest)
    bead_forces = near_forces + BEADS / CBEADS * contracted_force
    return (psi_new[None], bead_forces)


def solution(mesh):
    placed = (P("rep", None, "ga"), P(), P("rep", None, None, "ga"), P("rep", None))
    return jax.shard_map(
        per_device,
        mesh=mesh,
        in_specs=placed,
        out_specs=(P("rep", None, None, "ga"), P("rep", None, "ga")),
        check_vma=False,
    )
```

```python
import functools

import jax
import jax.numpy as jnp
import numpy as np
from jax import lax
from jax.experimental import pallas as pl
from jax.experimental.pallas import tpu as pltpu
from jax.sharding import PartitionSpec as P

BEADS = 32
CBEADS = 1
WATERS = 256
NGRID = 32
GVECS = 32768


box_length = 20.0
bond_stiff = 0.5
bond_rest = 1.8
spring_stiff = 2.0
width_square = 0.09
step_size = 0.02
nonlocal_strength = 250.0
occupation = 2.0
highest = lax.Precision.HIGHEST
bf16 = jnp.bfloat16
f32 = jnp.float32

PLANE = NGRID * NGRID
GROUP = 8
SLAB = 128
LANES = 256
WIDE = 1024
PIECE = 512
VMEM_BYTES = 56 * 2**20
TAIL_VMEM_BYTES = 60 * 2**20
LAST_VMEM_BYTES = 28 * 2**20


def frequency(index, count):
    signed = jnp.where(index < count // 2, index, index - count)
    return signed.astype(jnp.float32) * (2.0 * jnp.pi / box_length)


def field_forces(positions):
    oxygen = positions[:, :, 0::3]
    toward_one = positions[:, :, 1::3] - oxygen
    toward_two = positions[:, :, 2::3] - oxygen

    def stretch(offset):
        length = jnp.sqrt(jnp.sum(offset * offset, axis=1, keepdims=True))
        return -bond_stiff * (length - bond_rest) * offset / length

    pull_one = stretch(toward_one)
    pull_two = stretch(toward_two)
    bonds = jnp.stack([-(pull_one + pull_two), pull_one, pull_two], axis=3).reshape(positions.shape)
    springs = 2.0 * positions - jnp.roll(positions, 1, axis=0) - jnp.roll(positions, -1, axis=0)
    return bonds - spring_stiff * springs


def inner(left_mat, right_mat):
    return lax.dot_general(
        left_mat, right_mat, (((1,), (1,)), ((), ())), preferred_element_type=jnp.float32
    )


def matmul(left_mat, right_mat):
    return jnp.dot(left_mat, right_mat, preferred_element_type=jnp.float32)


def exchange(blocks, groups=None):
    return lax.all_to_all(
        blocks, "ga", split_axis=0, concat_axis=0, tiled=True, axis_index_groups=groups
    )


def other_core(block, parts):
    return lax.ppermute(block, "ga", [(device, device ^ 1) for device in range(parts)])


def transform_tables():
    index = np.arange(PLANE)
    first, second = index // NGRID, index % NGRID
    product = (first[:, None] * first[None, :] + second[:, None] * second[None, :]) % NGRID
    angle = product * (2.0 * np.pi / NGRID)
    line = np.arange(NGRID)
    x_angle = (line[:, None] * line[None, :] % NGRID) * (2.0 * np.pi / NGRID)
    cosine, sine = np.cos(x_angle), np.sin(x_angle)
    same = np.eye(GROUP)
    rows = 2 * NGRID * GROUP

    def spread(mixing, order):
        return np.einsum("xycd,bm->" + order, mixing, same).reshape(rows, rows)

    def mixed(rr, ri, ir, ii):
        return np.stack([np.stack([rr, ri], -1), np.stack([ir, ii], -1)], -2)

    on_cosine = spread(mixed(cosine, -sine, sine, cosine), "xcbymd")
    on_sine = spread(mixed(-sine, -cosine, cosine, -sine), "xcbymd")
    backward = np.concatenate([on_cosine, on_sine], 1)
    forward = spread(mixed(cosine, sine, -sine, cosine), "xcbydm")
    still, none = np.eye(NGRID), np.zeros((NGRID, NGRID))
    order = spread(mixed(still, none, none, still), "xcbymd")
    return [
        jnp.asarray(table.astype(np.float32), dtype=bf16)
        for table in (np.cos(angle), np.sin(angle), backward, forward, order)
    ]


def cosine_and_sine(phases):
    turns = jnp.round(phases * (0.5 / np.pi))
    left = (phases - turns * 6.28125) - turns * (2.0 * np.pi - 6.28125)
    quarter = left * 0.25
    square = quarter * quarter
    sine = 1.0 + square * (
        -1.0 / 6 + square * (1.0 / 120 + square * (-1.0 / 5040 + square * (1.0 / 362880)))
    )
    sine = quarter * sine
    versine = square * (
        0.5
        + square
        * (-1.0 / 24 + square * (1.0 / 720 + square * (-1.0 / 40320 + square * (1.0 / 3628800))))
    )
    for _ in range(2):
        sine, versine = 2.0 * sine * (1.0 - versine), 2.0 * sine * sine
    return 1.0 - versine, sine


def pack_kernel(positions_ref, weights_ref, psi_ref, out_ref, lanes, stage, in_sems, out_sems):
    parts, total, _, width = out_ref.shape
    extra = lanes.shape[0] // 2
    pieces = psi_ref.shape[3] // width
    own = (total - extra) // pieces
    arrivals = [
        [
            pltpu.make_async_copy(
                psi_ref.at[0, pl.ds(owner * own, own), :, pl.ds(piece * width, width)],
                stage.at[owner, pl.ds(piece * own, own)],
                in_sems.at[owner, piece],
            )
            for piece in range(pieces)
        ]
        for owner in range(parts)
    ]
    for copies in arrivals:
        for copy in copies:
            copy.start()
    weights = weights_ref[...].astype(f32)
    mixing = weights / jnp.sum(weights, axis=1, keepdims=True)
    lanes[...] = jnp.zeros_like(lanes)
    atoms = positions_ref.shape[2]
    for axis in range(3):
        left = jnp.dot(
            mixing, positions_ref[axis], precision=highest, preferred_element_type=jnp.float32
        )
        for piece in range(3):
            sent = left.astype(bf16).astype(f32)
            left = left - sent
            place = (3 * piece + axis) * segment(atoms)
            row, column = place // width, place % width
            lanes[row : row + 1, column : column + atoms] = sent
    for row in range(extra):
        ending = lanes[2 * row : 2 * row + 2, :].astype(bf16)
        for owner in range(parts):
            stage[owner, own * pieces + row] = ending
    departures = [
        pltpu.make_async_copy(stage.at[owner], out_ref.at[owner], out_sems.at[owner])
        for owner in range(parts)
    ]
    for copies, departure in zip(arrivals, departures):
        for copy in copies:
            copy.wait()
        departure.start()
    for copy in departures:
        copy.wait()


def segment(atoms):
    return -(-atoms // 64) * 64


def pack_first(positions, weights, psi, parts, share):
    local_g = psi.shape[3]
    atoms = positions.shape[2]
    width = min(PIECE, local_g)
    pieces = local_g // width
    extra = -(-9 * segment(atoms) // (2 * width))
    block = (parts, pieces * share // parts + extra, 2, width)
    return pl.pallas_call(
        pack_kernel,
        in_specs=[
            pl.BlockSpec(memory_space=pltpu.VMEM),
            pl.BlockSpec(memory_space=pltpu.VMEM),
            pl.BlockSpec(memory_space=pl.ANY),
        ],
        out_specs=pl.BlockSpec(memory_space=pl.ANY),
        out_shape=jax.ShapeDtypeStruct(block, bf16),
        scratch_shapes=[
            pltpu.VMEM((2 * extra, width), f32),
            pltpu.VMEM(block, bf16),
            pltpu.SemaphoreType.DMA((parts, pieces)),
            pltpu.SemaphoreType.DMA((parts,)),
        ],
        compiler_params=pltpu.CompilerParams(vmem_limit_bytes=TAIL_VMEM_BYTES),
        cost_estimate=pl.CostEstimate(
            flops=0, bytes_accessed=8 * share * local_g, transcendentals=0
        ),
    )(jnp.swapaxes(positions, 0, 1), weights, psi)


def unpack_oxygens(rows, atoms):
    parts, each = rows.shape[0], segment(atoms)
    pieces = rows.reshape(parts, -1)[:, : 9 * each].reshape(parts, 3, 3, each)
    found = jnp.sum(pieces[..., 0:atoms:3].astype(f32), axis=1)
    return jnp.swapaxes(found, 0, 1).reshape(3, -1)


def projector_tables(oxygens):
    line = frequency(jnp.arange(NGRID, dtype=jnp.int32), NGRID)
    second, third = jnp.repeat(line, NGRID), jnp.tile(line, NGRID)
    envelope = jnp.exp(-0.5 * width_square * (second * second + third * third))
    cosine, sine = cosine_and_sine(
        oxygens[1][:, None] * second[None, :] + oxygens[2][:, None] * third[None, :]
    )
    in_plane = jnp.concatenate([envelope * cosine, envelope * sine], 0)
    in_plane = jnp.concatenate([in_plane, second * in_plane, third * in_plane], 0).astype(bf16)
    envelope = jnp.exp(-0.5 * width_square * line * line)[:, None]
    cosine, sine = cosine_and_sine(line[:, None] * oxygens[0][None, :])
    cosine, sine = envelope * cosine, envelope * sine
    along = jnp.stack([cosine, sine, line[:, None] * cosine, line[:, None] * sine])
    return in_plane, along


def wave_kernel(
    band_count,
    wave_ref,
    cos_ref,
    sin_ref,
    back_ref,
    fore_ref,
    order_ref,
    pot_ref,
    kept_ref,
    in_plane_ref,
    along_ref,
    out_ref,
    force_ref,
    rows,
    planes,
    turned,
    sums,
    pulls,
    kinetic,
):
    parts, _, _, local_g = out_ref.shape
    width = wave_ref.shape[3]
    waters = along_ref.shape[2]
    band_rows = 2 * GROUP
    all_rows = NGRID * band_rows
    piece = min(width, PLANE)
    first = pl.program_id(0) * GROUP if width < local_g else 0
    for start in range(0, NGRID * PLANE, piece):
        owner, offset = start // local_g, start % local_g
        x, column = start // PLANE, start % PLANE
        bands = pl.ds(first + offset // width * band_count, GROUP)
        block = wave_ref[owner, bands, :, offset % width : offset % width + piece]
        rows[x * band_rows : (x + 1) * band_rows, column : column + piece] = block.reshape(
            band_rows, piece
        )

    @pl.loop(0, sums.shape[0] // 2)
    def _(step):
        columns = pl.ds(pl.multiple_of(step * 2 * SLAB, 2 * SLAB), 2 * SLAB)
        found = inner(rows[...], in_plane_ref[columns, :])
        sums[2 * step] = found[:, :SLAB]
        sums[2 * step + 1] = found[:, SLAB:]

    @pl.when(pl.program_id(0) == 0)
    def _():
        force_ref[...] = jnp.zeros_like(force_ref)

    slabs = waters // SLAB
    real, imag = (pl.ds(first, all_rows // 2, stride=2) for first in range(2))
    shape = (NGRID, GROUP, SLAB)
    for slab in range(slabs):
        inside = slice(slab * SLAB, (slab + 1) * SLAB)
        factors = [along_ref[which, :, inside][:, None, :] for which in range(4)]

        def planewise(factor):
            first = 2 * factor * slabs + slab
            second = first + slabs
            found_re = sums[first, real, :] - sums[second, imag, :]
            found_im = sums[second, real, :] + sums[first, imag, :]
            return found_re.reshape(shape), found_im.reshape(shape)

        def over_x(found, cosines, sines):
            return (
                jnp.sum(found[0] * cosines - found[1] * sines, axis=0),
                jnp.sum(found[0] * sines + found[1] * cosines, axis=0),
            )

        plain = planewise(0)
        proj_re, proj_im = over_x(plain, *factors[:2])
        proj_re = (proj_re * (1.0 / GVECS)).astype(bf16).astype(f32)
        proj_im = (proj_im * (1.0 / GVECS)).astype(bf16).astype(f32)
        for axis in range(3):
            if axis == 0:
                slope_re, slope_im = over_x(plain, *factors[2:])
            else:
                slope_re, slope_im = over_x(planewise(axis), *factors[:2])
            force_ref[axis, :, inside] += proj_re * slope_im - proj_im * slope_re

        cosines, sines = factors[:2]
        strength = step_size * nonlocal_strength
        pull_re = strength * (cosines * proj_re[None] + sines * proj_im[None])
        pull_im = strength * (cosines * proj_im[None] - sines * proj_re[None])
        for half, pull in enumerate(((pull_re, pull_im), (pull_im, -pull_re))):
            both = jnp.concatenate(pull, 1).reshape(all_rows, SLAB).astype(bf16)
            start = half * waters + slab * SLAB
            pulls[:, start : start + SLAB] = both

    @pl.loop(0, PLANE // LANES)
    def _(step):
        columns = pl.ds(pl.multiple_of(step * LANES, LANES), LANES)
        planes[:all_rows, columns] = matmul(rows[...], cos_ref[:, columns]).astype(bf16)
        planes[all_rows:, columns] = matmul(rows[...], sin_ref[:, columns]).astype(bf16)
        moved = matmul(order_ref[...], rows[:, columns]).reshape(NGRID, band_rows, LANES)
        kinetic[:, columns] = (moved * kept_ref[:, columns][:, None, :]).reshape(all_rows, LANES)

    @pl.loop(0, PLANE // LANES)
    def _(step):
        columns = pl.ds(pl.multiple_of(step * LANES, LANES), LANES)
        space = matmul(back_ref[...], planes[:, columns]).reshape(NGRID, band_rows, LANES)
        space = space * pot_ref[:, columns][:, None, :]
        space = space.reshape(all_rows, LANES).astype(bf16)
        waves = matmul(fore_ref[...], space)
        turned[:, columns] = waves.astype(bf16)
        halves = waves.reshape(NGRID, 2, GROUP, LANES)
        other = jnp.concatenate([halves[:, 1:], -halves[:, :1]], 1).reshape(all_rows, LANES)
        rows[:, columns] = other.astype(bf16)

    @pl.loop(0, PLANE // LANES)
    def _(step):
        columns = pl.ds(pl.multiple_of(step * LANES, LANES), LANES)
        waves = matmul(turned[...], cos_ref[:, columns]) + matmul(rows[...], sin_ref[:, columns])
        waves += matmul(pulls[...], in_plane_ref[: 2 * waters, columns])
        planes[:all_rows, columns] = (kinetic[:, columns] - waves).astype(bf16)

    piece = min(local_g, PLANE)
    for start in range(0, NGRID * PLANE, piece):
        owner, offset = start // local_g, start % local_g
        x, column = start // PLANE, start % PLANE
        out_ref[owner, 0, :, offset : offset + piece] = planes[
            x * band_rows : (x + 1) * band_rows, column : column + piece
        ]


def make_trial(waves, band_count, local_g, tables, grid_potential, kept, in_plane, along):
    parts, total, _, width = waves.shape
    if width < local_g:
        taken = pl.BlockSpec((parts, total, 2, width), lambda step: (0, 0, 0, 0))
    else:
        taken = pl.BlockSpec((parts, GROUP, 2, width), lambda step: (0, step, 0, 0))
    waters = along.shape[2]
    steps = band_count // GROUP
    band_rows = 2 * GROUP
    all_rows = NGRID * band_rows
    whole = lambda step: (0, 0)
    return pl.pallas_call(
        functools.partial(wave_kernel, band_count),
        grid=(steps,),
        in_specs=[
            taken,
            pl.BlockSpec((PLANE, PLANE), whole),
            pl.BlockSpec((PLANE, PLANE), whole),
            pl.BlockSpec((all_rows, 2 * all_rows), whole),
            pl.BlockSpec((all_rows, all_rows), whole),
            pl.BlockSpec((all_rows, all_rows), whole),
            pl.BlockSpec((NGRID, PLANE), whole),
            pl.BlockSpec((NGRID, PLANE), whole),
            pl.BlockSpec((6 * waters, PLANE), whole),
            pl.BlockSpec((4, NGRID, waters), lambda step: (0, 0, 0)),
        ],
        out_specs=[
            pl.BlockSpec((parts, 1, band_rows, local_g), lambda step: (0, step, 0, 0)),
            pl.BlockSpec((3, GROUP, waters), lambda step: (0, 0, 0)),
        ],
        out_shape=[
            jax.ShapeDtypeStruct((parts, steps, band_rows, local_g), bf16),
            jax.ShapeDtypeStruct((3, GROUP, waters), f32),
        ],
        scratch_shapes=[
            pltpu.VMEM((all_rows, PLANE), bf16),
            pltpu.VMEM((2 * all_rows, PLANE), bf16),
            pltpu.VMEM((all_rows, PLANE), bf16),
            pltpu.VMEM((6 * waters // SLAB, all_rows, SLAB), f32),
            pltpu.VMEM((all_rows, 2 * waters), bf16),
            pltpu.VMEM((all_rows, PLANE), f32),
        ],
        compiler_params=pltpu.CompilerParams(vmem_limit_bytes=VMEM_BYTES),
        cost_estimate=pl.CostEstimate(
            flops=steps * 2 * all_rows * PLANE * (4 * PLANE + 4 * all_rows + 8 * waters),
            bytes_accessed=8 * steps * band_rows * parts * local_g + 8 * PLANE * PLANE,
            transcendentals=0,
        ),
    )(waves, *tables, grid_potential, kept, in_plane, along)


def split_rows(block):
    count, width = block.shape
    block = block.astype(f32).reshape(count // (2 * GROUP), 2, GROUP, width)
    return [block[:, half].reshape(count // 2, width).astype(bf16) for half in range(2)]


def margin_kernel(first, last, core_ref, trial_ref, *refs):
    refs = list(refs)
    pieces_ref = refs.pop(0) if last else None
    before_ref, margin_ref = (None, None) if first else (refs.pop(0), refs.pop(0))
    mine_ref = refs.pop(0)
    real, imag = split_rows(trial_ref[...])
    share = real.shape[0]

    def margins(other_real, other_imag):
        even = inner(real, other_real) + inner(imag, other_imag)
        odd = inner(imag, other_real) - inner(real, other_imag)
        return even * (1.0 / GVECS), odd * (1.0 / GVECS)

    even, odd = margins(real, imag)
    row = lax.broadcasted_iota(jnp.int32, (share, share), 0)
    column = lax.broadcasted_iota(jnp.int32, (share, share), 1)
    own = jnp.where(row <= column, even, odd)
    if not last:
        mine_ref[...] = own
        return
    other_ref, packed = refs
    start = packed.shape[0] - share
    packed[start:, start:] = own
    if not first:
        even, odd = margins(*split_rows(before_ref[...]))
        packed[:start, :start] = margin_ref[...]
        packed[start:, :start] = odd
        packed[:start, start:] = even
    chips, rows, bands = mine_ref.shape
    rows -= GROUP
    half = chips * rows
    core = core_ref[0]
    mine = packed[pl.ds(pl.multiple_of(core * half, half), half), :]
    others = packed[pl.ds(pl.multiple_of((1 - core) * half, half), half), :]
    mine_ref[:, :rows, :] = mine.reshape(chips, rows, bands)
    other_ref[:, :rows, :] = others.reshape(chips, rows, bands).astype(bf16)

    row = lax.broadcasted_iota(jnp.int32, (half, bands), 0)
    column = lax.broadcasted_iota(jnp.int32, (half, bands), 1)
    place = lax.broadcasted_iota(jnp.int32, (chips, GROUP, bands), 1)

    def diagonal(block, which, spot):
        found = jnp.where(row + which * half == column, block, 0.0)
        found = jnp.sum(found.reshape(chips, rows, bands), axis=1, keepdims=True)
        high = found.astype(bf16).astype(f32)
        placed = jnp.where(place == spot, high, 0.0)
        return jnp.where(place == spot + 1, found - high, placed)

    mine_ref[:, rows:, :] = pieces_ref[...] + diagonal(mine, core, GROUP - 2)
    other_ref[:, rows:, :] = diagonal(others, 1 - core, GROUP - 4).astype(bf16)


def make_margin(first, last, bands, core, trial, pieces, before, margin):
    share, local_g = trial.shape[0] // 2, trial.shape[1]
    chips = pieces.shape[0]
    if last:
        rows = bands // (2 * chips) + GROUP
        out_shape = [
            jax.ShapeDtypeStruct((chips, rows, bands), f32),
            jax.ShapeDtypeStruct((chips, rows, bands), bf16),
        ]
    else:
        out_shape = [jax.ShapeDtypeStruct((share, share), f32)]
    operands = [core, trial] + ([pieces] if last else []) + ([] if first else [before, margin])
    inside = pl.BlockSpec(memory_space=pltpu.VMEM)
    return pl.pallas_call(
        functools.partial(margin_kernel, first, last),
        in_specs=[pl.BlockSpec(memory_space=pltpu.SMEM)] + [inside] * (len(operands) - 1),
        out_specs=[inside] * len(out_shape),
        out_shape=out_shape,
        scratch_shapes=[pltpu.VMEM((bands, bands), f32)] if last else [],
        compiler_params=pltpu.CompilerParams(vmem_limit_bytes=LAST_VMEM_BYTES),
        cost_estimate=pl.CostEstimate(
            flops=8 * share * (share if first else 2 * share) * local_g,
            bytes_accessed=8 * share * local_g,
            transcendentals=0,
        ),
    )(*operands)


def update_kernel(count, core_ref, mine_ref, other_ref, *refs):
    trials, (out_ref, even, odd) = refs[:count], refs[count:]

    @pl.when(pl.program_id(0) == 0)
    def _():
        mine, others = mine_ref[...].astype(f32), other_ref[...].astype(f32)
        first = core_ref[0] == 0
        packed = jnp.concatenate(
            [jnp.where(first, mine, others), jnp.where(first, others, mine)], 0
        )
        share = packed.shape[0] // count
        row = lax.broadcasted_iota(jnp.int32, (share, share), 0)
        column = lax.broadcasted_iota(jnp.int32, (share, share), 1)
        spans = [slice(chunk * share, (chunk + 1) * share) for chunk in range(count)]
        for lower, down in enumerate(spans):
            own = packed[down, down]
            flipped = own.T
            even[down, down] = jnp.where(row <= column, own, flipped).astype(bf16)
            above = jnp.where(row == column, 0.0, -flipped)
            odd[down, down] = jnp.where(row > column, own, above).astype(bf16)
            for over in spans[:lower]:
                both, opposite = packed[over, down], packed[down, over]
                even[down, over] = both.astype(bf16)
                even[over, down] = both.T.astype(bf16)
                odd[down, over] = opposite.astype(bf16)
                odd[over, down] = -opposite.T.astype(bf16)

    parted = [split_rows(trial[...]) for trial in trials]
    real = jnp.concatenate([part[0] for part in parted], 0)
    imag = jnp.concatenate([part[1] for part in parted], 0)
    out_ref[:, 0, :] = (matmul(even[...], real) - matmul(odd[...], imag)).astype(bf16)
    out_ref[:, 1, :] = (matmul(even[...], imag) + matmul(odd[...], real)).astype(bf16)


def update_waves(core, mine, others, trials):
    rows, local_g = trials[0].shape
    count = len(trials)
    bands = rows // 2 * count
    width = min(WIDE, local_g)
    return pl.pallas_call(
        functools.partial(update_kernel, count),
        grid=(local_g // width,),
        in_specs=[
            pl.BlockSpec(memory_space=pltpu.SMEM),
            pl.BlockSpec((bands // 2, bands), lambda step: (0, 0)),
            pl.BlockSpec((bands // 2, bands), lambda step: (0, 0)),
        ]
        + [pl.BlockSpec((rows, width), lambda step: (0, step))] * count,
        out_specs=pl.BlockSpec((bands, 2, width), lambda step: (0, 0, step)),
        out_shape=jax.ShapeDtypeStruct((bands, 2, local_g), bf16),
        scratch_shapes=[pltpu.VMEM((bands, bands), bf16)] * 2,
        compiler_params=pltpu.CompilerParams(vmem_limit_bytes=LAST_VMEM_BYTES),
        cost_estimate=pl.CostEstimate(
            flops=8 * bands * bands * local_g,
            bytes_accessed=8 * bands * local_g,
            transcendentals=0,
        ),
    )(core, mine, others, *trials)


def per_device(positions, weights, psi, vloc):
    parts = lax.axis_size("ga")
    bands = psi.shape[1]
    local_g = psi.shape[3]

    weight_float = weights.astype(jnp.float32)
    mixing = weight_float / jnp.sum(weight_float, axis=1, keepdims=True)
    count = 2 if bands // parts % (2 * GROUP) == 0 else 1
    share = bands // count

    sent = pack_first(positions, weights, psi, parts, share)
    waves = [exchange(sent)]
    for chunk in range(1, count):
        block = psi[0, chunk * share : (chunk + 1) * share]
        waves.append(exchange(block.reshape(parts, share // parts, 2, local_g)))
    psi_rows = local_g // sent.shape[3] * share // parts
    oxygens = unpack_oxygens(waves[0][:, psi_rows:], positions.shape[2])
    tables = transform_tables()
    in_plane, along = projector_tables(oxygens)
    grid_potential = vloc[0].reshape(NGRID, PLANE) * (step_size / GVECS)
    line = frequency(jnp.arange(NGRID, dtype=jnp.int32), NGRID) ** 2
    square = line[:, None, None] + line[None, :, None] + line[None, None, :]
    kept = (1.0 - step_size * 0.5 * square).reshape(NGRID, PLANE)
    trials, forces = [], []
    for wave in waves:
        moved, force = make_trial(
            wave, share // parts, local_g, tables, grid_potential, kept, in_plane, along
        )
        trials.append(exchange(moved).reshape(2 * share, local_g))
        forces.append(force)
    force_part = jnp.sum(sum(forces), axis=1) * (2.0 * occupation * nonlocal_strength / GVECS)

    chip, core = lax.axis_index("ga") // 2, lax.axis_index("ga") % 2
    chips = parts // 2
    rows = bands // parts
    same_core = [[2 * number + which for number in range(chips)] for which in range(2)]
    core_ref = core.reshape(1).astype(jnp.int32)
    near_chip = WATERS // chips
    pieces, left = [], force_part
    for _ in range(3):
        pieces.append(lax.reduce_precision(left, 8, 7))
        left = left - pieces[-1]
    pieces = jnp.swapaxes(jnp.stack(pieces).reshape(9, chips, near_chip), 0, 1)
    pieces = jnp.pad(pieces.reshape(chips, -1), ((0, 0), (0, GROUP * bands - 9 * near_chip)))
    pieces = pieces.reshape(chips, GROUP, bands)
    before, margin = None, None
    for chunk, trial in enumerate(trials):
        margin, *others = make_margin(
            chunk == 0, chunk == count - 1, bands, core_ref, trial, pieces, before, margin
        )
        before = trial
    pair = (margin + other_core(others[0], parts).astype(f32)).astype(bf16)
    summed = jnp.sum(exchange(pair, same_core).astype(f32), axis=0)
    diagonal = jnp.sum(summed[rows + GROUP - 4 :], axis=0, keepdims=True)
    summed, found = summed[:rows], summed[rows:].reshape(-1)[: 9 * near_chip]
    found = jnp.sum(found.reshape(3, 3, near_chip), axis=0)
    found = (found + other_core(found, parts)).reshape(3, 2, near_chip // 2)
    oxygen_force = lax.dynamic_index_in_dim(found, core, 1, keepdims=False)
    row = (core * chips + chip) * rows + lax.broadcasted_iota(jnp.int32, (rows, bands), 0)
    column = lax.broadcasted_iota(jnp.int32, (rows, bands), 1)
    own_mixer = jnp.where(row == column, 1.5 - 0.5 * diagonal, -0.5 * summed).astype(bf16)
    half_mixer = exchange(
        jnp.broadcast_to(own_mixer[None], (chips, rows, bands)), same_core
    ).reshape(bands // 2, bands)
    psi_new = update_waves(core_ref, half_mixer, other_core(half_mixer, parts), trials)

    hydrogen_zero = jnp.zeros_like(oxygen_force)
    dft_force = jnp.stack([oxygen_force, hydrogen_zero, hydrogen_zero], axis=2).reshape(1, 3, -1)

    near_forces = field_forces(positions)
    contracted_force = jnp.einsum("cj,can->jan", mixing, dft_force, precision=highest)
    bead_forces = near_forces + BEADS / CBEADS * contracted_force
    return (psi_new[None], bead_forces)


def solution(mesh):
    placed = (P("rep", None, "ga"), P(), P("rep", None, None, "ga"), P("rep", None))
    return jax.shard_map(
        per_device,
        mesh=mesh,
        in_specs=placed,
        out_specs=(P("rep", None, None, "ga"), P("rep", None, "ga")),
        check_vma=False,
    )
```

```python
import functools

import jax
import jax.numpy as jnp
import numpy as np
from jax import lax
from jax.experimental import pallas as pl
from jax.experimental.pallas import tpu as pltpu
from jax.sharding import PartitionSpec as P

BEADS = 32
CBEADS = 1
WATERS = 256
NGRID = 32
GVECS = 32768


box_length = 20.0
bond_stiff = 0.5
bond_rest = 1.8
spring_stiff = 2.0
width_square = 0.09
step_size = 0.02
nonlocal_strength = 250.0
occupation = 2.0
highest = lax.Precision.HIGHEST
bf16 = jnp.bfloat16
f32 = jnp.float32

PLANE = NGRID * NGRID
GROUP = 8
SLAB = 128
LANES = 256
WIDE = 1024
PIECE = 512
VMEM_BYTES = 56 * 2**20
TAIL_VMEM_BYTES = 60 * 2**20
LAST_VMEM_BYTES = 28 * 2**20


def frequency(index, count):
    signed = jnp.where(index < count // 2, index, index - count)
    return signed.astype(jnp.float32) * (2.0 * jnp.pi / box_length)


def field_forces(positions):
    oxygen = positions[:, :, 0::3]
    toward_one = positions[:, :, 1::3] - oxygen
    toward_two = positions[:, :, 2::3] - oxygen

    def stretch(offset):
        length = jnp.sqrt(jnp.sum(offset * offset, axis=1, keepdims=True))
        return -bond_stiff * (length - bond_rest) * offset / length

    pull_one = stretch(toward_one)
    pull_two = stretch(toward_two)
    bonds = jnp.stack([-(pull_one + pull_two), pull_one, pull_two], axis=3).reshape(positions.shape)
    springs = 2.0 * positions - jnp.roll(positions, 1, axis=0) - jnp.roll(positions, -1, axis=0)
    return bonds - spring_stiff * springs


def inner(left_mat, right_mat):
    return lax.dot_general(
        left_mat, right_mat, (((1,), (1,)), ((), ())), preferred_element_type=jnp.float32
    )


def matmul(left_mat, right_mat):
    return jnp.dot(left_mat, right_mat, preferred_element_type=jnp.float32)


def exchange(blocks, groups=None):
    return lax.all_to_all(
        blocks, "ga", split_axis=0, concat_axis=0, tiled=True, axis_index_groups=groups
    )


def other_core(block, parts):
    return lax.ppermute(block, "ga", [(device, device ^ 1) for device in range(parts)])


def transform_tables():
    index = np.arange(PLANE)
    first, second = index // NGRID, index % NGRID
    product = (first[:, None] * first[None, :] + second[:, None] * second[None, :]) % NGRID
    angle = product * (2.0 * np.pi / NGRID)
    line = np.arange(NGRID)
    x_angle = (line[:, None] * line[None, :] % NGRID) * (2.0 * np.pi / NGRID)
    cosine, sine = np.cos(x_angle), np.sin(x_angle)
    same = np.eye(GROUP)
    rows = 2 * NGRID * GROUP

    def spread(mixing, order):
        return np.einsum("xycd,bm->" + order, mixing, same).reshape(rows, rows)

    def mixed(rr, ri, ir, ii):
        return np.stack([np.stack([rr, ri], -1), np.stack([ir, ii], -1)], -2)

    on_cosine = spread(mixed(cosine, -sine, sine, cosine), "xcbymd")
    on_sine = spread(mixed(-sine, -cosine, cosine, -sine), "xcbymd")
    backward = np.concatenate([on_cosine, on_sine], 1)
    forward = spread(mixed(cosine, sine, -sine, cosine), "xcbydm")
    still, none = np.eye(NGRID), np.zeros((NGRID, NGRID))
    order = spread(mixed(still, none, none, still), "xcbymd")
    return [
        jnp.asarray(table.astype(np.float32), dtype=bf16)
        for table in (np.cos(angle), np.sin(angle), backward, forward, order)
    ]


def cosine_and_sine(phases):
    turns = jnp.round(phases * (0.5 / np.pi))
    left = (phases - turns * 6.28125) - turns * (2.0 * np.pi - 6.28125)
    quarter = left * 0.25
    square = quarter * quarter
    sine = 1.0 + square * (
        -1.0 / 6 + square * (1.0 / 120 + square * (-1.0 / 5040 + square * (1.0 / 362880)))
    )
    sine = quarter * sine
    versine = square * (
        0.5
        + square
        * (-1.0 / 24 + square * (1.0 / 720 + square * (-1.0 / 40320 + square * (1.0 / 3628800))))
    )
    for _ in range(2):
        sine, versine = 2.0 * sine * (1.0 - versine), 2.0 * sine * sine
    return 1.0 - versine, sine


def pack_kernel(positions_ref, weights_ref, psi_ref, out_ref, lanes, stage, in_sems, out_sems):
    parts, total, _, width = out_ref.shape
    extra = lanes.shape[0] // 2
    pieces = psi_ref.shape[3] // width
    own = (total - extra) // pieces
    arrivals = [
        [
            pltpu.make_async_copy(
                psi_ref.at[0, pl.ds(owner * own, own), :, pl.ds(piece * width, width)],
                stage.at[owner, pl.ds(piece * own, own)],
                in_sems.at[owner, piece],
            )
            for piece in range(pieces)
        ]
        for owner in range(parts)
    ]
    for copies in arrivals:
        for copy in copies:
            copy.start()
    weights = weights_ref[...].astype(f32)
    mixing = weights / jnp.sum(weights, axis=1, keepdims=True)
    lanes[...] = jnp.zeros_like(lanes)
    atoms = positions_ref.shape[2]
    for axis in range(3):
        left = jnp.dot(
            mixing, positions_ref[axis], precision=highest, preferred_element_type=jnp.float32
        )
        for piece in range(3):
            sent = left.astype(bf16).astype(f32)
            left = left - sent
            place = (3 * piece + axis) * segment(atoms)
            row, column = place // width, place % width
            lanes[row : row + 1, column : column + atoms] = sent
    for row in range(extra):
        ending = lanes[2 * row : 2 * row + 2, :].astype(bf16)
        for owner in range(parts):
            stage[owner, own * pieces + row] = ending
    departures = [
        pltpu.make_async_copy(stage.at[owner], out_ref.at[owner], out_sems.at[owner])
        for owner in range(parts)
    ]
    for copies, departure in zip(arrivals, departures):
        for copy in copies:
            copy.wait()
        departure.start()
    for copy in departures:
        copy.wait()


def segment(atoms):
    return -(-atoms // 64) * 64


def pack_first(positions, weights, psi, parts, share):
    local_g = psi.shape[3]
    atoms = positions.shape[2]
    width = min(PIECE, local_g)
    pieces = local_g // width
    extra = -(-9 * segment(atoms) // (2 * width))
    block = (parts, pieces * share // parts + extra, 2, width)
    return pl.pallas_call(
        pack_kernel,
        in_specs=[
            pl.BlockSpec(memory_space=pltpu.VMEM),
            pl.BlockSpec(memory_space=pltpu.VMEM),
            pl.BlockSpec(memory_space=pl.ANY),
        ],
        out_specs=pl.BlockSpec(memory_space=pl.ANY),
        out_shape=jax.ShapeDtypeStruct(block, bf16),
        scratch_shapes=[
            pltpu.VMEM((2 * extra, width), f32),
            pltpu.VMEM(block, bf16),
            pltpu.SemaphoreType.DMA((parts, pieces)),
            pltpu.SemaphoreType.DMA((parts,)),
        ],
        compiler_params=pltpu.CompilerParams(vmem_limit_bytes=TAIL_VMEM_BYTES),
        cost_estimate=pl.CostEstimate(
            flops=0, bytes_accessed=8 * share * local_g, transcendentals=0
        ),
    )(jnp.swapaxes(positions, 0, 1), weights, psi)


def unpack_oxygens(rows, atoms):
    parts, each = rows.shape[0], segment(atoms)
    pieces = rows.reshape(parts, -1)[:, : 9 * each].reshape(parts, 3, 3, each)
    found = jnp.sum(pieces[..., 0:atoms:3].astype(f32), axis=1)
    return jnp.swapaxes(found, 0, 1).reshape(3, -1)


def projector_tables(oxygens):
    line = frequency(jnp.arange(NGRID, dtype=jnp.int32), NGRID)
    second, third = jnp.repeat(line, NGRID), jnp.tile(line, NGRID)
    envelope = jnp.exp(-0.5 * width_square * (second * second + third * third))
    cosine, sine = cosine_and_sine(
        oxygens[1][:, None] * second[None, :] + oxygens[2][:, None] * third[None, :]
    )
    in_plane = jnp.concatenate([envelope * cosine, envelope * sine], 0)
    in_plane = jnp.concatenate([in_plane, second * in_plane, third * in_plane], 0).astype(bf16)
    envelope = jnp.exp(-0.5 * width_square * line * line)[:, None]
    cosine, sine = cosine_and_sine(line[:, None] * oxygens[0][None, :])
    cosine, sine = envelope * cosine, envelope * sine
    along = jnp.stack([cosine, sine, line[:, None] * cosine, line[:, None] * sine])
    return in_plane, along


def wave_kernel(
    band_count,
    wave_ref,
    cos_ref,
    sin_ref,
    back_ref,
    fore_ref,
    order_ref,
    pot_ref,
    kept_ref,
    in_plane_ref,
    along_ref,
    out_ref,
    force_ref,
    rows,
    planes,
    turned,
    sums,
    pulls,
    kinetic,
):
    parts, _, _, local_g = out_ref.shape
    width = wave_ref.shape[3]
    waters = along_ref.shape[2]
    band_rows = 2 * GROUP
    all_rows = NGRID * band_rows
    piece = min(width, PLANE)
    first = pl.program_id(0) * GROUP if width < local_g else 0
    for start in range(0, NGRID * PLANE, piece):
        owner, offset = start // local_g, start % local_g
        x, column = start // PLANE, start % PLANE
        bands = pl.ds(first + offset // width * band_count, GROUP)
        block = wave_ref[owner, bands, :, offset % width : offset % width + piece]
        rows[x * band_rows : (x + 1) * band_rows, column : column + piece] = block.reshape(
            band_rows, piece
        )

    @pl.loop(0, sums.shape[0] // 2)
    def _(step):
        columns = pl.ds(pl.multiple_of(step * 2 * SLAB, 2 * SLAB), 2 * SLAB)
        found = inner(rows[...], in_plane_ref[columns, :])
        sums[2 * step] = found[:, :SLAB]
        sums[2 * step + 1] = found[:, SLAB:]

    @pl.when(pl.program_id(0) == 0)
    def _():
        force_ref[...] = jnp.zeros_like(force_ref)

    slabs = waters // SLAB
    real, imag = (pl.ds(first, all_rows // 2, stride=2) for first in range(2))
    shape = (NGRID, GROUP, SLAB)
    for slab in range(slabs):
        inside = slice(slab * SLAB, (slab + 1) * SLAB)
        factors = [along_ref[which, :, inside][:, None, :] for which in range(4)]

        def planewise(factor):
            first = 2 * factor * slabs + slab
            second = first + slabs
            found_re = sums[first, real, :] - sums[second, imag, :]
            found_im = sums[second, real, :] + sums[first, imag, :]
            return found_re.reshape(shape), found_im.reshape(shape)

        def over_x(found, cosines, sines):
            return (
                jnp.sum(found[0] * cosines - found[1] * sines, axis=0),
                jnp.sum(found[0] * sines + found[1] * cosines, axis=0),
            )

        plain = planewise(0)
        proj_re, proj_im = over_x(plain, *factors[:2])
        proj_re = (proj_re * (1.0 / GVECS)).astype(bf16).astype(f32)
        proj_im = (proj_im * (1.0 / GVECS)).astype(bf16).astype(f32)
        for axis in range(3):
            if axis == 0:
                slope_re, slope_im = over_x(plain, *factors[2:])
            else:
                slope_re, slope_im = over_x(planewise(axis), *factors[:2])
            force_ref[axis, :, inside] += proj_re * slope_im - proj_im * slope_re

        cosines, sines = factors[:2]
        strength = step_size * nonlocal_strength
        pull_re = strength * (cosines * proj_re[None] + sines * proj_im[None])
        pull_im = strength * (cosines * proj_im[None] - sines * proj_re[None])
        for half, pull in enumerate(((pull_re, pull_im), (pull_im, -pull_re))):
            both = jnp.concatenate(pull, 1).reshape(all_rows, SLAB).astype(bf16)
            start = half * waters + slab * SLAB
            pulls[:, start : start + SLAB] = both

    @pl.loop(0, PLANE // LANES)
    def _(step):
        columns = pl.ds(pl.multiple_of(step * LANES, LANES), LANES)
        planes[:all_rows, columns] = matmul(rows[...], cos_ref[:, columns]).astype(bf16)
        planes[all_rows:, columns] = matmul(rows[...], sin_ref[:, columns]).astype(bf16)
        moved = matmul(order_ref[...], rows[:, columns]).reshape(NGRID, band_rows, LANES)
        kinetic[:, columns] = (moved * kept_ref[:, columns][:, None, :]).reshape(all_rows, LANES)

    @pl.loop(0, PLANE // LANES)
    def _(step):
        columns = pl.ds(pl.multiple_of(step * LANES, LANES), LANES)
        space = matmul(back_ref[...], planes[:, columns]).reshape(NGRID, band_rows, LANES)
        space = space * pot_ref[:, columns][:, None, :]
        space = space.reshape(all_rows, LANES).astype(bf16)
        waves = matmul(fore_ref[...], space)
        turned[:, columns] = waves.astype(bf16)
        halves = waves.reshape(NGRID, 2, GROUP, LANES)
        other = jnp.concatenate([halves[:, 1:], -halves[:, :1]], 1).reshape(all_rows, LANES)
        rows[:, columns] = other.astype(bf16)

    @pl.loop(0, PLANE // LANES)
    def _(step):
        columns = pl.ds(pl.multiple_of(step * LANES, LANES), LANES)
        waves = matmul(turned[...], cos_ref[:, columns]) + matmul(rows[...], sin_ref[:, columns])
        waves += matmul(pulls[...], in_plane_ref[: 2 * waters, columns])
        planes[:all_rows, columns] = (kinetic[:, columns] - waves).astype(bf16)

    piece = min(local_g, PLANE)
    for start in range(0, NGRID * PLANE, piece):
        owner, offset = start // local_g, start % local_g
        x, column = start // PLANE, start % PLANE
        out_ref[owner, 0, :, offset : offset + piece] = planes[
            x * band_rows : (x + 1) * band_rows, column : column + piece
        ]


def make_trial(waves, band_count, local_g, tables, grid_potential, kept, in_plane, along):
    parts, total, _, width = waves.shape
    if width < local_g:
        taken = pl.BlockSpec((parts, total, 2, width), lambda step: (0, 0, 0, 0))
    else:
        taken = pl.BlockSpec((parts, GROUP, 2, width), lambda step: (0, step, 0, 0))
    waters = along.shape[2]
    steps = band_count // GROUP
    band_rows = 2 * GROUP
    all_rows = NGRID * band_rows
    whole = lambda step: (0, 0)
    return pl.pallas_call(
        functools.partial(wave_kernel, band_count),
        grid=(steps,),
        in_specs=[
            taken,
            pl.BlockSpec((PLANE, PLANE), whole),
            pl.BlockSpec((PLANE, PLANE), whole),
            pl.BlockSpec((all_rows, 2 * all_rows), whole),
            pl.BlockSpec((all_rows, all_rows), whole),
            pl.BlockSpec((all_rows, all_rows), whole),
            pl.BlockSpec((NGRID, PLANE), whole),
            pl.BlockSpec((NGRID, PLANE), whole),
            pl.BlockSpec((6 * waters, PLANE), whole),
            pl.BlockSpec((4, NGRID, waters), lambda step: (0, 0, 0)),
        ],
        out_specs=[
            pl.BlockSpec((parts, 1, band_rows, local_g), lambda step: (0, step, 0, 0)),
            pl.BlockSpec((3, GROUP, waters), lambda step: (0, 0, 0)),
        ],
        out_shape=[
            jax.ShapeDtypeStruct((parts, steps, band_rows, local_g), bf16),
            jax.ShapeDtypeStruct((3, GROUP, waters), f32),
        ],
        scratch_shapes=[
            pltpu.VMEM((all_rows, PLANE), bf16),
            pltpu.VMEM((2 * all_rows, PLANE), bf16),
            pltpu.VMEM((all_rows, PLANE), bf16),
            pltpu.VMEM((6 * waters // SLAB, all_rows, SLAB), f32),
            pltpu.VMEM((all_rows, 2 * waters), bf16),
            pltpu.VMEM((all_rows, PLANE), f32),
        ],
        compiler_params=pltpu.CompilerParams(vmem_limit_bytes=VMEM_BYTES),
        cost_estimate=pl.CostEstimate(
            flops=steps * 2 * all_rows * PLANE * (4 * PLANE + 4 * all_rows + 8 * waters),
            bytes_accessed=8 * steps * band_rows * parts * local_g + 8 * PLANE * PLANE,
            transcendentals=0,
        ),
    )(waves, *tables, grid_potential, kept, in_plane, along)


def split_rows(block):
    count, width = block.shape
    block = block.astype(f32).reshape(count // (2 * GROUP), 2, GROUP, width)
    return [block[:, half].reshape(count // 2, width).astype(bf16) for half in range(2)]


def margin_kernel(first, last, core_ref, trial_ref, *refs):
    refs = list(refs)
    pieces_ref = refs.pop(0) if last else None
    before_ref, margin_ref = (None, None) if first else (refs.pop(0), refs.pop(0))
    mine_ref = refs.pop(0)
    real, imag = split_rows(trial_ref[...])
    share = real.shape[0]

    def margins(other_real, other_imag):
        even = inner(real, other_real) + inner(imag, other_imag)
        odd = inner(imag, other_real) - inner(real, other_imag)
        return even * (1.0 / GVECS), odd * (1.0 / GVECS)

    even = (inner(real, real) + inner(imag, imag)) * (1.0 / GVECS)
    odd = inner(imag, real) * (1.0 / GVECS)
    odd = odd - odd.T
    row = lax.broadcasted_iota(jnp.int32, (share, share), 0)
    column = lax.broadcasted_iota(jnp.int32, (share, share), 1)
    own = jnp.where(row <= column, even, odd)
    if not last:
        mine_ref[...] = own
        return
    other_ref, packed = refs
    start = packed.shape[0] - share
    packed[start:, start:] = own
    if not first:
        even, odd = margins(*split_rows(before_ref[...]))
        packed[:start, :start] = margin_ref[...]
        packed[start:, :start] = odd
        packed[:start, start:] = even
    chips, rows, bands = mine_ref.shape
    rows -= GROUP
    half = chips * rows
    core = core_ref[0]
    mine = packed[pl.ds(pl.multiple_of(core * half, half), half), :]
    others = packed[pl.ds(pl.multiple_of((1 - core) * half, half), half), :]
    mine_ref[:, :rows, :] = mine.reshape(chips, rows, bands)
    other_ref[:, :rows, :] = others.reshape(chips, rows, bands).astype(bf16)

    row = lax.broadcasted_iota(jnp.int32, (half, bands), 0)
    column = lax.broadcasted_iota(jnp.int32, (half, bands), 1)
    place = lax.broadcasted_iota(jnp.int32, (chips, GROUP, bands), 1)

    def diagonal(block, which, spot):
        found = jnp.where(row + which * half == column, block, 0.0)
        found = jnp.sum(found.reshape(chips, rows, bands), axis=1, keepdims=True)
        high = found.astype(bf16).astype(f32)
        placed = jnp.where(place == spot, high, 0.0)
        return jnp.where(place == spot + 1, found - high, placed)

    mine_ref[:, rows:, :] = pieces_ref[...] + diagonal(mine, core, GROUP - 2)
    other_ref[:, rows:, :] = diagonal(others, 1 - core, GROUP - 4).astype(bf16)


def make_margin(first, last, bands, core, trial, pieces, before, margin):
    share, local_g = trial.shape[0] // 2, trial.shape[1]
    chips = pieces.shape[0]
    if last:
        rows = bands // (2 * chips) + GROUP
        out_shape = [
            jax.ShapeDtypeStruct((chips, rows, bands), f32),
            jax.ShapeDtypeStruct((chips, rows, bands), bf16),
        ]
    else:
        out_shape = [jax.ShapeDtypeStruct((share, share), f32)]
    operands = [core, trial] + ([pieces] if last else []) + ([] if first else [before, margin])
    inside = pl.BlockSpec(memory_space=pltpu.VMEM)
    return pl.pallas_call(
        functools.partial(margin_kernel, first, last),
        in_specs=[pl.BlockSpec(memory_space=pltpu.SMEM)] + [inside] * (len(operands) - 1),
        out_specs=[inside] * len(out_shape),
        out_shape=out_shape,
        scratch_shapes=[pltpu.VMEM((bands, bands), f32)] if last else [],
        compiler_params=pltpu.CompilerParams(vmem_limit_bytes=LAST_VMEM_BYTES),
        cost_estimate=pl.CostEstimate(
            flops=8 * share * (share if first else 2 * share) * local_g,
            bytes_accessed=8 * share * local_g,
            transcendentals=0,
        ),
    )(*operands)


def update_kernel(count, core_ref, mine_ref, other_ref, *refs):
    trials, (out_ref, even, odd) = refs[:count], refs[count:]

    @pl.when(pl.program_id(0) == 0)
    def _():
        mine, others = mine_ref[...], other_ref[...]
        first = core_ref[0] == 0
        packed = jnp.concatenate(
            [jnp.where(first, mine, others), jnp.where(first, others, mine)], 0
        )
        share = packed.shape[0] // count
        row = lax.broadcasted_iota(jnp.int32, (share, share), 0)
        column = lax.broadcasted_iota(jnp.int32, (share, share), 1)
        spans = [slice(chunk * share, (chunk + 1) * share) for chunk in range(count)]
        for lower, down in enumerate(spans):
            own = packed[down, down]
            flipped = own.T
            even[down, down] = jnp.where(row <= column, own, flipped)
            above = jnp.where(row == column, jnp.zeros_like(own), -flipped)
            odd[down, down] = jnp.where(row > column, own, above)
            for over in spans[:lower]:
                both, opposite = packed[over, down], packed[down, over]
                even[down, over] = both
                even[over, down] = both.T
                odd[down, over] = opposite
                odd[over, down] = -opposite.T

    parted = [split_rows(trial[...]) for trial in trials]
    real = jnp.concatenate([part[0] for part in parted], 0)
    imag = jnp.concatenate([part[1] for part in parted], 0)
    both = jnp.concatenate([real, imag], 0)
    out_ref[:, 0, :] = matmul(jnp.concatenate([even[...], -odd[...]], 1), both).astype(bf16)
    out_ref[:, 1, :] = matmul(jnp.concatenate([odd[...], even[...]], 1), both).astype(bf16)


def update_waves(core, mine, others, trials):
    rows, local_g = trials[0].shape
    count = len(trials)
    bands = rows // 2 * count
    width = min(WIDE, local_g)
    return pl.pallas_call(
        functools.partial(update_kernel, count),
        grid=(local_g // width,),
        in_specs=[
            pl.BlockSpec(memory_space=pltpu.SMEM),
            pl.BlockSpec((bands // 2, bands), lambda step: (0, 0)),
            pl.BlockSpec((bands // 2, bands), lambda step: (0, 0)),
        ]
        + [pl.BlockSpec((rows, width), lambda step: (0, step))] * count,
        out_specs=pl.BlockSpec((bands, 2, width), lambda step: (0, 0, step)),
        out_shape=jax.ShapeDtypeStruct((bands, 2, local_g), bf16),
        scratch_shapes=[pltpu.VMEM((bands, bands), bf16)] * 2,
        compiler_params=pltpu.CompilerParams(vmem_limit_bytes=LAST_VMEM_BYTES),
        cost_estimate=pl.CostEstimate(
            flops=8 * bands * bands * local_g,
            bytes_accessed=8 * bands * local_g,
            transcendentals=0,
        ),
    )(core, mine, others, *trials)


def per_device(positions, weights, psi, vloc):
    parts = lax.axis_size("ga")
    bands = psi.shape[1]
    local_g = psi.shape[3]

    weight_float = weights.astype(jnp.float32)
    mixing = weight_float / jnp.sum(weight_float, axis=1, keepdims=True)
    count = 2 if bands // parts % (2 * GROUP) == 0 else 1
    share = bands // count

    sent = pack_first(positions, weights, psi, parts, share)
    waves = [exchange(sent)]
    for chunk in range(1, count):
        block = psi[0, chunk * share : (chunk + 1) * share]
        waves.append(exchange(block.reshape(parts, share // parts, 2, local_g)))
    psi_rows = local_g // sent.shape[3] * share // parts
    oxygens = unpack_oxygens(waves[0][:, psi_rows:], positions.shape[2])
    tables = transform_tables()
    in_plane, along = projector_tables(oxygens)
    grid_potential = vloc[0].reshape(NGRID, PLANE) * (step_size / GVECS)
    line = frequency(jnp.arange(NGRID, dtype=jnp.int32), NGRID) ** 2
    square = line[:, None, None] + line[None, :, None] + line[None, None, :]
    kept = (1.0 - step_size * 0.5 * square).reshape(NGRID, PLANE)
    trials, forces = [], []
    for wave in waves:
        moved, force = make_trial(
            wave, share // parts, local_g, tables, grid_potential, kept, in_plane, along
        )
        trials.append(exchange(moved).reshape(2 * share, local_g))
        forces.append(force)
    force_part = jnp.sum(sum(forces), axis=1) * (2.0 * occupation * nonlocal_strength / GVECS)

    chip, core = lax.axis_index("ga") // 2, lax.axis_index("ga") % 2
    chips = parts // 2
    rows = bands // parts
    same_core = [[2 * number + which for number in range(chips)] for which in range(2)]
    core_ref = core.reshape(1).astype(jnp.int32)
    near_chip = WATERS // chips
    pieces, left = [], force_part
    for _ in range(3):
        pieces.append(lax.reduce_precision(left, 8, 7))
        left = left - pieces[-1]
    pieces = jnp.swapaxes(jnp.stack(pieces).reshape(9, chips, near_chip), 0, 1)
    pieces = jnp.pad(pieces.reshape(chips, -1), ((0, 0), (0, GROUP * bands - 9 * near_chip)))
    pieces = pieces.reshape(chips, GROUP, bands)
    before, margin = None, None
    for chunk, trial in enumerate(trials):
        margin, *others = make_margin(
            chunk == 0, chunk == count - 1, bands, core_ref, trial, pieces, before, margin
        )
        before = trial
    pair = (margin + other_core(others[0], parts).astype(f32)).astype(bf16)
    summed = jnp.sum(exchange(pair, same_core).astype(f32), axis=0)
    diagonal = jnp.sum(summed[rows + GROUP - 4 :], axis=0, keepdims=True)
    summed, found = summed[:rows], summed[rows:].reshape(-1)[: 9 * near_chip]
    found = jnp.sum(found.reshape(3, 3, near_chip), axis=0)
    found = (found + other_core(found, parts)).reshape(3, 2, near_chip // 2)
    oxygen_force = lax.dynamic_index_in_dim(found, core, 1, keepdims=False)
    row = (core * chips + chip) * rows + lax.broadcasted_iota(jnp.int32, (rows, bands), 0)
    column = lax.broadcasted_iota(jnp.int32, (rows, bands), 1)
    own_mixer = jnp.where(row == column, 1.5 - 0.5 * diagonal, -0.5 * summed).astype(bf16)
    half_mixer = exchange(
        jnp.broadcast_to(own_mixer[None], (chips, rows, bands)), same_core
    ).reshape(bands // 2, bands)
    psi_new = update_waves(core_ref, half_mixer, other_core(half_mixer, parts), trials)

    hydrogen_zero = jnp.zeros_like(oxygen_force)
    dft_force = jnp.stack([oxygen_force, hydrogen_zero, hydrogen_zero], axis=2).reshape(1, 3, -1)

    near_forces = field_forces(positions)
    contracted_force = jnp.einsum("cj,can->jan", mixing, dft_force, precision=highest)
    bead_forces = near_forces + BEADS / CBEADS * contracted_force
    return (psi_new[None], bead_forces)


def solution(mesh):
    placed = (P("rep", None, "ga"), P(), P("rep", None, None, "ga"), P("rep", None))
    return jax.shard_map(
        per_device,
        mesh=mesh,
        in_specs=placed,
        out_specs=(P("rep", None, None, "ga"), P("rep", None, "ga")),
        check_vma=False,
    )
```

```python
import functools

import jax
import jax.numpy as jnp
import numpy as np
from jax import lax
from jax.experimental import pallas as pl
from jax.experimental.pallas import tpu as pltpu
from jax.sharding import PartitionSpec as P

BEADS = 32
CBEADS = 1
WATERS = 256
NGRID = 32
GVECS = 32768


box_length = 20.0
bond_stiff = 0.5
bond_rest = 1.8
spring_stiff = 2.0
width_square = 0.09
step_size = 0.02
nonlocal_strength = 250.0
occupation = 2.0
highest = lax.Precision.HIGHEST
bf16 = jnp.bfloat16
f32 = jnp.float32

PLANE = NGRID * NGRID
GROUP = 8
SLAB = 128
LANES = 256
WIDE = 512
PIECE = 512
VMEM_BYTES = 56 * 2**20
TAIL_VMEM_BYTES = 60 * 2**20
LAST_VMEM_BYTES = 28 * 2**20


def frequency(index, count):
    signed = jnp.where(index < count // 2, index, index - count)
    return signed.astype(jnp.float32) * (2.0 * jnp.pi / box_length)


def field_forces(positions):
    oxygen = positions[:, :, 0::3]
    toward_one = positions[:, :, 1::3] - oxygen
    toward_two = positions[:, :, 2::3] - oxygen

    def stretch(offset):
        length = jnp.sqrt(jnp.sum(offset * offset, axis=1, keepdims=True))
        return -bond_stiff * (length - bond_rest) * offset / length

    pull_one = stretch(toward_one)
    pull_two = stretch(toward_two)
    bonds = jnp.stack([-(pull_one + pull_two), pull_one, pull_two], axis=3).reshape(positions.shape)
    springs = 2.0 * positions - jnp.roll(positions, 1, axis=0) - jnp.roll(positions, -1, axis=0)
    return bonds - spring_stiff * springs


def inner(left_mat, right_mat):
    return lax.dot_general(
        left_mat, right_mat, (((1,), (1,)), ((), ())), preferred_element_type=jnp.float32
    )


def matmul(left_mat, right_mat):
    return jnp.dot(left_mat, right_mat, preferred_element_type=jnp.float32)


def exchange(blocks, groups=None):
    return lax.all_to_all(
        blocks, "ga", split_axis=0, concat_axis=0, tiled=True, axis_index_groups=groups
    )


def other_core(block, parts):
    return lax.ppermute(block, "ga", [(device, device ^ 1) for device in range(parts)])


def transform_tables():
    index = np.arange(PLANE)
    first, second = index // NGRID, index % NGRID
    product = (first[:, None] * first[None, :] + second[:, None] * second[None, :]) % NGRID
    angle = product * (2.0 * np.pi / NGRID)
    line = np.arange(NGRID)
    x_angle = (line[:, None] * line[None, :] % NGRID) * (2.0 * np.pi / NGRID)
    cosine, sine = np.cos(x_angle), np.sin(x_angle)
    same = np.eye(GROUP)
    rows = 2 * NGRID * GROUP

    def spread(mixing, order):
        return np.einsum("xycd,bm->" + order, mixing, same).reshape(rows, rows)

    def mixed(rr, ri, ir, ii):
        return np.stack([np.stack([rr, ri], -1), np.stack([ir, ii], -1)], -2)

    on_cosine = spread(mixed(cosine, -sine, sine, cosine), "xcbymd")
    on_sine = spread(mixed(-sine, -cosine, cosine, -sine), "xcbymd")
    backward = np.concatenate([on_cosine, on_sine], 1)
    forward = spread(mixed(cosine, sine, -sine, cosine), "xcbydm")
    still, none = np.eye(NGRID), np.zeros((NGRID, NGRID))
    order = spread(mixed(still, none, none, still), "xcbymd")
    return [
        jnp.asarray(table.astype(np.float32), dtype=bf16)
        for table in (np.cos(angle), np.sin(angle), backward, forward, order)
    ]


def cosine_and_sine(phases):
    turns = jnp.round(phases * (0.5 / np.pi))
    left = (phases - turns * 6.28125) - turns * (2.0 * np.pi - 6.28125)
    quarter = left * 0.25
    square = quarter * quarter
    sine = 1.0 + square * (
        -1.0 / 6 + square * (1.0 / 120 + square * (-1.0 / 5040 + square * (1.0 / 362880)))
    )
    sine = quarter * sine
    versine = square * (
        0.5
        + square
        * (-1.0 / 24 + square * (1.0 / 720 + square * (-1.0 / 40320 + square * (1.0 / 3628800))))
    )
    for _ in range(2):
        sine, versine = 2.0 * sine * (1.0 - versine), 2.0 * sine * sine
    return 1.0 - versine, sine


def pack_kernel(positions_ref, weights_ref, psi_ref, out_ref, lanes, stage, in_sems, out_sems):
    parts, total, _, width = out_ref.shape
    extra = lanes.shape[0] // 2
    pieces = psi_ref.shape[3] // width
    own = (total - extra) // pieces
    arrivals = [
        [
            pltpu.make_async_copy(
                psi_ref.at[0, pl.ds(owner * own, own), :, pl.ds(piece * width, width)],
                stage.at[owner, pl.ds(piece * own, own)],
                in_sems.at[owner, piece],
            )
            for piece in range(pieces)
        ]
        for owner in range(parts)
    ]
    for copies in arrivals:
        for copy in copies:
            copy.start()
    weights = weights_ref[...].astype(f32)
    mixing = weights / jnp.sum(weights, axis=1, keepdims=True)
    lanes[...] = jnp.zeros_like(lanes)
    atoms = positions_ref.shape[2]
    for axis in range(3):
        left = jnp.dot(
            mixing, positions_ref[axis], precision=highest, preferred_element_type=jnp.float32
        )
        for piece in range(3):
            sent = left.astype(bf16).astype(f32)
            left = left - sent
            place = (3 * piece + axis) * segment(atoms)
            row, column = place // width, place % width
            lanes[row : row + 1, column : column + atoms] = sent
    for row in range(extra):
        ending = lanes[2 * row : 2 * row + 2, :].astype(bf16)
        for owner in range(parts):
            stage[owner, own * pieces + row] = ending
    departures = [
        pltpu.make_async_copy(stage.at[owner], out_ref.at[owner], out_sems.at[owner])
        for owner in range(parts)
    ]
    for copies, departure in zip(arrivals, departures):
        for copy in copies:
            copy.wait()
        departure.start()
    for copy in departures:
        copy.wait()


def segment(atoms):
    return -(-atoms // 64) * 64


def pack_first(positions, weights, psi, parts, share):
    local_g = psi.shape[3]
    atoms = positions.shape[2]
    width = min(PIECE, local_g)
    pieces = local_g // width
    extra = -(-9 * segment(atoms) // (2 * width))
    block = (parts, pieces * share // parts + extra, 2, width)
    return pl.pallas_call(
        pack_kernel,
        in_specs=[
            pl.BlockSpec(memory_space=pltpu.VMEM),
            pl.BlockSpec(memory_space=pltpu.VMEM),
            pl.BlockSpec(memory_space=pl.ANY),
        ],
        out_specs=pl.BlockSpec(memory_space=pl.ANY),
        out_shape=jax.ShapeDtypeStruct(block, bf16),
        scratch_shapes=[
            pltpu.VMEM((2 * extra, width), f32),
            pltpu.VMEM(block, bf16),
            pltpu.SemaphoreType.DMA((parts, pieces)),
            pltpu.SemaphoreType.DMA((parts,)),
        ],
        compiler_params=pltpu.CompilerParams(vmem_limit_bytes=TAIL_VMEM_BYTES),
        cost_estimate=pl.CostEstimate(
            flops=0, bytes_accessed=8 * share * local_g, transcendentals=0
        ),
    )(jnp.swapaxes(positions, 0, 1), weights, psi)


def unpack_oxygens(rows, atoms):
    parts, each = rows.shape[0], segment(atoms)
    pieces = rows.reshape(parts, -1)[:, : 9 * each].reshape(parts, 3, 3, each)
    found = jnp.sum(pieces[..., 0:atoms:3].astype(f32), axis=1)
    return jnp.swapaxes(found, 0, 1).reshape(3, -1)


def projector_tables(oxygens):
    line = frequency(jnp.arange(NGRID, dtype=jnp.int32), NGRID)
    second, third = jnp.repeat(line, NGRID), jnp.tile(line, NGRID)
    envelope = jnp.exp(-0.5 * width_square * (second * second + third * third))
    cosine, sine = cosine_and_sine(
        oxygens[1][:, None] * second[None, :] + oxygens[2][:, None] * third[None, :]
    )
    in_plane = jnp.concatenate([envelope * cosine, envelope * sine], 0)
    in_plane = jnp.concatenate([in_plane, second * in_plane, third * in_plane], 0).astype(bf16)
    envelope = jnp.exp(-0.5 * width_square * line * line)[:, None]
    cosine, sine = cosine_and_sine(line[:, None] * oxygens[0][None, :])
    cosine, sine = envelope * cosine, envelope * sine
    along = jnp.stack([cosine, sine, line[:, None] * cosine, line[:, None] * sine])
    return in_plane, along


def wave_kernel(
    band_count,
    wave_ref,
    cos_ref,
    sin_ref,
    back_ref,
    fore_ref,
    order_ref,
    pot_ref,
    kept_ref,
    in_plane_ref,
    along_ref,
    out_ref,
    force_ref,
    rows,
    planes,
    turned,
    sums,
    pulls,
    kinetic,
):
    parts, _, _, local_g = out_ref.shape
    width = wave_ref.shape[3]
    waters = along_ref.shape[2]
    band_rows = 2 * GROUP
    all_rows = NGRID * band_rows
    piece = min(width, PLANE)
    first = pl.program_id(0) * GROUP if width < local_g else 0
    for start in range(0, NGRID * PLANE, piece):
        owner, offset = start // local_g, start % local_g
        x, column = start // PLANE, start % PLANE
        bands = pl.ds(first + offset // width * band_count, GROUP)
        block = wave_ref[owner, bands, :, offset % width : offset % width + piece]
        rows[x * band_rows : (x + 1) * band_rows, column : column + piece] = block.reshape(
            band_rows, piece
        )

    @pl.loop(0, sums.shape[0] // 2)
    def _(step):
        columns = pl.ds(pl.multiple_of(step * 2 * SLAB, 2 * SLAB), 2 * SLAB)
        found = inner(rows[...], in_plane_ref[columns, :])
        sums[2 * step] = found[:, :SLAB]
        sums[2 * step + 1] = found[:, SLAB:]

    @pl.when(pl.program_id(0) == 0)
    def _():
        force_ref[...] = jnp.zeros_like(force_ref)

    slabs = waters // SLAB
    real, imag = (pl.ds(first, all_rows // 2, stride=2) for first in range(2))
    shape = (NGRID, GROUP, SLAB)
    for slab in range(slabs):
        inside = slice(slab * SLAB, (slab + 1) * SLAB)
        factors = [along_ref[which, :, inside][:, None, :] for which in range(4)]

        def planewise(factor):
            first = 2 * factor * slabs + slab
            second = first + slabs
            found_re = sums[first, real, :] - sums[second, imag, :]
            found_im = sums[second, real, :] + sums[first, imag, :]
            return found_re.reshape(shape), found_im.reshape(shape)

        def over_x(found, cosines, sines):
            return (
                jnp.sum(found[0] * cosines - found[1] * sines, axis=0),
                jnp.sum(found[0] * sines + found[1] * cosines, axis=0),
            )

        plain = planewise(0)
        proj_re, proj_im = over_x(plain, *factors[:2])
        proj_re = (proj_re * (1.0 / GVECS)).astype(bf16).astype(f32)
        proj_im = (proj_im * (1.0 / GVECS)).astype(bf16).astype(f32)
        for axis in range(3):
            if axis == 0:
                slope_re, slope_im = over_x(plain, *factors[2:])
            else:
                slope_re, slope_im = over_x(planewise(axis), *factors[:2])
            force_ref[axis, :, inside] += proj_re * slope_im - proj_im * slope_re

        cosines, sines = factors[:2]
        strength = step_size * nonlocal_strength
        pull_re = strength * (cosines * proj_re[None] + sines * proj_im[None])
        pull_im = strength * (cosines * proj_im[None] - sines * proj_re[None])
        for half, pull in enumerate(((pull_re, pull_im), (pull_im, -pull_re))):
            both = jnp.concatenate(pull, 1).reshape(all_rows, SLAB).astype(bf16)
            start = half * waters + slab * SLAB
            pulls[:, start : start + SLAB] = both

    @pl.loop(0, PLANE // LANES)
    def _(step):
        columns = pl.ds(pl.multiple_of(step * LANES, LANES), LANES)
        planes[:all_rows, columns] = matmul(rows[...], cos_ref[:, columns]).astype(bf16)
        planes[all_rows:, columns] = matmul(rows[...], sin_ref[:, columns]).astype(bf16)
        moved = matmul(order_ref[...], rows[:, columns]).reshape(NGRID, band_rows, LANES)
        kinetic[:, columns] = (moved * kept_ref[:, columns][:, None, :]).reshape(all_rows, LANES)

    @pl.loop(0, PLANE // LANES)
    def _(step):
        columns = pl.ds(pl.multiple_of(step * LANES, LANES), LANES)
        space = matmul(back_ref[...], planes[:, columns]).reshape(NGRID, band_rows, LANES)
        space = space * pot_ref[:, columns][:, None, :]
        space = space.reshape(all_rows, LANES).astype(bf16)
        waves = matmul(fore_ref[...], space)
        turned[:, columns] = waves.astype(bf16)
        halves = waves.reshape(NGRID, 2, GROUP, LANES)
        other = jnp.concatenate([halves[:, 1:], -halves[:, :1]], 1).reshape(all_rows, LANES)
        rows[:, columns] = other.astype(bf16)

    @pl.loop(0, PLANE // LANES)
    def _(step):
        columns = pl.ds(pl.multiple_of(step * LANES, LANES), LANES)
        waves = matmul(turned[...], cos_ref[:, columns]) + matmul(rows[...], sin_ref[:, columns])
        waves += matmul(pulls[...], in_plane_ref[: 2 * waters, columns])
        planes[:all_rows, columns] = (kinetic[:, columns] - waves).astype(bf16)

    piece = min(local_g, PLANE)
    for start in range(0, NGRID * PLANE, piece):
        owner, offset = start // local_g, start % local_g
        x, column = start // PLANE, start % PLANE
        out_ref[owner, 0, :, offset : offset + piece] = planes[
            x * band_rows : (x + 1) * band_rows, column : column + piece
        ]


def make_trial(waves, band_count, local_g, tables, grid_potential, kept, in_plane, along):
    parts, total, _, width = waves.shape
    if width < local_g:
        taken = pl.BlockSpec((parts, total, 2, width), lambda step: (0, 0, 0, 0))
    else:
        taken = pl.BlockSpec((parts, GROUP, 2, width), lambda step: (0, step, 0, 0))
    waters = along.shape[2]
    steps = band_count // GROUP
    band_rows = 2 * GROUP
    all_rows = NGRID * band_rows
    whole = lambda step: (0, 0)
    return pl.pallas_call(
        functools.partial(wave_kernel, band_count),
        grid=(steps,),
        in_specs=[
            taken,
            pl.BlockSpec((PLANE, PLANE), whole),
            pl.BlockSpec((PLANE, PLANE), whole),
            pl.BlockSpec((all_rows, 2 * all_rows), whole),
            pl.BlockSpec((all_rows, all_rows), whole),
            pl.BlockSpec((all_rows, all_rows), whole),
            pl.BlockSpec((NGRID, PLANE), whole),
            pl.BlockSpec((NGRID, PLANE), whole),
            pl.BlockSpec((6 * waters, PLANE), whole),
            pl.BlockSpec((4, NGRID, waters), lambda step: (0, 0, 0)),
        ],
        out_specs=[
            pl.BlockSpec((parts, 1, band_rows, local_g), lambda step: (0, step, 0, 0)),
            pl.BlockSpec((3, GROUP, waters), lambda step: (0, 0, 0)),
        ],
        out_shape=[
            jax.ShapeDtypeStruct((parts, steps, band_rows, local_g), bf16),
            jax.ShapeDtypeStruct((3, GROUP, waters), f32),
        ],
        scratch_shapes=[
            pltpu.VMEM((all_rows, PLANE), bf16),
            pltpu.VMEM((2 * all_rows, PLANE), bf16),
            pltpu.VMEM((all_rows, PLANE), bf16),
            pltpu.VMEM((6 * waters // SLAB, all_rows, SLAB), f32),
            pltpu.VMEM((all_rows, 2 * waters), bf16),
            pltpu.VMEM((all_rows, PLANE), f32),
        ],
        compiler_params=pltpu.CompilerParams(vmem_limit_bytes=VMEM_BYTES),
        cost_estimate=pl.CostEstimate(
            flops=steps * 2 * all_rows * PLANE * (4 * PLANE + 4 * all_rows + 8 * waters),
            bytes_accessed=8 * steps * band_rows * parts * local_g + 8 * PLANE * PLANE,
            transcendentals=0,
        ),
    )(waves, *tables, grid_potential, kept, in_plane, along)


def split_rows(block):
    count, width = block.shape
    block = block.astype(f32).reshape(count // (2 * GROUP), 2, GROUP, width)
    return [block[:, half].reshape(count // 2, width).astype(bf16) for half in range(2)]


def margin_kernel(first, last, core_ref, trial_ref, *refs):
    refs = list(refs)
    pieces_ref = refs.pop(0) if last else None
    before_ref, margin_ref = (None, None) if first else (refs.pop(0), refs.pop(0))
    mine_ref = refs.pop(0)
    real, imag = split_rows(trial_ref[...])
    share = real.shape[0]

    def margins(other_real, other_imag):
        even = inner(real, other_real) + inner(imag, other_imag)
        odd = inner(imag, other_real) - inner(real, other_imag)
        return even * (1.0 / GVECS), odd * (1.0 / GVECS)

    even = (inner(real, real) + inner(imag, imag)) * (1.0 / GVECS)
    odd = inner(imag, real) * (1.0 / GVECS)
    odd = odd - odd.T
    row = lax.broadcasted_iota(jnp.int32, (share, share), 0)
    column = lax.broadcasted_iota(jnp.int32, (share, share), 1)
    own = jnp.where(row <= column, even, odd)
    if not last:
        mine_ref[...] = own
        return
    other_ref, packed = refs
    start = packed.shape[0] - share
    packed[start:, start:] = own
    if not first:
        even, odd = margins(*split_rows(before_ref[...]))
        packed[:start, :start] = margin_ref[...]
        packed[start:, :start] = odd
        packed[:start, start:] = even
    chips, rows, bands = mine_ref.shape
    rows -= GROUP
    half = chips * rows
    core = core_ref[0]
    mine = packed[pl.ds(pl.multiple_of(core * half, half), half), :]
    others = packed[pl.ds(pl.multiple_of((1 - core) * half, half), half), :]
    mine_ref[:, :rows, :] = mine.reshape(chips, rows, bands)
    other_ref[:, :rows, :] = others.reshape(chips, rows, bands).astype(bf16)

    row = lax.broadcasted_iota(jnp.int32, (half, bands), 0)
    column = lax.broadcasted_iota(jnp.int32, (half, bands), 1)
    place = lax.broadcasted_iota(jnp.int32, (chips, GROUP, bands), 1)

    def diagonal(block, which, spot):
        found = jnp.where(row + which * half == column, block, 0.0)
        found = jnp.sum(found.reshape(chips, rows, bands), axis=1, keepdims=True)
        high = found.astype(bf16).astype(f32)
        placed = jnp.where(place == spot, high, 0.0)
        return jnp.where(place == spot + 1, found - high, placed)

    mine_ref[:, rows:, :] = pieces_ref[...] + diagonal(mine, core, GROUP - 2)
    other_ref[:, rows:, :] = diagonal(others, 1 - core, GROUP - 4).astype(bf16)


def make_margin(first, last, bands, core, trial, pieces, before, margin):
    share, local_g = trial.shape[0] // 2, trial.shape[1]
    chips = pieces.shape[0]
    if last:
        rows = bands // (2 * chips) + GROUP
        out_shape = [
            jax.ShapeDtypeStruct((chips, rows, bands), f32),
            jax.ShapeDtypeStruct((chips, rows, bands), bf16),
        ]
    else:
        out_shape = [jax.ShapeDtypeStruct((share, share), f32)]
    operands = [core, trial] + ([pieces] if last else []) + ([] if first else [before, margin])
    inside = pl.BlockSpec(memory_space=pltpu.VMEM)
    return pl.pallas_call(
        functools.partial(margin_kernel, first, last),
        in_specs=[pl.BlockSpec(memory_space=pltpu.SMEM)] + [inside] * (len(operands) - 1),
        out_specs=[inside] * len(out_shape),
        out_shape=out_shape,
        scratch_shapes=[pltpu.VMEM((bands, bands), f32)] if last else [],
        compiler_params=pltpu.CompilerParams(vmem_limit_bytes=LAST_VMEM_BYTES),
        cost_estimate=pl.CostEstimate(
            flops=8 * share * (share if first else 2 * share) * local_g,
            bytes_accessed=8 * share * local_g,
            transcendentals=0,
        ),
    )(*operands)


def update_kernel(count, core_ref, mine_ref, other_ref, *refs):
    trials, (out_ref, even, odd) = refs[:count], refs[count:]

    @pl.when(pl.program_id(0) == 0)
    def _():
        mine, others = mine_ref[...], other_ref[...]
        first = core_ref[0] == 0
        packed = jnp.concatenate(
            [jnp.where(first, mine, others), jnp.where(first, others, mine)], 0
        )
        share = packed.shape[0] // count
        row = lax.broadcasted_iota(jnp.int32, (share, share), 0)
        column = lax.broadcasted_iota(jnp.int32, (share, share), 1)
        spans = [slice(chunk * share, (chunk + 1) * share) for chunk in range(count)]
        for lower, down in enumerate(spans):
            own = packed[down, down]
            flipped = own.T
            even[down, down] = jnp.where(row <= column, own, flipped)
            above = jnp.where(row == column, jnp.zeros_like(own), -flipped)
            odd[down, down] = jnp.where(row > column, own, above)
            for over in spans[:lower]:
                both, opposite = packed[over, down], packed[down, over]
                even[down, over] = both
                even[over, down] = both.T
                odd[down, over] = opposite
                odd[over, down] = -opposite.T

    parted = [split_rows(trial[...]) for trial in trials]
    real = jnp.concatenate([part[0] for part in parted], 0)
    imag = jnp.concatenate([part[1] for part in parted], 0)
    both = jnp.concatenate([real, imag], 0)
    out_ref[:, 0, :] = matmul(jnp.concatenate([even[...], -odd[...]], 1), both).astype(bf16)
    out_ref[:, 1, :] = matmul(jnp.concatenate([odd[...], even[...]], 1), both).astype(bf16)


def update_waves(core, mine, others, trials):
    rows, local_g = trials[0].shape
    count = len(trials)
    bands = rows // 2 * count
    width = min(WIDE, local_g)
    return pl.pallas_call(
        functools.partial(update_kernel, count),
        grid=(local_g // width,),
        in_specs=[
            pl.BlockSpec(memory_space=pltpu.SMEM),
            pl.BlockSpec((bands // 2, bands), lambda step: (0, 0)),
            pl.BlockSpec((bands // 2, bands), lambda step: (0, 0)),
        ]
        + [pl.BlockSpec((rows, width), lambda step: (0, step))] * count,
        out_specs=pl.BlockSpec((bands, 2, width), lambda step: (0, 0, step)),
        out_shape=jax.ShapeDtypeStruct((bands, 2, local_g), bf16),
        scratch_shapes=[pltpu.VMEM((bands, bands), bf16)] * 2,
        compiler_params=pltpu.CompilerParams(vmem_limit_bytes=LAST_VMEM_BYTES),
        cost_estimate=pl.CostEstimate(
            flops=8 * bands * bands * local_g,
            bytes_accessed=8 * bands * local_g,
            transcendentals=0,
        ),
    )(core, mine, others, *trials)


def per_device(positions, weights, psi, vloc):
    parts = lax.axis_size("ga")
    bands = psi.shape[1]
    local_g = psi.shape[3]

    weight_float = weights.astype(jnp.float32)
    mixing = weight_float / jnp.sum(weight_float, axis=1, keepdims=True)
    count = 2 if bands // parts % (2 * GROUP) == 0 else 1
    share = bands // count

    sent = pack_first(positions, weights, psi, parts, share)
    waves = [exchange(sent)]
    for chunk in range(1, count):
        block = psi[0, chunk * share : (chunk + 1) * share]
        waves.append(exchange(block.reshape(parts, share // parts, 2, local_g)))
    psi_rows = local_g // sent.shape[3] * share // parts
    oxygens = unpack_oxygens(waves[0][:, psi_rows:], positions.shape[2])
    tables = transform_tables()
    in_plane, along = projector_tables(oxygens)
    grid_potential = vloc[0].reshape(NGRID, PLANE) * (step_size / GVECS)
    line = frequency(jnp.arange(NGRID, dtype=jnp.int32), NGRID) ** 2
    square = line[:, None, None] + line[None, :, None] + line[None, None, :]
    kept = (1.0 - step_size * 0.5 * square).reshape(NGRID, PLANE)
    trials, forces = [], []
    for wave in waves:
        moved, force = make_trial(
            wave, share // parts, local_g, tables, grid_potential, kept, in_plane, along
        )
        trials.append(exchange(moved).reshape(2 * share, local_g))
        forces.append(force)
    force_part = jnp.sum(sum(forces), axis=1) * (2.0 * occupation * nonlocal_strength / GVECS)

    chip, core = lax.axis_index("ga") // 2, lax.axis_index("ga") % 2
    chips = parts // 2
    rows = bands // parts
    same_core = [[2 * number + which for number in range(chips)] for which in range(2)]
    core_ref = core.reshape(1).astype(jnp.int32)
    near_chip = WATERS // chips
    pieces, left = [], force_part
    for _ in range(3):
        pieces.append(lax.reduce_precision(left, 8, 7))
        left = left - pieces[-1]
    pieces = jnp.swapaxes(jnp.stack(pieces).reshape(9, chips, near_chip), 0, 1)
    pieces = jnp.pad(pieces.reshape(chips, -1), ((0, 0), (0, GROUP * bands - 9 * near_chip)))
    pieces = pieces.reshape(chips, GROUP, bands)
    before, margin = None, None
    for chunk, trial in enumerate(trials):
        margin, *others = make_margin(
            chunk == 0, chunk == count - 1, bands, core_ref, trial, pieces, before, margin
        )
        before = trial
    pair = (margin + other_core(others[0], parts).astype(f32)).astype(bf16)
    summed = jnp.sum(exchange(pair, same_core).astype(f32), axis=0)
    diagonal = jnp.sum(summed[rows + GROUP - 4 :], axis=0, keepdims=True)
    summed, found = summed[:rows], summed[rows:].reshape(-1)[: 9 * near_chip]
    found = jnp.sum(found.reshape(3, 3, near_chip), axis=0)
    found = (found + other_core(found, parts)).reshape(3, 2, near_chip // 2)
    oxygen_force = lax.dynamic_index_in_dim(found, core, 1, keepdims=False)
    row = (core * chips + chip) * rows + lax.broadcasted_iota(jnp.int32, (rows, bands), 0)
    column = lax.broadcasted_iota(jnp.int32, (rows, bands), 1)
    own_mixer = jnp.where(row == column, 1.5 - 0.5 * diagonal, -0.5 * summed).astype(bf16)
    half_mixer = exchange(
        jnp.broadcast_to(own_mixer[None], (chips, rows, bands)), same_core
    ).reshape(bands // 2, bands)
    psi_new = update_waves(core_ref, half_mixer, other_core(half_mixer, parts), trials)

    hydrogen_zero = jnp.zeros_like(oxygen_force)
    dft_force = jnp.stack([oxygen_force, hydrogen_zero, hydrogen_zero], axis=2).reshape(1, 3, -1)

    near_forces = field_forces(positions)
    contracted_force = jnp.einsum("cj,can->jan", mixing, dft_force, precision=highest)
    bead_forces = near_forces + BEADS / CBEADS * contracted_force
    return (psi_new[None], bead_forces)


def solution(mesh):
    placed = (P("rep", None, "ga"), P(), P("rep", None, None, "ga"), P("rep", None))
    return jax.shard_map(
        per_device,
        mesh=mesh,
        in_specs=placed,
        out_specs=(P("rep", None, None, "ga"), P("rep", None, "ga")),
        check_vma=False,
    )
```
